128 devices in a mesh: section: 2 (over x_lo), dp: 32 (over z, x_hi, y), tensor: 2 (over core).
Axes of the slice: x: 4 (x_hi: 2, x_lo: 2; x = x_hi * 2 + x_lo), y: 4, z: 4, core: 2. Of those that a mesh axis runs over, the one named last changes fastest.
Arguments:
- block_input: bfloat16 [16384, 1024], P('dp'), may hold values from -6 to 6
- doc_lengths: int32 [64, 4], P('dp'), may hold values from 1 to 128, 256 in all within a row
- out_cotangent: bfloat16 [16384, 1024], P('dp'), may hold values from -6 to 6
- attn_gain: float32 [2, 1024], P('section'), may hold values from 0.5 to 1.5
- q_gain: float32 [2, 128], P('section'), may hold values from 0.5 to 1.5
- k_gain: float32 [2, 128], P('section'), may hold values from 0.5 to 1.5
- mlp_gain: float32 [2, 1024], P('section'), may hold values from 0.5 to 1.5
- q_weight: bfloat16 [2, 1024, 2048], P('section', None, 'tensor'), may hold values from -0.1875 to 0.1875
- key_matrix: bfloat16 [2, 1024, 1024], P('section', None, 'tensor'), may hold values from -0.1875 to 0.1875
- value_matrix: bfloat16 [2, 1024, 1024], P('section', None, 'tensor'), may hold values from -0.1875 to 0.1875
- o_weight: bfloat16 [2, 1024, 2048], P('section', None, 'tensor'), may hold values from -0.25 to 0.25
- gate_weight: bfloat16 [2, 1024, 3072], P('section', None, 'tensor'), may hold values from -0.1875 to 0.1875
- up_weight: bfloat16 [2, 1024, 3072], P('section', None, 'tensor'), may hold values from -0.1875 to 0.1875
- down_weight: bfloat16 [2, 1024, 3072], P('section', None, 'tensor'), may hold values from -0.109375 to 0.109375
Outputs:
- hidden_out: float32 [2, 16384, 1024], P('section', 'dp')
- hidden_grad: float32 [2, 16384, 1024], P('section', 'dp')
- attn_gain_grad: float32 [2, 1024], P('section')
- q_gain_grad: float32 [2, 128], P('section')
- k_gain_grad: float32 [2, 128], P('section')
- mlp_gain_grad: float32 [2, 1024], P('section')
- q_grad: float32 [2, 1024, 2048], P('section', 'dp', 'tensor')
- k_grad: float32 [2, 1024, 1024], P('section', 'dp', 'tensor')
- v_grad: float32 [2, 1024, 1024], P('section', 'dp', 'tensor')
- o_grad: float32 [2, 1024, 2048], P('section', 'dp', 'tensor')
- gate_grad: float32 [2, 1024, 3072], P('section', 'dp', 'tensor')
- up_grad: float32 [2, 1024, 3072], P('section', 'dp', 'tensor')
- down_grad: float32 [2, 1024, 3072], P('section', 'dp', 'tensor')
The draws below stay inside these ranges and needn't reach their ends.
Inputs may be any that keep to these rules, and one draw needn't show every extreme that they name: `doc_lengths`: each row's 4 lengths sum to 256, and each row's largest is exactly 128; row m of a dp index's 2 rows is its m-th micro-batch.
All inputs are finite; a program needn't handle non-finite values.
Results may differ from the reference program's by a relative error of at most 0.03.
Values may be sent and summed in bfloat16 or wider, within the bound.
A program may use at most 192 MiB of HBM per device.

```python
import math
import jax
import jax.numpy as jnp
import numpy as np
from jax import lax

MODEL_WIDTH = 1024
QUERY_HEADS = 16
KEY_VALUE_HEADS = 8
HEAD_SIZE = 128
FF = 3072
MICRO = 2
DOCS = 4
PACKED_ROW = 256
TOKENS = 16384
NROWS = 64
LAYER_COUNT = 2
N_DP = 32


def levels(own_key, shape, shards, least, largest):
    factor_of = 1.0
    for dim, blocks in shards:
        steps = jax.random.uniform(jax.random.fold_in(jax.random.fold_in(own_key, 6), dim), (blocks,), jnp.float32, least / len(shards), largest / len(shards))
        factor_of = factor_of * jnp.repeat(jnp.exp(steps), shape[dim] // blocks).reshape((-1,) + (1,) * (len(shape) - 1 - dim))
    return factor_of


def length_profile(count, total, most, slope):
    loads = [(1 << 20) // math.isqrt(standing ** slope) + 1 for standing in range(2, count + 1)]
    spare, given = total - most - (count - 1), [1] * (count - 1)
    while spare > 0:
        movable = [i for i in range(count - 1) if given[i] < most]
        pool, budget = sum([loads[i] for i in movable]), spare
        for i in movable:
            more = min(most - given[i], max(1, budget * loads[i] // pool), spare)
            given[i] = given[i] + more
            spare = spare - more
    return np.array([most] + given)


def uneven_parts(rng, number_of, total, most, slope):
    if number_of == 2:
        one = jax.random.randint(rng, (), max(1, total - most), min(most, total - 1) + 1)
        return jnp.stack([one, total - one])
    sizes = jnp.asarray(length_profile(number_of, total, most, slope), jnp.int32)
    couples = (number_of - 1) // 2
    giver, taker = sizes[1:1 + 2 * couples:2], sizes[2:2 + 2 * couples:2]
    margin = jnp.minimum(giver - 1, most - taker)
    shifted = jax.random.randint(jax.random.fold_in(rng, 1), (couples,), 0, 1 << 20) % (margin + 1)
    sizes = sizes.at[1:1 + 2 * couples:2].set(giver - shifted).at[2:2 + 2 * couples:2].set(taker + shifted)
    return sizes[jax.random.permutation(jax.random.fold_in(rng, 2), number_of)]


def noise(rng, shape, width, limit, shards=(), kind=jnp.bfloat16):
    level = levels(rng, shape, shards, -0.22, 0.18) if shards else 1.0
    values = jax.random.normal(rng, shape, jnp.float32) * width * level
    return jnp.minimum(jnp.maximum(values, -limit), limit).astype(kind)


def setup_inputs(seed: int = 0) -> dict:
    keys = jax.random.split(jax.random.key(seed), 15)
    block_input = noise(keys[0], (TOKENS, MODEL_WIDTH), 1.0, 6.0, ((0, 32),))
    doc_lengths = jax.vmap(lambda own: uneven_parts(own, DOCS, PACKED_ROW, PACKED_ROW // 2, 2))(jax.random.split(keys[1], NROWS)).reshape((NROWS, DOCS)).astype(jnp.int32)
    out_cotangent = noise(keys[2], (TOKENS, MODEL_WIDTH), 1.0, 6.0, ((0, 32),))
    attn_gain = jnp.clip(1.0 + 0.1 * jax.random.normal(keys[3], (LAYER_COUNT, MODEL_WIDTH), jnp.float32), 0.5, 1.5)
    q_gain = jnp.clip(1.0 + 0.1 * jax.random.normal(keys[4], (LAYER_COUNT, HEAD_SIZE), jnp.float32), 0.5, 1.5)
    k_gain = jnp.clip(1.0 + 0.1 * jax.random.normal(keys[5], (LAYER_COUNT, HEAD_SIZE), jnp.float32), 0.5, 1.5)
    mlp_gain = jnp.clip(1.0 + 0.1 * jax.random.normal(keys[6], (LAYER_COUNT, MODEL_WIDTH), jnp.float32), 0.5, 1.5)
    q_weight = noise(keys[7], (LAYER_COUNT, MODEL_WIDTH, QUERY_HEADS * HEAD_SIZE), MODEL_WIDTH ** -0.5, 0.1875, ((0, 2), (2, 2)))
    key_matrix = noise(keys[8], (LAYER_COUNT, MODEL_WIDTH, KEY_VALUE_HEADS * HEAD_SIZE), MODEL_WIDTH ** -0.5, 0.1875, ((0, 2), (2, 2)))
    value_matrix = noise(keys[9], (LAYER_COUNT, MODEL_WIDTH, KEY_VALUE_HEADS * HEAD_SIZE), MODEL_WIDTH ** -0.5, 0.1875, ((0, 2), (2, 2)))
    o_weight = noise(keys[10], (LAYER_COUNT, MODEL_WIDTH, QUERY_HEADS * HEAD_SIZE), (QUERY_HEADS * HEAD_SIZE // 4) ** -0.5, 0.25, ((0, 2), (2, 2)))
    gate_weight = noise(keys[11], (LAYER_COUNT, MODEL_WIDTH, FF), MODEL_WIDTH ** -0.5, 0.1875, ((0, 2), (2, 2)))
    up_weight = noise(keys[12], (LAYER_COUNT, MODEL_WIDTH, FF), MODEL_WIDTH ** -0.5, 0.1875, ((0, 2), (2, 2)))
    down_weight = noise(keys[13], (LAYER_COUNT, MODEL_WIDTH, FF), FF ** -0.5, 0.109375, ((0, 2), (2, 2)))
    return {"block_input": block_input, "doc_lengths": doc_lengths, "out_cotangent": out_cotangent, "attn_gain": attn_gain, "q_gain": q_gain, "k_gain": k_gain, "mlp_gain": mlp_gain, "q_weight": q_weight, "key_matrix": key_matrix, "value_matrix": value_matrix, "o_weight": o_weight, "gate_weight": gate_weight, "up_weight": up_weight, "down_weight": down_weight}


EPSILON = 1e-06
THETA = 1000000.0

@jax.custom_vjp
def lowered_value(v):
    return lax.optimization_barrier(v.astype(jnp.bfloat16)).astype(jnp.float32)

@jax.custom_vjp
def lowered_backward(v):
    return v

def low_keep(v):
    return (lowered_value(v), None)

def low_pass(kept, grad):
    return (grad,)

def back_keep(v):
    return (v, None)

def back_low(kept, grad):
    return (lowered_value(grad),)
lowered_value.defvjp(low_keep, low_pass)
lowered_backward.defvjp(back_keep, back_low)

def doc_tables(lengths, rows):
    ends = jnp.cumsum(lengths, axis=-1, dtype=jnp.int32)
    starts = ends - lengths
    place = jnp.arange(rows, dtype=jnp.int32)
    inside = (place[None, :, None] >= starts[:, None, :]) & (place[None, :, None] < ends[:, None, :])
    begins = lax.optimization_barrier(jnp.sum(jnp.where(inside, starts[:, None, :], 0), axis=-1, dtype=jnp.int32))
    finished = lax.optimization_barrier(jnp.sum((place[None, :, None] >= ends[:, None, :]).astype(jnp.int32), axis=-1, dtype=jnp.int32))
    offsets = place[None, :] - begins
    allowed = (finished[:, :, None] == finished[:, None, :]) & (place[None, None, :] <= place[None, :, None])
    return (offsets, allowed)

def rope_tables(offsets, size):
    half = size // 2
    rates = jnp.power(THETA, -2.0 * jnp.arange(half, dtype=jnp.float32) / size)
    angle = offsets.astype(jnp.float32)[..., None] * rates
    angle = jnp.concatenate([angle, angle], axis=-1)
    return (jnp.cos(angle), jnp.sin(angle))

def norm_rows(value, gain):
    return value * lax.rsqrt(lax.optimization_barrier(jnp.mean(value * value, axis=-1, keepdims=True)) + EPSILON) * gain

def turn_half(value):
    half = value.shape[-1] // 2
    return jnp.concatenate([-value[..., half:], value[..., :half]], axis=-1)

def product_term(form, left, right):
    return jnp.einsum(form, left, right, precision=lax.Precision.HIGHEST)

def layer(hidden, cosine, sine, allowed, weights):
    attn_gain, q_gain, k_gain, mlp_gain, q_weight, key_matrix, value_matrix, o_weight, gate_weight, up_weight, down_weight = weights
    token_batch = hidden.shape[0]
    shared_portion = QUERY_HEADS // KEY_VALUE_HEADS
    cos_four = cosine[:, :, None, :]
    sin_four = sine[:, :, None, :]
    normed_input = lowered_value(norm_rows(hidden, attn_gain))
    query = lowered_backward(product_term('cus,sn->cun', normed_input, q_weight)).reshape(token_batch, PACKED_ROW, QUERY_HEADS, HEAD_SIZE)
    key_rows = lowered_backward(product_term('cus,sn->cun', normed_input, key_matrix)).reshape(token_batch, PACKED_ROW, KEY_VALUE_HEADS, HEAD_SIZE)
    value_rows = lowered_value(lowered_backward(product_term('cus,sn->cun', normed_input, value_matrix))).reshape(token_batch, PACKED_ROW, KEY_VALUE_HEADS, HEAD_SIZE)
    query_norm = norm_rows(query, q_gain)
    key_norm = norm_rows(key_rows, k_gain)
    rotated_query = lowered_value(query_norm * cos_four + turn_half(query_norm) * sin_four)
    key_rot = lowered_value(key_norm * cos_four + turn_half(key_norm) * sin_four)
    grouped_heads = rotated_query.reshape(token_batch, PACKED_ROW, KEY_VALUE_HEADS, shared_portion, HEAD_SIZE)
    scores = lowered_backward(product_term('brkgd,bckd->bkgrc', grouped_heads, key_rot) * HEAD_SIZE ** (-0.5))
    scores = jnp.where(allowed[:, None, None], scores, -1000000000.0)
    probs = lowered_value(jax.nn.softmax(scores, axis=-1))
    mixed = lowered_value(lowered_backward(product_term('bkgrc,bckd->brkgd', probs, value_rows))).reshape(token_batch, PACKED_ROW, QUERY_HEADS * HEAD_SIZE)
    attended = lowered_backward(product_term('brf,df->brd', mixed, o_weight))
    middle = hidden + attended
    normed_two = lowered_value(norm_rows(middle, mlp_gain))
    gate = lowered_backward(product_term('cus,sn->cun', normed_two, gate_weight))
    up = lowered_backward(product_term('cus,sn->cun', normed_two, up_weight))
    act = lowered_value(jax.nn.silu(gate) * up)
    moved = lowered_backward(product_term('brf,df->brd', act, down_weight))
    return middle + moved

def reference(block_input, doc_lengths, out_cotangent, attn_gain, q_gain, k_gain, mlp_gain, q_weight, key_matrix, value_matrix, o_weight, gate_weight, up_weight, down_weight):
    params = tuple((piece.astype(jnp.float32) for piece in (attn_gain, q_gain, k_gain, mlp_gain, q_weight, key_matrix, value_matrix, o_weight, gate_weight, up_weight, down_weight)))
    inputs = block_input.astype(jnp.float32).reshape(N_DP, MICRO, PACKED_ROW, MODEL_WIDTH)
    lengths = doc_lengths.reshape(N_DP, MICRO, DOCS)
    cotangents = out_cotangent.astype(jnp.float32).reshape(N_DP, MICRO, PACKED_ROW, MODEL_WIDTH)

    def one_group(totals, pieces):
        group_input, group_lengths, group_cotangent = pieces
        offsets, allowed = doc_tables(group_lengths, PACKED_ROW)
        cosine, sine = rope_tables(offsets, HEAD_SIZE)

        def stack(hidden, probe, weights):
            first = layer(hidden, cosine, sine, allowed, [piece[0] for piece in weights])
            passed = lowered_value(lowered_backward(first)) + probe
            second = layer(passed, cosine, sine, allowed, [piece[1] for piece in weights])
            return (first, second)
        (first, second), pull = jax.vjp(stack, group_input, jnp.zeros_like(group_input), params)
        grad_input, grad_probe, grad_weights = pull((jnp.zeros_like(first), group_cotangent))
        totals = jax.tree.map(jnp.add, totals, grad_weights)
        return (totals, (first, second, grad_input, grad_probe))
    zeros = jax.tree.map(jnp.zeros_like, params)
    totals, (first, second, grad_input, grad_probe) = lax.scan(one_group, zeros, (inputs, lengths, cotangents))
    hidden_out = jnp.stack([first.reshape(TOKENS, MODEL_WIDTH), second.reshape(TOKENS, MODEL_WIDTH)])
    hidden_grad = jnp.stack([grad_input.reshape(TOKENS, MODEL_WIDTH), grad_probe.reshape(TOKENS, MODEL_WIDTH)])
    return (hidden_out, hidden_grad, totals[0], totals[1], totals[2], totals[3], totals[4], totals[5], totals[6], totals[7], totals[8], totals[9], totals[10])
```

```python
import functools

import jax
import jax.numpy as jnp
from jax import lax
from jax.experimental import pallas as pl
from jax.experimental.pallas import tpu as pltpu
from jax.sharding import PartitionSpec as P

HEAD_SIZE = 128


EPSILON = 1e-06
THETA = 1000000.0
CONTRACT_ROWS = (((0,), (0,)), ((), ()))
CONTRACT_COLS = (((1,), (1,)), ((), ()))

MESH = pl.DeviceIdType.MESH
CHUNK = 512
RING_FIRST = (("z", "y", "x"), 8), (("y", "z", "x"), 7)
LAGS = (0, 2, 4, 4, 6, 8, 8, 10)


def pair_sum_kernel(part_ref, sum_ref, mine, theirs, send_sem, recv_sem):
    other = {"tensor": 1 - lax.axis_index("tensor")}
    barrier = pltpu.get_barrier_semaphore()
    pl.semaphore_signal(barrier, inc=1, device_id=other, device_id_type=MESH)
    mine[...] = part_ref[...].astype(jnp.bfloat16)
    pl.semaphore_wait(barrier, 1)
    copy = pltpu.make_async_remote_copy(
        src_ref=mine,
        dst_ref=theirs,
        send_sem=send_sem,
        recv_sem=recv_sem,
        device_id=other,
        device_id_type=MESH,
    )
    copy.start()
    copy.wait()
    sum_ref[...] = mine[...].astype(jnp.float32) + theirs[...].astype(jnp.float32)


def pair_sum(part):
    return pl.pallas_call(
        pair_sum_kernel,
        out_shape=jax.ShapeDtypeStruct(part.shape, jnp.float32),
        in_specs=[pl.BlockSpec(memory_space=pltpu.VMEM)],
        out_specs=pl.BlockSpec(memory_space=pltpu.VMEM),
        scratch_shapes=[
            pltpu.VMEM(part.shape, jnp.bfloat16),
            pltpu.VMEM(part.shape, jnp.bfloat16),
            pltpu.SemaphoreType.DMA,
            pltpu.SemaphoreType.DMA,
        ],
        compiler_params=pltpu.CompilerParams(
            collective_id=1, has_side_effects=True, vmem_limit_bytes=16 * 2**20
        ),
    )(part)


class Place:
    def __init__(self):
        dp = lax.axis_index("dp")
        self.at = {"z": dp // 8, "x": dp // 4 % 2, "y": dp % 4}

    def device(self, axis, index):
        at = {**self.at, axis: index}
        return {"dp": at["z"] * 8 + at["x"] * 4 + at["y"]}


def remote(src, dst, send_sem, recv_sem, device):
    return pltpu.make_async_remote_copy(
        src_ref=src,
        dst_ref=dst,
        send_sem=send_sem,
        recv_sem=recv_sem,
        device_id=device,
        device_id_type=MESH,
    )


def part_of(chunk, pos, index, split=None, half=0):
    where = [chunk]
    for kept in range(5):
        if kept == pos:
            where.append(index)
        elif split is not None and kept - (kept > pos) == split[0]:
            where.append(pl.ds(half * split[1], split[1]))
        else:
            where.append(slice(None))
    return tuple(where)


def phases_of(order):
    left, found = ["z", "x", "y"], []
    for axis in order:
        pos = left.index(axis)
        left = [name for name in left if name != axis]
        shape = tuple({"z": 4, "x": 2, "y": 4}[name] for name in left) + (32, CHUNK)
        split = None
        if axis != "x":
            along = left.index("x") if "x" in left else 0
            split = (along, shape[along] // 2)
        found.append((axis, pos, shape, split))
    return found


def ring_scratch(order, count):
    found = []
    for step, (axis, _, shape, split) in enumerate(phases_of(order)):
        if split is None:
            found.append(pltpu.VMEM((count, *shape), jnp.bfloat16))
            sems = 1
        else:
            half = list(shape)
            half[split[0]] = split[1]
            found.append(pltpu.VMEM((count, 6, *half), jnp.bfloat16))
            sems = 6
        if step < 2:
            found.append(pltpu.VMEM((count, *shape), jnp.bfloat16))
        found.append(pltpu.SemaphoreType.DMA((count, sems)))
        found.append(pltpu.SemaphoreType.DMA((count, sems)))
    return found


def part_at(ref, chunk, phase, index, half):
    where = part_of(chunk, phase[1], index, phase[3], half)
    return where[: len(ref.shape)]


def ring_stages(order, src, scratch, place, finish):
    stages = []
    for step, phase in enumerate(phases_of(order)):
        axis, pos, shape, split = phase
        last = step == 2
        arrived = scratch[0]
        result = None if last else scratch[1]
        send_sem, recv_sem = scratch[1 if last else 2], scratch[2 if last else 3]
        scratch = scratch[3 if last else 4 :]
        mine = place.at[axis]

        def put(chunk, half, total, result=result, split=split, shape=shape):
            if result is None:
                finish(chunk, half, total)
                return
            where = [chunk] + [slice(None)] * len(shape)
            if split is not None:
                where[1 + split[0]] = pl.ds(half * split[1], split[1])
            result[tuple(where)] = total.astype(jnp.bfloat16)

        if split is None:

            def swap(
                chunk,
                src=src,
                arrived=arrived,
                send_sem=send_sem,
                recv_sem=recv_sem,
                phase=phase,
                axis=axis,
                mine=mine,
            ):
                return remote(
                    src.at[part_at(src, chunk, phase, 1 - mine, 0)],
                    arrived.at[chunk],
                    send_sem.at[chunk, 0],
                    recv_sem.at[chunk, 0],
                    place.device(axis, 1 - mine),
                )

            def start(chunk, swap=swap):
                swap(chunk).start()

            def end(chunk, swap=swap, src=src, arrived=arrived, phase=phase, mine=mine, put=put):
                swap(chunk).wait()
                own = src[part_at(src, chunk, phase, mine, 0)].astype(jnp.float32)
                put(chunk, 0, own + arrived[chunk].astype(jnp.float32))

            stages += [start, end]
        else:
            right, left = lax.rem(mine + 1, 4), lax.rem(mine + 3, 4)
            sends = (
                (lax.rem(mine + 2, 4), 0, right),
                (lax.rem(mine + 2, 4), 1, left),
                (right, 1, right),
                (left, 0, left),
                (right, 0, right),
                (left, 1, left),
            )

            def send(
                chunk,
                k,
                src=src,
                arrived=arrived,
                send_sem=send_sem,
                recv_sem=recv_sem,
                phase=phase,
                axis=axis,
                sends=sends,
            ):
                index, half, to = sends[k]
                piece = src.at[part_at(src, chunk, phase, index, half)] if k < 4 else arrived.at[chunk, k - 4]
                return remote(
                    piece,
                    arrived.at[chunk, k],
                    send_sem.at[chunk, k],
                    recv_sem.at[chunk, k],
                    place.device(axis, to),
                )

            def start(chunk, send=send):
                for k in range(4):
                    send(chunk, k).start()

            def pass_on(chunk, send=send, src=src, arrived=arrived, phase=phase, sends=sends):
                for k in (0, 1):
                    send(chunk, k).wait_recv()
                    index, half, _ = sends[4 + k]
                    where = part_at(src, chunk, phase, index, half)
                    total = src[where].astype(jnp.float32) + arrived[chunk, k].astype(jnp.float32)
                    arrived[chunk, k] = total.astype(jnp.bfloat16)
                    send(chunk, 4 + k).start()

            def end(chunk, send=send, src=src, arrived=arrived, phase=phase, mine=mine, put=put):
                for k in range(2, 6):
                    send(chunk, k).wait_recv()
                for k in range(6):
                    send(chunk, k).wait_send()
                for half in (0, 1):
                    own = src[part_at(src, chunk, phase, mine, half)].astype(jnp.float32)
                    near = arrived[chunk, 4 - 2 * half].astype(jnp.float32)
                    far = arrived[chunk, 3 + 2 * half].astype(jnp.float32)
                    put(chunk, half, own + near + far)

            stages += [start, pass_on, end]
        src = result
    return stages


GAIN_ROWS = 24


def gain_scratch():
    found = [pltpu.VMEM((4, GAIN_ROWS, 128), jnp.float32)]
    for size in (4, 4, 2, 2):
        found.append(pltpu.SemaphoreType.DMA((size,)))
        found.append(pltpu.SemaphoreType.DMA((size,)))
        found.append(pltpu.VMEM((size, GAIN_ROWS, 128), jnp.float32))
    return found


def gain_axes(place):
    tensor = lax.axis_index("tensor")
    return (
        (4, place.at["y"], lambda k: place.device("y", k)),
        (4, place.at["z"], lambda k: place.device("z", k)),
        (2, place.at["x"], lambda k: place.device("x", k)),
        (2, tensor, lambda k: {"tensor": k}),
    )


def gain_stages(own_ref, total_ref, scratch, place):
    held = scratch[0]
    stages = []
    for step, (size, mine, device) in enumerate(gain_axes(place)):
        send_sem, recv_sem, slots = scratch[1 + 3 * step : 4 + 3 * step]
        src = own_ref if step == 0 else held.at[step]
        dst = total_ref if step == 3 else held.at[step + 1]

        def send(k, src=src, slots=slots, send_sem=send_sem, recv_sem=recv_sem, size=size, mine=mine, device=device):
            to = lax.rem(mine + k, size)
            return remote(src, slots.at[mine], send_sem.at[k], recv_sem.at[mine], device(to))

        def arrival(k, src=src, slots=slots, send_sem=send_sem, recv_sem=recv_sem, size=size, mine=mine, device=device):
            frm = lax.rem(mine + k, size)
            return remote(src, slots.at[frm], send_sem.at[k], recv_sem.at[frm], device(frm))

        def start(chunk, send=send, src=src, slots=slots, size=size, mine=mine):
            slots[mine] = src[...]
            for k in range(1, size):
                send(k).start()

        def end(chunk, send=send, arrival=arrival, slots=slots, size=size, dst=dst):
            for k in range(1, size):
                arrival(k).wait_recv()
                send(k).wait_send()
            total = slots[0]
            for k in range(1, size):
                total = total + slots[k]
            dst[...] = total

        stages += [start, end]
    return stages


def reduce_kernel(first_ref, second_ref, gains_ref, out_ref, gains_out_ref, *scratch):
    place = Place()
    barrier = pltpu.get_barrier_semaphore()
    for size, mine, device in gain_axes(place):
        for k in range(1, size):
            pl.semaphore_signal(
                barrier, inc=1, device_id=device(lax.rem(mine + k, size)), device_id_type=MESH
            )
    pl.semaphore_wait(barrier, 8)
    groups, base = [], 0
    for (order, count), src in zip(RING_FIRST, (first_ref, second_ref)):
        own, scratch = scratch[:11], scratch[11:]

        def finish(chunk, half, total, base=base):
            out_ref[base + chunk] = total

        groups.append((count, LAGS, ring_stages(order, src, own, place, finish)))
        base += count
    gains = gain_stages(gains_ref, gains_out_ref, scratch, place)
    groups.append((1, (0, 2, 2, 4, 4, 6, 6, 8), gains))

    def turn(now, carry):
        for stage in range(8):
            for count, lags, stages in groups:
                chunk = now - lags[stage]

                @pl.when((chunk >= 0) & (chunk < count))
                def _(chunk=chunk, run=stages[stage]):
                    run(chunk)

        return carry

    lax.fori_loop(0, max(count + lags[-1] for count, lags, _ in groups), turn, 0)


def reduce_over_dp(first, second, gains):
    scratch = []
    for order, count in RING_FIRST:
        scratch += ring_scratch(order, count)
    count = sum(count for _, count in RING_FIRST)
    return pl.pallas_call(
        reduce_kernel,
        out_shape=(
            jax.ShapeDtypeStruct((count, 32, CHUNK), jnp.float32),
            jax.ShapeDtypeStruct(gains.shape, jnp.float32),
        ),
        in_specs=[pl.BlockSpec(memory_space=pltpu.VMEM)] * 3,
        out_specs=[pl.BlockSpec(memory_space=pltpu.VMEM)] * 2,
        scratch_shapes=scratch + gain_scratch(),
        compiler_params=pltpu.CompilerParams(
            collective_id=0, has_side_effects=True, vmem_limit_bytes=60 * 2**20
        ),
    )(first, second, gains)


def summed_over_dp(terms, gains):
    chunks = []
    for term in terms:
        low = term.astype(jnp.bfloat16)
        for start in range(0, term.shape[1], CHUNK):
            chunks.append(low[:, start : start + CHUNK].reshape(4, 2, 4, 32, CHUNK))
    flat = jnp.concatenate(gains)
    packed = jnp.pad(flat, (0, GAIN_ROWS * 128 - flat.shape[0])).reshape(GAIN_ROWS, 128)
    out, packed = reduce_over_dp(jnp.stack(chunks[:8]), jnp.stack(chunks[8:]), packed)
    done, at = [], 0
    for term in terms:
        count = term.shape[1] // CHUNK
        done.append(jnp.concatenate([out[at + k] for k in range(count)], axis=1))
        at += count
    flat = packed.reshape(-1)
    summed, at = [], 0
    for gain in gains:
        summed.append(flat[at : at + gain.shape[0]])
        at += gain.shape[0]
    return done, summed


def passed_along(shard, axis, by):
    peers = lax.axis_size(axis)
    pairs = [(i, i + by) for i in range(peers) if 0 <= i + by < peers]
    return lax.ppermute(shard, axis, pairs)


def doc_tables(lengths, rows):
    ends = jnp.cumsum(lengths, axis=-1, dtype=jnp.int32)
    starts = ends - lengths
    place = jnp.arange(rows, dtype=jnp.int32)
    inside = (place[None, :, None] >= starts[:, None, :]) & (
        place[None, :, None] < ends[:, None, :]
    )
    begins = jnp.sum(jnp.where(inside, starts[:, None, :], 0), axis=-1, dtype=jnp.int32)
    finished = jnp.sum(
        (place[None, :, None] >= ends[:, None, :]).astype(jnp.int32), axis=-1, dtype=jnp.int32
    )
    offsets = place[None, :] - begins
    allowed = (finished[:, :, None] == finished[:, None, :]) & (
        place[None, None, :] <= place[None, :, None]
    )
    return (offsets, allowed)


def rope_tables(offsets, size):
    half = size // 2
    rates = jnp.power(THETA, -2.0 * jnp.arange(half, dtype=jnp.float32) / size)
    angle = offsets.astype(jnp.float32)[..., None] * rates
    angle = jnp.concatenate([angle, angle], axis=-1)
    return (jnp.cos(angle), jnp.sin(angle))


def turn_half(value):
    half = value.shape[-1] // 2
    return jnp.concatenate([-value[..., half:], value[..., :half]], axis=-1)


def rotate(value, cosine, sine):
    return value * cosine[:, None, :] + turn_half(value) * sine[:, None, :]


def unrotate(grad, cosine, sine):
    half = grad.shape[-1] // 2
    moved = grad * sine[:, None, :]
    return grad * cosine[:, None, :] + jnp.concatenate(
        [moved[..., half:], -moved[..., :half]], axis=-1
    )


def inverse_rms(value):
    return lax.rsqrt(jnp.mean(value * value, axis=-1, keepdims=True) + EPSILON)


def norm_back(grad, value, scale, gain):
    inner = grad * gain
    return scale * inner - value * (scale * scale * scale) * jnp.mean(
        inner * value, axis=-1, keepdims=True
    )


def scores_for(rotated_query, key_rot, allowed):
    raw = jnp.einsum(
        "rkgd,ckd->kgrc", rotated_query, key_rot, preferred_element_type=jnp.float32
    ) * HEAD_SIZE ** (-0.5)
    return jnp.where(allowed[None, None], raw, -1000000000.0)


def pick(table, index):
    return lax.dynamic_index_in_dim(table, index, 0, keepdims=False)


def layer_forward(hidden, cosine, sine, allowed, weights):
    (
        attn_gain,
        q_gain,
        k_gain,
        mlp_gain,
        q_weight,
        key_matrix,
        value_matrix,
        o_weight,
        gate_weight,
        up_weight,
        down_weight,
    ) = weights
    rows = hidden.shape[0]
    heads = q_weight.shape[1] // HEAD_SIZE
    groups = key_matrix.shape[1] // HEAD_SIZE
    scale_one = inverse_rms(hidden)
    normed_input = (hidden * scale_one * attn_gain).astype(jnp.bfloat16)
    query = jnp.dot(normed_input, q_weight, preferred_element_type=jnp.float32).reshape(
        rows, heads, HEAD_SIZE
    )
    key_rows = jnp.dot(normed_input, key_matrix, preferred_element_type=jnp.float32).reshape(
        rows, groups, HEAD_SIZE
    )
    value_rows = (
        jnp.dot(normed_input, value_matrix, preferred_element_type=jnp.float32)
        .astype(jnp.bfloat16)
        .reshape(rows, groups, HEAD_SIZE)
    )
    q_scale = inverse_rms(query)
    k_scale = inverse_rms(key_rows)
    rotated_query = (
        rotate(query * q_scale * q_gain, cosine, sine)
        .astype(jnp.bfloat16)
        .reshape(rows, groups, heads // groups, HEAD_SIZE)
    )
    key_rot = rotate(key_rows * k_scale * k_gain, cosine, sine).astype(jnp.bfloat16)
    scores = scores_for(rotated_query, key_rot, allowed)
    peak = jnp.max(scores, axis=-1, keepdims=True)
    log_total = peak + jnp.log(jnp.sum(jnp.exp(scores - peak), axis=-1, keepdims=True))
    probs_low = jnp.exp(scores - log_total).astype(jnp.bfloat16)
    mixed = (
        jnp.einsum("kgrc,ckd->rkgd", probs_low, value_rows, preferred_element_type=jnp.float32)
        .reshape(rows, heads * HEAD_SIZE)
        .astype(jnp.bfloat16)
    )
    attended = pair_sum(
        lax.dot_general(mixed, o_weight, CONTRACT_COLS, preferred_element_type=jnp.float32)
    )
    middle = hidden + attended
    scale_two = inverse_rms(middle)
    normed_two = (middle * scale_two * mlp_gain).astype(jnp.bfloat16)
    gate = jnp.dot(normed_two, gate_weight, preferred_element_type=jnp.float32)
    up = jnp.dot(normed_two, up_weight, preferred_element_type=jnp.float32)
    act = (jax.nn.silu(gate) * up).astype(jnp.bfloat16)
    moved = pair_sum(
        lax.dot_general(act, down_weight, CONTRACT_COLS, preferred_element_type=jnp.float32)
    )
    kept = (
        hidden,
        scale_one,
        normed_input,
        query,
        q_scale,
        key_rows,
        k_scale,
        value_rows,
        rotated_query,
        key_rot,
        log_total,
        mixed,
        middle,
        scale_two,
        normed_two,
        gate,
        up,
        act,
    )
    return (middle + moved, kept)


def mlp_backward(grad_out, kept, weights):
    mlp_gain = weights[3]
    gate_weight, up_weight, down_weight = (weights[8], weights[9], weights[10])
    middle, scale_two, normed_two, gate, up, act = kept[12:18]
    moved_grad = grad_out.astype(jnp.bfloat16)
    down_term = lax.dot_general(moved_grad, act, CONTRACT_ROWS, preferred_element_type=jnp.float32)
    act_grad = jnp.dot(moved_grad, down_weight, preferred_element_type=jnp.float32)
    sigma = jax.nn.sigmoid(gate)
    gate_low = (act_grad * up * sigma * (1.0 + gate * (1.0 - sigma))).astype(jnp.bfloat16)
    up_low = (act_grad * gate * sigma).astype(jnp.bfloat16)
    gate_term = lax.dot_general(
        normed_two, gate_low, CONTRACT_ROWS, preferred_element_type=jnp.float32
    )
    up_term = lax.dot_general(normed_two, up_low, CONTRACT_ROWS, preferred_element_type=jnp.float32)
    normed_part = lax.dot_general(
        gate_low, gate_weight, CONTRACT_COLS, preferred_element_type=jnp.float32
    )
    normed_part = normed_part + lax.dot_general(
        up_low, up_weight, CONTRACT_COLS, preferred_element_type=jnp.float32
    )
    gain_part = jnp.sum(normed_part * middle * scale_two, axis=0)
    normed_grad = pair_sum(normed_part)
    middle_grad = grad_out + norm_back(normed_grad, middle, scale_two, mlp_gain)
    return (middle_grad, gain_part, (gate_term, up_term, down_term))


def attention_backward(middle_grad, kept, cosine, sine, allowed, weights):
    attn_gain, q_gain, k_gain = (weights[0], weights[1], weights[2])
    q_weight, key_matrix, value_matrix, o_weight = (weights[4], weights[5], weights[6], weights[7])
    (
        hidden,
        scale_one,
        normed_input,
        query,
        q_scale,
        key_rows,
        k_scale,
        value_rows,
        rotated_query,
        key_rot,
        log_total,
        mixed,
    ) = kept[:12]
    rows = query.shape[0]
    heads = query.shape[1]
    groups = key_rows.shape[1]
    scale = HEAD_SIZE ** (-0.5)
    attended_grad = middle_grad.astype(jnp.bfloat16)
    o_term = lax.dot_general(
        attended_grad, mixed, CONTRACT_ROWS, preferred_element_type=jnp.float32
    )
    mixed_grad = jnp.dot(attended_grad, o_weight, preferred_element_type=jnp.float32).astype(
        jnp.bfloat16
    )
    mixed_grad = mixed_grad.reshape(rows, groups, heads // groups, HEAD_SIZE)
    probs = jnp.exp(scores_for(rotated_query, key_rot, allowed) - log_total)
    probs_low = probs.astype(jnp.bfloat16)
    probs_grad = jnp.einsum(
        "rkgd,ckd->kgrc", mixed_grad, value_rows, preferred_element_type=jnp.float32
    )
    value_grad = jnp.einsum(
        "kgrc,rkgd->ckd", probs_low, mixed_grad, preferred_element_type=jnp.float32
    )
    score_grad = (
        probs * (probs_grad - jnp.sum(probs * probs_grad, axis=-1, keepdims=True))
    ).astype(jnp.bfloat16)
    query_rot_grad = (
        jnp.einsum(
            "kgrc,ckd->rkgd", score_grad, key_rot, preferred_element_type=jnp.float32
        ).reshape(rows, heads, HEAD_SIZE)
        * scale
    )
    key_rot_grad = (
        jnp.einsum("kgrc,rkgd->ckd", score_grad, rotated_query, preferred_element_type=jnp.float32)
        * scale
    )
    query_turn = unrotate(query_rot_grad, cosine, sine)
    key_turn = unrotate(key_rot_grad, cosine, sine)
    q_gain_part = jnp.sum(query_turn * query * q_scale, axis=(0, 1))
    k_gain_part = jnp.sum(key_turn * key_rows * k_scale, axis=(0, 1))
    query_grad = (
        norm_back(query_turn, query, q_scale, q_gain)
        .reshape(rows, heads * HEAD_SIZE)
        .astype(jnp.bfloat16)
    )
    key_grad = (
        norm_back(key_turn, key_rows, k_scale, k_gain)
        .reshape(rows, groups * HEAD_SIZE)
        .astype(jnp.bfloat16)
    )
    value_low = value_grad.reshape(rows, groups * HEAD_SIZE).astype(jnp.bfloat16)
    q_term = lax.dot_general(
        normed_input, query_grad, CONTRACT_ROWS, preferred_element_type=jnp.float32
    )
    k_term = lax.dot_general(
        normed_input, key_grad, CONTRACT_ROWS, preferred_element_type=jnp.float32
    )
    v_term = lax.dot_general(
        normed_input, value_low, CONTRACT_ROWS, preferred_element_type=jnp.float32
    )
    normed_part = lax.dot_general(
        query_grad, q_weight, CONTRACT_COLS, preferred_element_type=jnp.float32
    )
    normed_part = normed_part + lax.dot_general(
        key_grad, key_matrix, CONTRACT_COLS, preferred_element_type=jnp.float32
    )
    normed_part = normed_part + lax.dot_general(
        value_low, value_matrix, CONTRACT_COLS, preferred_element_type=jnp.float32
    )
    attn_gain_part = jnp.sum(normed_part * hidden * scale_one, axis=0)
    normed_grad = pair_sum(normed_part)
    grad_in = middle_grad + norm_back(normed_grad, hidden, scale_one, attn_gain)
    return (grad_in, (attn_gain_part, q_gain_part, k_gain_part), (q_term, k_term, v_term, o_term))


def shards(
    block_input,
    doc_lengths,
    out_cotangent,
    attn_gain,
    q_gain,
    k_gain,
    mlp_gain,
    q_weight,
    key_matrix,
    value_matrix,
    o_weight,
    gate_weight,
    up_weight,
    down_weight,
):
    weights = (
        attn_gain[0],
        q_gain[0],
        k_gain[0],
        mlp_gain[0],
        q_weight[0],
        key_matrix[0],
        value_matrix[0],
        o_weight[0],
        gate_weight[0],
        up_weight[0],
        down_weight[0],
    )
    section = lax.axis_index("section")
    first = section == 0
    micro = doc_lengths.shape[0]
    rows = block_input.shape[0] // micro
    width = block_input.shape[1]
    inputs = block_input.reshape(micro, rows, width)
    cotangents = out_cotangent.reshape(micro, rows, width)
    offsets, allowed_all = doc_tables(doc_lengths, rows)
    cosine_all, sine_all = rope_tables(offsets, HEAD_SIZE)
    outputs = jnp.zeros((micro, rows, width), jnp.float32)
    arrived = jnp.zeros((rows, width), jnp.bfloat16)
    kept_ticks = []
    for tick in range(micro + 1):
        slot = tick - section
        valid = (slot >= 0) & (slot < micro)
        place = jnp.clip(slot, 0, micro - 1)
        hidden = jnp.where(first, pick(inputs, place), arrived).astype(jnp.float32)
        result, kept = layer_forward(
            hidden,
            pick(cosine_all, place),
            pick(sine_all, place),
            pick(allowed_all, place),
            weights,
        )
        kept_ticks.append(kept)
        outputs = lax.dynamic_update_index_in_dim(
            outputs, jnp.where(valid, result, pick(outputs, place)), place, 0
        )
        if tick < micro:
            arrived = passed_along(result.astype(jnp.bfloat16), "section", 1)

    def choose(early, late):
        return jnp.where(first, early, late)

    grads_in = jnp.zeros((micro, rows, width), jnp.float32)
    returned = jnp.zeros((rows, width), jnp.bfloat16)
    attn_totals = (
        jnp.zeros(weights[4].shape, jnp.float32),
        jnp.zeros(weights[5].shape, jnp.float32),
        jnp.zeros(weights[6].shape, jnp.float32),
        jnp.zeros(weights[7].shape, jnp.float32),
    )
    mlp_totals = (
        jnp.zeros(weights[8].shape, jnp.float32),
        jnp.zeros(weights[9].shape, jnp.float32),
        jnp.zeros(weights[10].shape, jnp.float32),
    )
    gain_totals = (
        jnp.zeros(weights[0].shape, jnp.float32),
        jnp.zeros(weights[1].shape, jnp.float32),
        jnp.zeros(weights[2].shape, jnp.float32),
        jnp.zeros(weights[3].shape, jnp.float32),
    )
    for tick in range(micro + 1):
        slot = tick - 1 + section
        valid = (slot >= 0) & (slot < micro)
        place = jnp.clip(slot, 0, micro - 1)
        grad_out = jnp.where(first, returned, pick(cotangents, place)).astype(jnp.float32)
        grad_out = jnp.where(valid, grad_out, 0.0)
        kept = jax.tree.map(choose, kept_ticks[max(tick - 1, 0)], kept_ticks[min(tick + 1, micro)])
        middle_grad, mlp_part, mlp_terms = mlp_backward(grad_out, kept, weights)
        mlp_totals = tuple((total + term for total, term in zip(mlp_totals, mlp_terms)))
        grad_in, attn_parts, attn_terms = attention_backward(
            middle_grad,
            kept,
            pick(cosine_all, place),
            pick(sine_all, place),
            pick(allowed_all, place),
            weights,
        )
        attn_totals = tuple((total + term for total, term in zip(attn_totals, attn_terms)))
        gain_totals = (
            gain_totals[0] + attn_parts[0],
            gain_totals[1] + attn_parts[1],
            gain_totals[2] + attn_parts[2],
            gain_totals[3] + mlp_part,
        )
        grads_in = lax.dynamic_update_index_in_dim(
            grads_in, jnp.where(valid, grad_in, pick(grads_in, place)), place, 0
        )
        if tick < micro:
            returned = passed_along(grad_in.astype(jnp.bfloat16), "section", -1)
    summed, gains = summed_over_dp(attn_totals + mlp_totals, gain_totals)
    attn_done = summed[:4]
    mlp_done = summed[4:]
    return (
        outputs.reshape(1, micro * rows, width),
        grads_in.reshape(1, micro * rows, width),
        gains[0][None],
        gains[1][None],
        gains[2][None],
        gains[3][None],
        attn_done[0][None],
        attn_done[1][None],
        attn_done[2][None],
        attn_done[3][None],
        mlp_done[0][None],
        mlp_done[1][None],
        mlp_done[2][None],
    )


def solution(mesh):
    return jax.shard_map(
        shards,
        mesh=mesh,
        in_specs=(
            P("dp", None),
            P("dp", None),
            P("dp", None),
            P("section", None),
            P("section", None),
            P("section", None),
            P("section", None),
            P("section", None, "tensor"),
            P("section", None, "tensor"),
            P("section", None, "tensor"),
            P("section", None, "tensor"),
            P("section", None, "tensor"),
            P("section", None, "tensor"),
            P("section", None, "tensor"),
        ),
        out_specs=(
            P("section", "dp", None),
            P("section", "dp", None),
            P("section", None),
            P("section", None),
            P("section", None),
            P("section", None),
            P("section", "dp", "tensor"),
            P("section", "dp", "tensor"),
            P("section", "dp", "tensor"),
            P("section", "dp", "tensor"),
            P("section", "dp", "tensor"),
            P("section", "dp", "tensor"),
            P("section", "dp", "tensor"),
        ),
        check_vma=False,
    )
```

```python
import functools

import jax
import jax.numpy as jnp
import numpy as np
from jax import lax
from jax.experimental import pallas as pl
from jax.experimental.pallas import tpu as pltpu
from jax.sharding import PartitionSpec as P

EPSILON = 1e-06
THETA = 1000000.0
HEAD = 128
ROW = 256
WIDTH = 1024
BLOCK = 32
SCORE_SCALE = HEAD ** (-0.5)
MESH = pl.DeviceIdType.MESH
BF16, F32 = jnp.bfloat16, jnp.float32
NT = (((1,), (1,)), ((), ()))
TN = (((0,), (0,)), ((), ()))

CHUNK = 512
GATE, UP, DOWN, QUERY, KEY, VALUE, OUT = 0, 3, 6, 9, 11, 12, 13
CHUNKS = 15
MLP_CHUNKS = 9
ORDERS = (("z", "y", "x"), ("y", "z", "x"))
COUNTS = (8, 7)
LAGS = (0, 0, 2, 2, 4, 6, 6, 8)
GAIN_ROWS = 24


def remote(src, dst, send_sem, recv_sem, device):
    return pltpu.make_async_remote_copy(
        src_ref=src,
        dst_ref=dst,
        send_sem=send_sem,
        recv_sem=recv_sem,
        device_id=device,
        device_id_type=MESH,
    )


def dot(left, right, form=None):
    if form is None:
        return jnp.dot(left, right, preferred_element_type=F32)
    return lax.dot_general(left, right, form, preferred_element_type=F32)


class Place:
    def __init__(self):
        dp = lax.axis_index("dp")
        self.at = {"z": dp // 8, "x": dp // 4 % 2, "y": dp % 4}

    def device(self, axis, index):
        at = {**self.at, axis: index}
        return {"dp": at["z"] * 8 + at["x"] * 4 + at["y"]}


def ring_phases(order):
    found, done = [], []
    for axis in order:
        left = [name for name in ("z", "x", "y") if name not in done and name != axis]
        halved = None if axis == "x" else "x" if "x" in left else left[0]
        shape = []
        for name in left:
            size = 2 if name == "x" else 4
            shape.append(size // 2 if name == halved else size)
        found.append((axis, tuple(done), halved, (*shape, 32, CHUNK)))
        done.append(axis)
    return found


def ring_scratch(order, count):
    found = []
    for _, _, halved, shape in ring_phases(order):
        parts = 6 if halved else 1
        found.append(pltpu.VMEM((count, parts, *shape), BF16))
        found.append(pltpu.SemaphoreType.DMA((count, parts)))
        found.append(pltpu.SemaphoreType.DMA((count, parts)))
    return found


def ring_stages(order, grads, first, scratch, place, finish):
    stages = []
    for step, (axis, done, halved, _) in enumerate(ring_phases(order)):
        arrived, send_sem, recv_sem = scratch[3 * step : 3 * step + 3]
        mine = place.at[axis]

        def where(i, index, half, axis=axis, done=done, halved=halved):
            found = [2 * i + first]
            for name in ("z", "x", "y"):
                if name in done:
                    found.append(place.at[name])
                elif name == axis:
                    found.append(index)
                elif name == halved:
                    size = 1 if name == "x" else 2
                    found.append(pl.ds(half * size, size))
                else:
                    found.append(slice(None))
            return tuple(found)

        def put(i, half, total, step=step, mine=mine, where=where):
            if step == 2:
                finish(2 * i + first, total)
            else:
                grads[where(i, mine, half)] = total.astype(BF16)

        if halved is None:

            def swap(
                i, where=where, arrived=arrived, send_sem=send_sem, recv_sem=recv_sem, mine=mine, axis=axis
            ):
                return remote(
                    grads.at[where(i, 1 - mine, 0)],
                    arrived.at[i, 0],
                    send_sem.at[i, 0],
                    recv_sem.at[i, 0],
                    place.device(axis, 1 - mine),
                )

            def start(i, swap=swap):
                swap(i).start()

            def end(i, swap=swap, arrived=arrived, where=where, mine=mine, put=put):
                swap(i).wait()
                put(i, 0, grads[where(i, mine, 0)].astype(F32) + arrived[i, 0].astype(F32))

            stages += [start, end]
            continue

        right, left = lax.rem(mine + 1, 4), lax.rem(mine + 3, 4)
        across = lax.rem(mine + 2, 4)
        sends = (
            (across, 0, right),
            (across, 1, left),
            (right, 1, right),
            (left, 0, left),
            (right, 0, right),
            (left, 1, left),
        )

        def send(
            i, k, where=where, arrived=arrived, send_sem=send_sem, recv_sem=recv_sem, axis=axis, sends=sends
        ):
            index, half, to = sends[k]
            return remote(
                grads.at[where(i, index, half)],
                arrived.at[i, k],
                send_sem.at[i, k],
                recv_sem.at[i, k],
                place.device(axis, to),
            )

        def start(i, send=send):
            for k in range(4):
                send(i, k).start()

        def pass_on(i, send=send, arrived=arrived, where=where, sends=sends):
            for k in (0, 1):
                send(i, k).wait_recv()
                index, half, _ = sends[4 + k]
                at = where(i, index, half)
                grads[at] = (grads[at].astype(F32) + arrived[i, k].astype(F32)).astype(BF16)
                send(i, 4 + k).start()

        def end(i, send=send, arrived=arrived, where=where, mine=mine, put=put):
            for k in range(2, 6):
                send(i, k).wait_recv()
            for k in range(6):
                send(i, k).wait_send()
            for half in (0, 1):
                own = grads[where(i, mine, half)].astype(F32)
                near = arrived[i, 4 - 2 * half].astype(F32)
                far = arrived[i, 3 + 2 * half].astype(F32)
                put(i, half, own + near + far)

        stages += [start, pass_on, end]
    return stages


def gain_scratch():
    found = [pltpu.VMEM((4, GAIN_ROWS, 128), F32)]
    for size in (4, 4, 2, 2):
        found.append(pltpu.SemaphoreType.DMA((size,)))
        found.append(pltpu.SemaphoreType.DMA((size,)))
        found.append(pltpu.VMEM((size, GAIN_ROWS, 128), F32))
    return found


def gain_axes(place):
    return (
        (4, place.at["y"], lambda k: place.device("y", k)),
        (4, place.at["z"], lambda k: place.device("z", k)),
        (2, place.at["x"], lambda k: place.device("x", k)),
        (2, lax.axis_index("tensor"), lambda k: {"tensor": k}),
    )


def gain_stages(total_ref, scratch, place):
    held = scratch[0]
    stages = []
    for step, (size, mine, device) in enumerate(gain_axes(place)):
        send_sem, recv_sem, slots = scratch[1 + 3 * step : 4 + 3 * step]
        src = held.at[step]
        dst = total_ref if step == 3 else held.at[step + 1]

        def send(k, src=src, slots=slots, send_sem=send_sem, recv_sem=recv_sem, size=size, mine=mine, device=device):
            to = lax.rem(mine + k, size)
            return remote(src, slots.at[mine], send_sem.at[k], recv_sem.at[mine], device(to))

        def arrival(k, src=src, slots=slots, send_sem=send_sem, recv_sem=recv_sem, size=size, mine=mine, device=device):
            frm = lax.rem(mine + k, size)
            return remote(src, slots.at[frm], send_sem.at[k], recv_sem.at[frm], device(frm))

        def start(i, send=send, src=src, slots=slots, size=size, mine=mine):
            slots[mine] = src[...]
            for k in range(1, size):
                send(k).start()

        def end(i, send=send, arrival=arrival, slots=slots, size=size, dst=dst):
            for k in range(1, size):
                arrival(k).wait_recv()
                send(k).wait_send()
            total = slots[0]
            for k in range(1, size):
                total = total + slots[k]
            dst[...] = total

        stages += [start, end]
    return stages


SCRATCH = dict(
    weights=pltpu.VMEM((CHUNKS, 4, 2, 4, 32, CHUNK), BF16),
    hidden=pltpu.VMEM((2 * ROW, WIDTH), BF16),
    normed=pltpu.VMEM((2 * ROW, WIDTH), BF16),
    heads=pltpu.VMEM((2 * ROW, 3072), BF16),
    query_rot=pltpu.VMEM((2 * ROW, 1024), BF16),
    key_rot=pltpu.VMEM((2 * ROW, 512), BF16),
    probs=pltpu.VMEM((2, 8, ROW, ROW), BF16),
    middle=pltpu.VMEM((2 * ROW, WIDTH), F32),
    normed_two=pltpu.VMEM((2 * ROW, WIDTH), BF16),
    ff=pltpu.VMEM((3, 2 * ROW, 1536), BF16),
    grad=pltpu.VMEM((2 * ROW, WIDTH), BF16),
    attended_grad=pltpu.VMEM((2 * ROW, WIDTH), BF16),
    mixed_grad=pltpu.VMEM((ROW, 1024), BF16),
    turned=pltpu.VMEM((2, WIDTH, 2 * ROW), BF16),
    mine=pltpu.VMEM((2, 4, ROW, 256), BF16),
    theirs=pltpu.VMEM((2, 4, ROW, 256), BF16),
    leaving=pltpu.VMEM((2 * ROW, WIDTH), BF16),
    stage=pltpu.VMEM((2 * ROW, WIDTH), F32),
    cosine=pltpu.VMEM((2 * ROW, HEAD), F32),
    sine=pltpu.VMEM((2 * ROW, HEAD), F32),
    bias=pltpu.VMEM((2 * ROW, ROW), F32),
    scale_one=pltpu.VMEM((2 * ROW, 128), F32),
    scale_two=pltpu.VMEM((2 * ROW, 128), F32),
    wide=pltpu.VMEM((2, ROW, CHUNK), F32),
    weight_sem=pltpu.SemaphoreType.DMA((CHUNKS,)),
    input_sem=pltpu.SemaphoreType.DMA((2,)),
    output_sem=pltpu.SemaphoreType.DMA((2, 2)),
    mine_sem=pltpu.SemaphoreType.DMA((2, 4)),
    theirs_sem=pltpu.SemaphoreType.DMA((2, 4)),
    cross_send=pltpu.SemaphoreType.DMA((2, 2)),
    cross_recv=pltpu.SemaphoreType.DMA((2, 2)),
    relay_send=pltpu.SemaphoreType.DMA((2, 2)),
    relay_recv=pltpu.SemaphoreType.DMA((2, 2)),
)


def rows_of(micro):
    return pl.ds(pl.multiple_of(micro * ROW, ROW), ROW)


def over_rows(micro, body):
    def one(block, carry):
        body(
            pl.ds(pl.multiple_of(micro * ROW + block * BLOCK, BLOCK), BLOCK),
            pl.ds(pl.multiple_of(block * BLOCK, BLOCK), BLOCK),
        )
        return carry

    lax.fori_loop(0, ROW // BLOCK, one, 0)


def columns(index, size=CHUNK):
    if isinstance(index, int):
        return pl.ds(index * size, size)
    return pl.ds(pl.multiple_of(index * size, size), size)


def inverse_rms(value):
    return lax.rsqrt(jnp.mean(value * value, axis=-1, keepdims=True) + EPSILON)


def kernel(
    lengths,
    block_input,
    cotangent,
    attn_gain,
    q_gain,
    k_gain,
    mlp_gain,
    q_weight,
    key_matrix,
    value_matrix,
    o_weight,
    gate_weight,
    up_weight,
    down_weight,
    table,
    hidden_out,
    hidden_grad,
    grads_out,
    gains_out,
    *scratch,
):
    s = dict(zip(SCRATCH, scratch))
    scratch = scratch[len(SCRATCH) :]
    weights, hidden, normed, heads = s["weights"], s["hidden"], s["normed"], s["heads"]
    query_rot, key_rot, probs = s["query_rot"], s["key_rot"], s["probs"]
    middle, normed_two, ff, grad = s["middle"], s["normed_two"], s["ff"], s["grad"]
    attended_grad, mixed_grad, turned = s["attended_grad"], s["mixed_grad"], s["turned"]
    mine, theirs, leaving, stage = s["mine"], s["theirs"], s["leaving"], s["stage"]
    cosine, sine, bias = s["cosine"], s["sine"], s["bias"]
    scale_one, scale_two, wide = s["scale_one"], s["scale_two"], s["wide"]
    place = Place()
    section, tensor = lax.axis_index("section"), lax.axis_index("tensor")
    over_tensor, over_section = {"tensor": 1 - tensor}, {"section": 1 - section}

    barrier = pltpu.get_barrier_semaphore()
    for size, own, device in gain_axes(place):
        for k in range(1, size):
            pl.semaphore_signal(
                barrier, inc=1, device_id=device(lax.rem(own + k, size)), device_id_type=MESH
            )
    pl.semaphore_signal(barrier, inc=1, device_id=over_section, device_id_type=MESH)

    sources = (
        [(q_weight, 0), (q_weight, 1), (key_matrix, 0), (value_matrix, 0), (o_weight, 0), (o_weight, 1)],
        [(ref, k) for ref in (gate_weight, up_weight, down_weight) for k in range(3)],
    )

    def load(chunk):
        ref, part = sources[1][chunk] if chunk < MLP_CHUNKS else sources[0][chunk - MLP_CHUNKS]
        return pltpu.make_async_copy(
            ref.at[:, :, :, :, columns(part)], weights.at[chunk], s["weight_sem"].at[chunk]
        )

    def load_input(micro):
        rows = rows_of(micro)
        return pltpu.make_async_copy(block_input.at[rows], hidden.at[rows], s["input_sem"].at[micro])

    def load_cotangent(micro):
        rows = rows_of(micro)
        return pltpu.make_async_copy(cotangent.at[rows], grad.at[rows], s["input_sem"].at[micro])

    @pl.when(section == 0)
    def _():
        load_input(0).start()
        load_input(1).start()

    for chunk in (9, 10, 11, 12, 13, 14, 0, 3, 1, 4, 2, 5, 6, 7, 8):
        load(chunk).start()

    @pl.when(section == 1)
    def _():
        load_cotangent(0).start()
        load_cotangent(1).start()

    gains = scratch[-13]
    gains[0] = jnp.zeros((GAIN_ROWS, 128), F32)

    def tables(micro, carry):
        rows = rows_of(micro)
        ends = [lengths[micro, 0]]
        for k in (1, 2):
            ends.append(ends[-1] + lengths[micro, k])

        def begins(shape):
            at = lax.broadcasted_iota(jnp.int32, shape, 0)
            found = jnp.zeros(shape, jnp.int32)
            for end in ends:
                found = jnp.where(at >= end, end, found)
            return at, found

        at, begin = begins((ROW, HEAD))
        chosen = (at - begin) == lax.broadcasted_iota(jnp.int32, (ROW, HEAD), 1)
        both = dot(chosen.astype(F32).astype(BF16), table[...])
        cosine[rows] = both[:, :128] + both[:, 128:256]
        sine[rows] = both[:, 256:384] + both[:, 384:]
        at, begin = begins((ROW, ROW))
        column = lax.broadcasted_iota(jnp.int32, (ROW, ROW), 1)
        bias[rows] = jnp.where((column >= begin) & (column <= at), 0.0, -1e9)
        return carry

    lax.fori_loop(0, 2, tables, 0)
    pl.semaphore_wait(barrier, 9)

    def pair(slot, part):
        return remote(
            mine.at[slot, part],
            theirs.at[slot, part],
            s["mine_sem"].at[slot, part],
            s["theirs_sem"].at[slot, part],
            over_tensor,
        )

    def pair_start(slot, part, value):
        mine[slot, part] = value.astype(BF16)
        pair(slot, part).start()

    def pair_wait(slot):
        for part in range(4):
            pair(slot, part).wait()

    def pair_sum(slot, block):
        return jnp.concatenate(
            [
                mine[slot, part, block].astype(F32) + theirs[slot, part, block].astype(F32)
                for part in range(4)
            ],
            axis=1,
        )

    def half_rows(micro):
        return pl.ds(pl.multiple_of(micro * ROW + tensor * (ROW // 2), ROW // 2), ROW // 2)

    def cross(way, micro):
        rows = half_rows(micro)
        into = hidden if way == 0 else grad
        return remote(
            leaving.at[rows],
            into.at[rows],
            s["cross_send"].at[way, micro],
            s["cross_recv"].at[way, micro],
            over_section,
        )

    def arrive(way, micro):
        rows = half_rows(micro)
        into = hidden if way == 0 else grad
        cross(way, micro).wait_recv()
        relay = remote(
            into.at[rows],
            into.at[rows],
            s["relay_send"].at[way, micro],
            s["relay_recv"].at[way, micro],
            over_tensor,
        )
        relay.start()
        relay.wait()

    def output(way, micro):
        rows = rows_of(micro)
        into = hidden_out if way == 0 else hidden_grad
        return pltpu.make_async_copy(stage.at[rows], into.at[rows], s["output_sem"].at[way, micro])

    def weight(chunk):
        return weights[chunk].reshape(WIDTH, CHUNK)

    def weight_part(chunk, part):
        return weights[chunk, part].reshape(256, CHUNK)

    def once(micro, chunks):
        @pl.when(micro == 0)
        def _():
            for chunk in chunks:
                load(chunk).wait()

    def rotated(value, cos, sin):
        return value * cos + pltpu.roll(value, HEAD // 2, 1) * sin

    def unrotated(value, cos, sin):
        return value * cos - pltpu.roll(value, HEAD // 2, 1) * sin

    def forward(micro, carry):
        rows = rows_of(micro)

        @pl.when(section == 0)
        def _():
            load_input(micro).wait()

        @pl.when(section == 1)
        def _():
            arrive(0, micro)

        def norm_one(at, block):
            value = hidden[at].astype(F32)
            scale = inverse_rms(value)
            normed[at] = (value * scale * attn_gain[...]).astype(BF16)
            scale_one[at] = jnp.broadcast_to(scale, (BLOCK, 128))

        over_rows(micro, norm_one)
        once(micro, range(QUERY, OUT))
        for chunk in range(4):
            wide[0] = dot(normed[rows], weight(QUERY + chunk))
            if chunk == 3:
                heads[rows, columns(chunk)] = wide[0].astype(BF16)
                continue
            gain = q_gain if chunk < 2 else k_gain
            for k in range(4):
                value = wide[0, :, columns(k, HEAD)]
                heads[rows, columns(chunk * 4 + k, HEAD)] = value.astype(BF16)
                turn = rotated(value * inverse_rms(value) * gain[...], cosine[rows], sine[rows])
                if chunk < 2:
                    query_rot[rows, columns(chunk * 4 + k, HEAD)] = turn.astype(BF16)
                else:
                    key_rot[rows, columns(k, HEAD)] = turn.astype(BF16)

        def attend(group, carry):
            keys = key_rot[rows, columns(group, HEAD)]
            values = heads[rows, columns(12 + group, HEAD)]
            for k in range(2):
                head = 2 * group + k
                scores = dot(query_rot[rows, columns(head, HEAD)], keys, NT) * SCORE_SCALE + bias[rows]
                peak = jnp.max(scores, axis=-1, keepdims=True)
                raw = jnp.exp(scores - peak)
                low = (raw / jnp.sum(raw, axis=-1, keepdims=True)).astype(BF16)
                probs[micro, head] = low
                heads[rows, columns(16 + head, HEAD)] = dot(low, values).astype(BF16)
            return carry

        lax.fori_loop(0, 4, attend, 0)
        once(micro, (OUT, OUT + 1))

        def attended(part, carry):
            value = dot(heads[rows, columns(4)], weight_part(OUT, part), NT)
            value = value + dot(heads[rows, columns(5)], weight_part(OUT + 1, part), NT)
            pair_start(0, part, value)
            return carry

        lax.fori_loop(0, 4, attended, 0)
        pair_wait(0)

        def norm_two(at, block):
            value = hidden[at].astype(F32) + pair_sum(0, block)
            middle[at] = value
            scale = inverse_rms(value)
            normed_two[at] = (value * scale * mlp_gain[...]).astype(BF16)
            scale_two[at] = jnp.broadcast_to(scale, (BLOCK, 128))

        over_rows(micro, norm_two)
        once(micro, range(QUERY))

        def hidden_units(chunk, carry):
            wide[0] = dot(normed_two[rows], weight(GATE + chunk))
            wide[1] = dot(normed_two[rows], weight(UP + chunk))

            def silu(at, block):
                gate, up = wide[0, block], wide[1, block]
                ff[0, at, columns(chunk)] = gate.astype(BF16)
                ff[1, at, columns(chunk)] = up.astype(BF16)
                ff[2, at, columns(chunk)] = (gate * jax.nn.sigmoid(gate) * up).astype(BF16)

            over_rows(micro, silu)
            return carry

        lax.fori_loop(0, 3, hidden_units, 0)

        def moved(part, carry):
            value = dot(ff[2, rows, columns(0)], weight_part(DOWN, part), NT)
            for k in (1, 2):
                value = value + dot(ff[2, rows, columns(k)], weight_part(DOWN + k, part), NT)
            pair_start(1, part, value)
            return carry

        lax.fori_loop(0, 4, moved, 0)
        pair_wait(1)

        def result(at, block):
            value = middle[at] + pair_sum(1, block)
            stage[at] = value
            leaving[at] = value.astype(BF16)

        over_rows(micro, result)
        output(0, micro).start()

        @pl.when(section == 0)
        def _():
            cross(0, micro).start()

        return carry

    lax.fori_loop(0, 2, forward, 0)

    def norm_back(total, value, scale, gain):
        inner = total * gain
        return scale * inner - value * (scale * scale * scale) * jnp.mean(
            inner * value, axis=-1, keepdims=True
        )

    def add_gain(row, value):
        gains[0, row : row + 1] = gains[0, row : row + 1] + value

    def add_gains(row, part, value):
        for k in range(2):
            at = pl.ds(row + part * 2 + k, 1)
            gains[0, at] = gains[0, at] + value[:, k * 128 : (k + 1) * 128]

    def turn(slot, value):
        for k in range(4):
            turned[slot, k * 256 : (k + 1) * 256] = value[:, columns(k, 256)].T

    def weight_grad(chunk, slot, right):
        for part in range(4):
            value = dot(turned[slot, columns(part, 256)], right)
            weights[chunk, part] = value.astype(BF16).reshape(2, 4, 32, CHUNK)

    def finish(chunk, total):
        if total.shape[0] == 1:
            total = total[0]
        grads_out[chunk] = total

    rings = []
    for first, (order, count) in enumerate(zip(ORDERS, COUNTS)):
        own, scratch = scratch[:9], scratch[9:]
        rings.append((count, LAGS, ring_stages(order, weights, first, own, place, finish)))

    def ring_start(chunk):
        for first in (0, 1):

            @pl.when(lax.rem(chunk, 2) == first)
            def _(first=first):
                rings[first][2][0]((chunk - first) // 2)

    def backward(micro, carry):
        rows = rows_of(micro)

        @pl.when(section == 0)
        def _():
            arrive(1, micro)
            cross(0, micro).wait_send()

        @pl.when(section == 1)
        def _():
            load_cotangent(micro).wait()

        def hidden_back(chunk, carry):
            wide[0] = dot(grad[rows], weight(DOWN + chunk))

            def silu_back(at, block):
                act_grad = wide[0, block]
                gate, up = ff[0, at, columns(chunk)].astype(F32), ff[1, at, columns(chunk)].astype(F32)
                sigma = jax.nn.sigmoid(gate)
                passed = act_grad * sigma
                ff[0, at, columns(chunk)] = (passed * up * (1.0 + gate * (1.0 - sigma))).astype(BF16)
                ff[1, at, columns(chunk)] = (passed * gate).astype(BF16)

            over_rows(micro, silu_back)
            return carry

        lax.fori_loop(0, 3, hidden_back, 0)

        def normed_two_back(part, carry):
            value = dot(ff[0, rows, columns(0)], weight_part(GATE, part), NT)
            for k in (1, 2):
                value = value + dot(ff[0, rows, columns(k)], weight_part(GATE + k, part), NT)
            for k in range(3):
                value = value + dot(ff[1, rows, columns(k)], weight_part(UP + k, part), NT)
            pair_start(0, part, value)
            scaled = middle[rows, columns(part, 256)] * scale_two[rows, :1]
            add_gains(8, part, jnp.sum(value * scaled, axis=0, keepdims=True))
            return carry

        lax.fori_loop(0, 4, normed_two_back, 0)
        pair_wait(0)
        output(0, micro).wait()

        def middle_back(at, block):
            value = grad[at].astype(F32) + norm_back(
                pair_sum(0, block), middle[at], scale_two[at, :1], mlp_gain[...]
            )
            stage[at] = value
            attended_grad[at] = value.astype(BF16)

        over_rows(micro, middle_back)

        @pl.when(micro == 1)
        def _():
            turn(0, normed_two)
            turn(1, grad)

            def one(chunk, carry):
                weight_grad(chunk, chunk // 6, ff[chunk // 3, :, columns(lax.rem(chunk, 3))])
                ring_start(chunk)
                return carry

            lax.fori_loop(0, MLP_CHUNKS, one, 0)

        for k in range(2):
            mixed_grad[:, columns(k)] = dot(attended_grad[rows], weight(OUT + k)).astype(BF16)

        def attend_back(group, carry):
            cos, sin = cosine[rows], sine[rows]
            keys = key_rot[rows, columns(group, HEAD)]
            values = heads[rows, columns(12 + group, HEAD)]
            key_rot_grad = jnp.zeros((ROW, HEAD), F32)
            value_grad = jnp.zeros((ROW, HEAD), F32)
            for k in range(2):
                head = 2 * group + k
                here = columns(head, HEAD)
                low = probs[micro, head]
                chance = low.astype(F32)
                out_grad = mixed_grad[:, here]
                weighted = chance * dot(out_grad, values, NT)
                score_grad = (weighted - chance * jnp.sum(weighted, axis=-1, keepdims=True)).astype(BF16)
                value_grad = value_grad + dot(low, out_grad, TN)
                key_rot_grad = key_rot_grad + dot(score_grad, query_rot[rows, here], TN)
                turn_grad = unrotated(dot(score_grad, keys) * SCORE_SCALE, cos, sin)
                query = heads[rows, here].astype(F32)
                scale = inverse_rms(query)
                add_gain(16, jnp.sum(turn_grad * query * scale, axis=0, keepdims=True))
                heads[rows, here] = norm_back(turn_grad, query, scale, q_gain[...]).astype(BF16)
            turn_grad = unrotated(key_rot_grad * SCORE_SCALE, cos, sin)
            here = columns(8 + group, HEAD)
            key = heads[rows, here].astype(F32)
            scale = inverse_rms(key)
            add_gain(17, jnp.sum(turn_grad * key * scale, axis=0, keepdims=True))
            heads[rows, here] = norm_back(turn_grad, key, scale, k_gain[...]).astype(BF16)
            heads[rows, columns(12 + group, HEAD)] = value_grad.astype(BF16)
            return carry

        lax.fori_loop(0, 4, attend_back, 0)

        def normed_back(part, carry):
            value = dot(heads[rows, columns(0)], weight_part(QUERY, part), NT)
            for k in (1, 2, 3):
                value = value + dot(heads[rows, columns(k)], weight_part(QUERY + k, part), NT)
            pair_start(1, part, value)
            scaled = hidden[rows, columns(part, 256)].astype(F32) * scale_one[rows, :1]
            add_gains(0, part, jnp.sum(value * scaled, axis=0, keepdims=True))
            return carry

        lax.fori_loop(0, 4, normed_back, 0)
        pair_wait(1)

        def hidden_back_end(at, block):
            value = stage[at] + norm_back(
                pair_sum(1, block), hidden[at].astype(F32), scale_one[at, :1], attn_gain[...]
            )
            stage[at] = value
            leaving[at] = value.astype(BF16)

        over_rows(micro, hidden_back_end)
        output(1, micro).start()

        @pl.when(section == 1)
        def _():
            cross(1, micro).start()

        return carry

    lax.fori_loop(0, 2, backward, 0)

    turn(0, normed)
    turn(1, attended_grad)

    def attention_grad(chunk, carry):
        weight_grad(MLP_CHUNKS + chunk, chunk // 4, heads[:, columns(chunk)])
        ring_start(MLP_CHUNKS + chunk)
        return carry

    lax.fori_loop(0, CHUNKS - MLP_CHUNKS, attention_grad, 0)

    groups = [(count, (None, *lags[1:]), stages) for count, lags, stages in rings]
    groups.append((1, (0, 2, 2, 4, 4, 6, 6, 8), gain_stages(gains_out, scratch, place)))

    def advance(now, carry):
        for step in range(8):
            for count, lags, stages in groups:
                if lags[step] is None:
                    continue
                i = now - lags[step]

                @pl.when((i >= 0) & (i < count))
                def _(i=i, run=stages[step]):
                    run(i)

        return carry

    lax.fori_loop(0, max(count + lags[-1] for count, lags, _ in groups), advance, 0)

    for micro in range(2):
        output(1, micro).wait()

        @pl.when(section == 1)
        def _(micro=micro):
            cross(1, micro).wait_send()


def rope_table():
    half = HEAD // 2
    rates = THETA ** (-2.0 * np.arange(half) / HEAD)
    angle = np.arange(HEAD)[:, None] * np.concatenate([rates, rates])[None]
    sign = np.where(np.arange(HEAD) < half, -1.0, 1.0)
    parts = []
    for value in (np.cos(angle), np.sin(angle) * sign):
        high = value.astype(jnp.bfloat16)
        parts += [high, (value - high.astype(np.float64)).astype(jnp.bfloat16)]
    return jnp.asarray(np.concatenate(parts, axis=1))


def by_place(weight):
    return weight.reshape(4, 2, 4, 32, weight.shape[-1])


def shards(
    block_input,
    doc_lengths,
    out_cotangent,
    attn_gain,
    q_gain,
    k_gain,
    mlp_gain,
    q_weight,
    key_matrix,
    value_matrix,
    o_weight,
    gate_weight,
    up_weight,
    down_weight,
):
    vmem = pl.BlockSpec(memory_space=pltpu.VMEM)
    smem = pl.BlockSpec(memory_space=pltpu.SMEM)
    anywhere = pl.BlockSpec(memory_space=pl.ANY)
    scratch = list(SCRATCH.values())
    for order, count in zip(ORDERS, COUNTS):
        scratch += ring_scratch(order, count)
    scratch += gain_scratch()
    full = jax.ShapeDtypeStruct(block_input.shape, F32)
    outputs, grads_in, grads, gains = pl.pallas_call(
        kernel,
        out_shape=(
            full,
            full,
            jax.ShapeDtypeStruct((CHUNKS, 32, CHUNK), F32),
            jax.ShapeDtypeStruct((GAIN_ROWS, 128), F32),
        ),
        in_specs=[smem, anywhere, anywhere] + [vmem] * 4 + [anywhere] * 7 + [vmem],
        out_specs=[anywhere, anywhere, vmem, vmem],
        scratch_shapes=scratch,
        compiler_params=pltpu.CompilerParams(
            collective_id=0, has_side_effects=True, vmem_limit_bytes=64 * 2**20 - 2**16
        ),
    )(
        doc_lengths,
        block_input,
        out_cotangent,
        attn_gain,
        q_gain,
        k_gain,
        mlp_gain,
        by_place(q_weight),
        by_place(key_matrix),
        by_place(value_matrix),
        by_place(o_weight),
        by_place(gate_weight),
        by_place(up_weight),
        by_place(down_weight),
        rope_table(),
    )

    def matrix(first, count):
        return jnp.concatenate([grads[first + k] for k in range(count)], axis=1)[None]

    flat = gains.reshape(1, -1)
    return (
        outputs[None],
        grads_in[None],
        flat[:, :1024],
        flat[:, 2048:2176],
        flat[:, 2176:2304],
        flat[:, 1024:2048],
        matrix(QUERY, 2),
        matrix(KEY, 1),
        matrix(VALUE, 1),
        matrix(OUT, 2),
        matrix(GATE, 3),
        matrix(UP, 3),
        matrix(DOWN, 3),
    )


def solution(mesh):
    weight = P("section", None, "tensor")
    gain = P("section", None)
    tokens = P("section", "dp", None)
    grad = P("section", "dp", "tensor")
    return jax.shard_map(
        shards,
        mesh=mesh,
        in_specs=(P("dp", None),) * 3 + (gain,) * 4 + (weight,) * 7,
        out_specs=(tokens,) * 2 + (gain,) * 4 + (grad,) * 7,
        check_vma=False,
    )
```

```python
import functools

import jax
import jax.numpy as jnp
import numpy as np
from jax import lax
from jax.experimental import pallas as pl
from jax.experimental.pallas import tpu as pltpu
from jax.sharding import PartitionSpec as P

EPSILON = 1e-06
THETA = 1000000.0
HEAD = 128
ROW = 256
WIDTH = 1024
BLOCK = 32
SCORE_SCALE = HEAD ** (-0.5)
LOG2_E = 1.4426950408889634
MESH = pl.DeviceIdType.MESH
BF16, F32 = jnp.bfloat16, jnp.float32
NT = (((1,), (1,)), ((), ()))
TN = (((0,), (0,)), ((), ()))

CHUNK = 512
GATE, UP, DOWN, QUERY, KEY, VALUE, OUT = 0, 3, 6, 9, 11, 12, 13
CHUNKS = 15
MLP_CHUNKS = 9
ORDERS = (("z", "y", "x"), ("y", "z", "x"))
COUNTS = (8, 7)
LAGS = (0, 0, 2, 2, 4, 6, 6, 8)
GAIN_ROWS = 24


def remote(src, dst, send_sem, recv_sem, device):
    return pltpu.make_async_remote_copy(
        src_ref=src,
        dst_ref=dst,
        send_sem=send_sem,
        recv_sem=recv_sem,
        device_id=device,
        device_id_type=MESH,
    )


def dot(left, right, form=None):
    if form is None:
        return jnp.dot(left, right, preferred_element_type=F32)
    return lax.dot_general(left, right, form, preferred_element_type=F32)


class Place:
    def __init__(self):
        dp = lax.axis_index("dp")
        self.at = {"z": dp // 8, "x": dp // 4 % 2, "y": dp % 4}

    def device(self, axis, index):
        at = {**self.at, axis: index}
        return {"dp": at["z"] * 8 + at["x"] * 4 + at["y"]}


def ring_phases(order):
    found, done = [], []
    for axis in order:
        left = [name for name in ("z", "x", "y") if name not in done and name != axis]
        halved = None if axis == "x" else "x" if "x" in left else left[0]
        shape = []
        for name in left:
            size = 2 if name == "x" else 4
            shape.append(size // 2 if name == halved else size)
        found.append((axis, tuple(done), halved, (*shape, 32, CHUNK)))
        done.append(axis)
    return found


def ring_scratch(order, count):
    found = []
    for _, _, halved, shape in ring_phases(order):
        parts = 6 if halved else 1
        found.append(pltpu.VMEM((count, parts, *shape), BF16))
        found.append(pltpu.SemaphoreType.DMA((count, parts)))
        found.append(pltpu.SemaphoreType.DMA((count, parts)))
    return found


def ring_stages(order, grads, first, scratch, place, finish):
    stages = []
    for step, (axis, done, halved, _) in enumerate(ring_phases(order)):
        arrived, send_sem, recv_sem = scratch[3 * step : 3 * step + 3]
        mine = place.at[axis]

        def where(i, index, half, axis=axis, done=done, halved=halved):
            found = [2 * i + first]
            for name in ("z", "x", "y"):
                if name in done:
                    found.append(place.at[name])
                elif name == axis:
                    found.append(index)
                elif name == halved:
                    size = 1 if name == "x" else 2
                    found.append(pl.ds(half * size, size))
                else:
                    found.append(slice(None))
            return tuple(found)

        def put(i, half, total, step=step, mine=mine, where=where):
            if step == 2:
                finish(2 * i + first, total)
            else:
                grads[where(i, mine, half)] = total.astype(BF16)

        if halved is None:

            def swap(
                i, where=where, arrived=arrived, send_sem=send_sem, recv_sem=recv_sem, mine=mine, axis=axis
            ):
                return remote(
                    grads.at[where(i, 1 - mine, 0)],
                    arrived.at[i, 0],
                    send_sem.at[i, 0],
                    recv_sem.at[i, 0],
                    place.device(axis, 1 - mine),
                )

            def start(i, swap=swap):
                swap(i).start()

            def end(i, swap=swap, arrived=arrived, where=where, mine=mine, put=put):
                swap(i).wait()
                put(i, 0, grads[where(i, mine, 0)].astype(F32) + arrived[i, 0].astype(F32))

            stages += [start, end]
            continue

        right, left = lax.rem(mine + 1, 4), lax.rem(mine + 3, 4)
        across = lax.rem(mine + 2, 4)
        sends = (
            (across, 0, right),
            (across, 1, left),
            (right, 1, right),
            (left, 0, left),
            (right, 0, right),
            (left, 1, left),
        )

        def send(
            i, k, where=where, arrived=arrived, send_sem=send_sem, recv_sem=recv_sem, axis=axis, sends=sends
        ):
            index, half, to = sends[k]
            return remote(
                grads.at[where(i, index, half)],
                arrived.at[i, k],
                send_sem.at[i, k],
                recv_sem.at[i, k],
                place.device(axis, to),
            )

        def start(i, send=send):
            for k in range(4):
                send(i, k).start()

        def pass_on(i, send=send, arrived=arrived, where=where, sends=sends):
            for k in (0, 1):
                send(i, k).wait_recv()
                index, half, _ = sends[4 + k]
                at = where(i, index, half)
                grads[at] = (grads[at].astype(F32) + arrived[i, k].astype(F32)).astype(BF16)
                send(i, 4 + k).start()

        def end(i, send=send, arrived=arrived, where=where, mine=mine, put=put):
            for k in range(2, 6):
                send(i, k).wait_recv()
            for k in range(6):
                send(i, k).wait_send()
            for half in (0, 1):
                own = grads[where(i, mine, half)].astype(F32)
                near = arrived[i, 4 - 2 * half].astype(F32)
                far = arrived[i, 3 + 2 * half].astype(F32)
                put(i, half, own + near + far)

        stages += [start, pass_on, end]
    return stages


def gain_scratch():
    found = [pltpu.VMEM((4, GAIN_ROWS, 128), F32)]
    for size in (4, 4, 2, 2):
        found.append(pltpu.SemaphoreType.DMA((size,)))
        found.append(pltpu.SemaphoreType.DMA((size,)))
        found.append(pltpu.VMEM((size, GAIN_ROWS, 128), F32))
    return found


def gain_axes(place):
    return (
        (4, place.at["y"], lambda k: place.device("y", k)),
        (4, place.at["z"], lambda k: place.device("z", k)),
        (2, place.at["x"], lambda k: place.device("x", k)),
        (2, lax.axis_index("tensor"), lambda k: {"tensor": k}),
    )


def gain_stages(total_ref, scratch, place):
    held = scratch[0]
    stages = []
    for step, (size, mine, device) in enumerate(gain_axes(place)):
        send_sem, recv_sem, slots = scratch[1 + 3 * step : 4 + 3 * step]
        src = held.at[step]
        dst = total_ref if step == 3 else held.at[step + 1]

        def send(k, src=src, slots=slots, send_sem=send_sem, recv_sem=recv_sem, size=size, mine=mine, device=device):
            to = lax.rem(mine + k, size)
            return remote(src, slots.at[mine], send_sem.at[k], recv_sem.at[mine], device(to))

        def arrival(k, src=src, slots=slots, send_sem=send_sem, recv_sem=recv_sem, size=size, mine=mine, device=device):
            frm = lax.rem(mine + k, size)
            return remote(src, slots.at[frm], send_sem.at[k], recv_sem.at[frm], device(frm))

        def start(i, send=send, src=src, slots=slots, size=size, mine=mine):
            slots[mine] = src[...]
            for k in range(1, size):
                send(k).start()

        def end(i, send=send, arrival=arrival, slots=slots, size=size, dst=dst):
            for k in range(1, size):
                arrival(k).wait_recv()
                send(k).wait_send()
            total = slots[0]
            for k in range(1, size):
                total = total + slots[k]
            dst[...] = total

        stages += [start, end]
    return stages


SCRATCH = dict(
    weights=pltpu.VMEM((CHUNKS, 4, 2, 4, 32, CHUNK), BF16),
    hidden=pltpu.VMEM((2 * ROW, WIDTH), BF16),
    normed=pltpu.VMEM((2 * ROW, WIDTH), BF16),
    heads=pltpu.VMEM((2 * ROW, 3072), BF16),
    query_rot=pltpu.VMEM((2 * ROW, 1024), BF16),
    key_rot=pltpu.VMEM((2 * ROW, 512), BF16),
    middle=pltpu.VMEM((2 * ROW, WIDTH), F32),
    normed_two=pltpu.VMEM((2 * ROW, WIDTH), BF16),
    ff=pltpu.VMEM((3, 2 * ROW, 1536), BF16),
    grad=pltpu.VMEM((2 * ROW, WIDTH), BF16),
    attended_grad=pltpu.VMEM((2 * ROW, WIDTH), BF16),
    mixed_grad=pltpu.VMEM((ROW, 1024), BF16),
    turned=pltpu.VMEM((4, 4, 2, 4, 32, CHUNK), BF16),
    mine=pltpu.VMEM((2, 2, ROW, CHUNK), BF16),
    theirs=pltpu.VMEM((2, 2, ROW, CHUNK), BF16),
    leaving=pltpu.VMEM((2 * ROW, WIDTH), BF16),
    stage=pltpu.VMEM((2 * ROW, WIDTH), F32),
    cosine=pltpu.VMEM((2 * ROW, HEAD), F32),
    sine=pltpu.VMEM((2 * ROW, HEAD), F32),
    bias=pltpu.VMEM((2 * ROW, ROW), F32),
    cosine_turned=pltpu.VMEM((2, HEAD, ROW), F32),
    sine_turned=pltpu.VMEM((2, HEAD, ROW), F32),
    bias_turned=pltpu.VMEM((2 * ROW, ROW), F32),
    q_gain_turned=pltpu.VMEM((HEAD, HEAD), F32),
    q_gain_sum=pltpu.VMEM((HEAD, ROW), F32),
    scale_one=pltpu.VMEM((2 * ROW, 128), F32),
    scale_two=pltpu.VMEM((2 * ROW, 128), F32),
    wide=pltpu.VMEM((2, ROW, CHUNK), F32),
    weight_sem=pltpu.SemaphoreType.DMA((CHUNKS,)),
    input_sem=pltpu.SemaphoreType.DMA((2,)),
    output_sem=pltpu.SemaphoreType.DMA((2, 2)),
    mine_sem=pltpu.SemaphoreType.DMA((2, 2)),
    theirs_sem=pltpu.SemaphoreType.DMA((2, 2)),
    cross_send=pltpu.SemaphoreType.DMA((2, 2)),
    cross_recv=pltpu.SemaphoreType.DMA((2, 2)),
    relay_send=pltpu.SemaphoreType.DMA((2, 2)),
    relay_recv=pltpu.SemaphoreType.DMA((2, 2)),
)


def rows_of(micro):
    return pl.ds(pl.multiple_of(micro * ROW, ROW), ROW)


def over_rows(micro, body):
    for block in range(ROW // BLOCK):
        body(
            pl.ds(pl.multiple_of(micro * ROW + block * BLOCK, BLOCK), BLOCK),
            pl.ds(block * BLOCK, BLOCK),
        )


def columns(index, size=CHUNK):
    if isinstance(index, int):
        return pl.ds(index * size, size)
    return pl.ds(pl.multiple_of(index * size, size), size)


def inverse_rms(value):
    return lax.rsqrt(jnp.mean(value * value, axis=-1, keepdims=True) + EPSILON)


def kernel(
    lengths,
    block_input,
    cotangent,
    attn_gain,
    q_gain,
    k_gain,
    mlp_gain,
    q_weight,
    key_matrix,
    value_matrix,
    o_weight,
    gate_weight,
    up_weight,
    down_weight,
    table,
    hidden_out,
    hidden_grad,
    grads_out,
    gains_out,
    *scratch,
):
    s = dict(zip(SCRATCH, scratch))
    scratch = scratch[len(SCRATCH) :]
    weights, hidden, normed, heads = s["weights"], s["hidden"], s["normed"], s["heads"]
    query_rot, key_rot = s["query_rot"], s["key_rot"]
    middle, normed_two, ff, grad = s["middle"], s["normed_two"], s["ff"], s["grad"]
    attended_grad, mixed_grad, turned = s["attended_grad"], s["mixed_grad"], s["turned"]
    mine, theirs, leaving, stage = s["mine"], s["theirs"], s["leaving"], s["stage"]
    cosine, sine, bias = s["cosine"], s["sine"], s["bias"]
    scale_one, scale_two, wide = s["scale_one"], s["scale_two"], s["wide"]
    place = Place()
    section, tensor = lax.axis_index("section"), lax.axis_index("tensor")
    over_tensor, over_section = {"tensor": 1 - tensor}, {"section": 1 - section}

    barrier = pltpu.get_barrier_semaphore()
    for size, own, device in gain_axes(place):
        for k in range(1, size):
            pl.semaphore_signal(
                barrier, inc=1, device_id=device(lax.rem(own + k, size)), device_id_type=MESH
            )
    pl.semaphore_signal(barrier, inc=1, device_id=over_section, device_id_type=MESH)

    sources = (
        [(q_weight, 0), (q_weight, 1), (key_matrix, 0), (value_matrix, 0), (o_weight, 0), (o_weight, 1)],
        [(ref, k) for ref in (gate_weight, up_weight, down_weight) for k in range(3)],
    )

    def load(chunk):
        ref, part = sources[1][chunk] if chunk < MLP_CHUNKS else sources[0][chunk - MLP_CHUNKS]
        return pltpu.make_async_copy(
            ref.at[:, :, :, :, columns(part)], weights.at[chunk], s["weight_sem"].at[chunk]
        )

    def load_input(micro):
        rows = rows_of(micro)
        return pltpu.make_async_copy(block_input.at[rows], hidden.at[rows], s["input_sem"].at[micro])

    def load_cotangent(micro):
        rows = rows_of(micro)
        return pltpu.make_async_copy(cotangent.at[rows], grad.at[rows], s["input_sem"].at[micro])

    @pl.when(section == 0)
    def _():
        load_input(0).start()
        load_input(1).start()

    for chunk in (9, 10, 11, 12, 13, 14, 0, 3, 1, 4, 2, 5, 6, 7, 8):
        load(chunk).start()

    @pl.when(section == 1)
    def _():
        load_cotangent(0).start()
        load_cotangent(1).start()

    gains = scratch[-13]
    gains[0] = jnp.zeros((GAIN_ROWS, 128), F32)

    def tables(micro, carry):
        rows = rows_of(micro)
        ends = [lengths[micro, 0]]
        for k in (1, 2):
            ends.append(ends[-1] + lengths[micro, k])

        def begins(shape, dim=0):
            at = lax.broadcasted_iota(jnp.int32, shape, dim)
            found = jnp.zeros(shape, jnp.int32)
            for end in ends:
                found = jnp.where(at >= end, end, found)
            return at, found

        at, begin = begins((ROW, HEAD))
        chosen = (at - begin) == lax.broadcasted_iota(jnp.int32, (ROW, HEAD), 1)
        both = dot(chosen.astype(F32).astype(BF16), table[...])
        cosine[rows] = both[:, :128] + both[:, 128:256]
        sine[rows] = both[:, 256:384] + both[:, 384:]
        s["cosine_turned"][micro] = cosine[rows].T
        s["sine_turned"][micro] = sine[rows].T
        for dim, into in ((0, bias), (1, s["bias_turned"])):
            at, begin = begins((ROW, ROW), dim)
            key = lax.broadcasted_iota(jnp.int32, (ROW, ROW), 1 - dim)
            into[rows] = jnp.where((key >= begin) & (key <= at), 0.0, -1e9)
        return carry

    lax.fori_loop(0, 2, tables, 0)
    s["q_gain_turned"][...] = jnp.broadcast_to(q_gain[...], (HEAD, HEAD)).T
    s["q_gain_sum"][...] = jnp.zeros((HEAD, ROW), F32)

    pl.semaphore_wait(barrier, 9)

    def pair(slot, part):
        return remote(
            mine.at[slot, part],
            theirs.at[slot, part],
            s["mine_sem"].at[slot, part],
            s["theirs_sem"].at[slot, part],
            over_tensor,
        )

    def pair_start(slot, part, value):
        mine[slot, part] = value.astype(BF16)
        pair(slot, part).start()

    def pair_wait(slot):
        for part in range(2):
            pair(slot, part).wait()

    def pair_sum(slot, block):
        return jnp.concatenate(
            [
                mine[slot, part, block].astype(F32) + theirs[slot, part, block].astype(F32)
                for part in range(2)
            ],
            axis=1,
        )

    def half_rows(micro):
        return pl.ds(pl.multiple_of(micro * ROW + tensor * (ROW // 2), ROW // 2), ROW // 2)

    def cross(way, micro):
        rows = half_rows(micro)
        into = hidden if way == 0 else grad
        return remote(
            leaving.at[rows],
            into.at[rows],
            s["cross_send"].at[way, micro],
            s["cross_recv"].at[way, micro],
            over_section,
        )

    def arrive(way, micro):
        rows = half_rows(micro)
        into = hidden if way == 0 else grad
        cross(way, micro).wait_recv()
        relay = remote(
            into.at[rows],
            into.at[rows],
            s["relay_send"].at[way, micro],
            s["relay_recv"].at[way, micro],
            over_tensor,
        )
        relay.start()
        relay.wait()

    def output(way, micro):
        rows = rows_of(micro)
        into = hidden_out if way == 0 else hidden_grad
        return pltpu.make_async_copy(stage.at[rows], into.at[rows], s["output_sem"].at[way, micro])

    def weight(chunk):
        return weights[chunk].reshape(WIDTH, CHUNK)

    def times_back(left, chunks, part):
        right = [weights[chunk, 2 * part : 2 * part + 2].reshape(CHUNK, CHUNK) for chunk in chunks]
        return dot(left, jnp.concatenate(right, axis=1), NT)

    def once(micro, chunks):
        @pl.when(micro == 0)
        def _():
            for chunk in chunks:
                load(chunk).wait()

    def rotated(value, cos, sin):
        return value * cos + pltpu.roll(value, HEAD // 2, 1) * sin

    def unrotated(value, cos, sin):
        return value * cos - pltpu.roll(value, HEAD // 2, 1) * sin

    def forward(micro, carry):
        rows = rows_of(micro)

        @pl.when(section == 0)
        def _():
            load_input(micro).wait()

        @pl.when(section == 1)
        def _():
            arrive(0, micro)

        def norm_one(at, block):
            value = hidden[at].astype(F32)
            scale = inverse_rms(value)
            normed[at] = (value * scale * attn_gain[...]).astype(BF16)
            scale_one[at] = jnp.broadcast_to(scale, (BLOCK, 128))

        over_rows(micro, norm_one)
        once(micro, range(QUERY, OUT))
        for chunk in range(4):
            wide[0] = dot(normed[rows], weight(QUERY + chunk))
            if chunk == 3:
                heads[rows, columns(chunk)] = wide[0].astype(BF16)
                continue
            gain = q_gain if chunk < 2 else k_gain
            for k in range(4):
                value = wide[0, :, columns(k, HEAD)]
                heads[rows, columns(chunk * 4 + k, HEAD)] = value.astype(BF16)
                turn = rotated(value * inverse_rms(value) * gain[...], cosine[rows], sine[rows])
                if chunk < 2:
                    query_rot[rows, columns(chunk * 4 + k, HEAD)] = turn.astype(BF16)
                else:
                    key_rot[rows, columns(k, HEAD)] = turn.astype(BF16)

        ones = jnp.ones((ROW, HEAD), BF16)

        def attend(group):
            keys = key_rot[rows, columns(group, HEAD)]
            values = heads[rows, columns(12 + group, HEAD)]
            for k in range(2):
                head = 2 * group + k
                scores = dot(query_rot[rows, columns(head, HEAD)], keys, NT)
                low = jnp.exp2(scores * (SCORE_SCALE * LOG2_E) + bias[rows]).astype(BF16)
                both = dot(low, jnp.concatenate([values, ones], axis=1))
                inverse = 1.0 / both[:, HEAD:]
                heads[rows, columns(16 + head, HEAD)] = (both[:, :HEAD] * inverse).astype(BF16)

        for index in range(4):
            attend(index)
        once(micro, (OUT, OUT + 1))

        def attended(part):
            value = times_back(heads[rows, 2048:], (OUT, OUT + 1), part)
            pair_start(0, part, value)

        for index in range(2):
            attended(index)

        pair_wait(0)

        def norm_two(at, block):
            value = hidden[at].astype(F32) + pair_sum(0, block)
            middle[at] = value
            scale = inverse_rms(value)
            normed_two[at] = (value * scale * mlp_gain[...]).astype(BF16)
            scale_two[at] = jnp.broadcast_to(scale, (BLOCK, 128))

        over_rows(micro, norm_two)
        once(micro, range(QUERY))

        def hidden_units(chunk):
            wide[0] = dot(normed_two[rows], weight(GATE + chunk))
            wide[1] = dot(normed_two[rows], weight(UP + chunk))

            def silu(at, block):
                gate, up = wide[0, block], wide[1, block]
                ff[0, at, columns(chunk)] = gate.astype(BF16)
                ff[1, at, columns(chunk)] = up.astype(BF16)
                ff[2, at, columns(chunk)] = (gate * jax.nn.sigmoid(gate) * up).astype(BF16)

            over_rows(micro, silu)

        for index in range(3):
            hidden_units(index)

        def moved(part):
            value = times_back(ff[2, rows], range(DOWN, QUERY), part)
            pair_start(1, part, value)

        for index in range(2):
            moved(index)

        pair_wait(1)

        def result(at, block):
            value = middle[at] + pair_sum(1, block)
            stage[at] = value
            leaving[at] = value.astype(BF16)

        over_rows(micro, result)
        output(0, micro).start()

        @pl.when(section == 0)
        def _():
            cross(0, micro).start()

        return carry

    lax.fori_loop(0, 2, forward, 0)

    def norm_back(total, value, scale, gain):
        inner = total * gain
        return scale * inner - value * (scale * scale * scale) * jnp.mean(
            inner * value, axis=-1, keepdims=True
        )

    def add_gain(row, value):
        gains[0, row : row + 1] = gains[0, row : row + 1] + value

    def add_gains(row, part, value):
        for k in range(4):
            at = slice(row + part * 4 + k, row + part * 4 + k + 1)
            gains[0, at] = gains[0, at] + value[:, k * 128 : (k + 1) * 128]

    def turn(slot, value):
        for k in range(4):
            turned[slot, k] = value[:, columns(k, 256)].T.reshape(2, 4, 32, CHUNK)

    @pl.when(section == 0)
    def _():
        turn(0, normed_two)

    def weight_grad(chunk, slot, right):
        for part in range(4):
            value = dot(turned[slot, part].reshape(256, CHUNK), right)
            weights[chunk, part] = value.astype(BF16).reshape(2, 4, 32, CHUNK)

    def finish(chunk, total):
        if total.shape[0] == 1:
            total = total[0]
        grads_out[chunk] = total

    rings = []
    for first, (order, count) in enumerate(zip(ORDERS, COUNTS)):
        own, scratch = scratch[:9], scratch[9:]
        rings.append((count, LAGS, ring_stages(order, weights, first, own, place, finish)))

    def ring_start(chunk):
        for first in (0, 1):

            @pl.when(lax.rem(chunk, 2) == first)
            def _(first=first):
                rings[first][2][0]((chunk - first) // 2)

    def backward(micro, carry):
        rows = rows_of(micro)

        @pl.when(section == 0)
        def _():
            arrive(1, micro)
            cross(0, micro).wait_send()

        @pl.when(section == 1)
        def _():
            load_cotangent(micro).wait()

        def hidden_back(chunk):
            wide[0] = dot(grad[rows], weight(DOWN + chunk))

            def silu_back(at, block):
                act_grad = wide[0, block]
                gate, up = ff[0, at, columns(chunk)].astype(F32), ff[1, at, columns(chunk)].astype(F32)
                sigma = jax.nn.sigmoid(gate)
                passed = act_grad * sigma
                ff[0, at, columns(chunk)] = (passed * up * (1.0 + gate * (1.0 - sigma))).astype(BF16)
                ff[1, at, columns(chunk)] = (passed * gate).astype(BF16)

            over_rows(micro, silu_back)

        for index in range(3):
            hidden_back(index)

        def normed_two_back(part):
            left = jnp.concatenate([ff[0, rows], ff[1, rows]], axis=1)
            value = times_back(left, range(GATE, DOWN), part)
            pair_start(0, part, value)
            scaled = middle[rows, columns(part)] * scale_two[rows, :1]
            add_gains(8, part, jnp.sum(value * scaled, axis=0, keepdims=True))

        for index in range(2):
            normed_two_back(index)
        pair_wait(0)
        output(0, micro).wait()

        def middle_back(at, block):
            value = grad[at].astype(F32) + norm_back(
                pair_sum(0, block), middle[at], scale_two[at, :1], mlp_gain[...]
            )
            stage[at] = value
            attended_grad[at] = value.astype(BF16)

        over_rows(micro, middle_back)

        @pl.when(micro == 1)
        def _():
            @pl.when(section == 1)
            def _():
                turn(0, normed_two)

            def one(chunk, carry):
                weight_grad(chunk, chunk // 6, ff[chunk // 3, :, columns(lax.rem(chunk, 3))])
                ring_start(chunk)
                return carry

            lax.fori_loop(0, DOWN, one, 0)
            turn(1, grad)
            lax.fori_loop(DOWN, MLP_CHUNKS, one, 0)

        for k in range(2):
            mixed_grad[:, columns(k)] = dot(attended_grad[rows], weight(OUT + k)).astype(BF16)

        def attend_back(group):
            cos, sin = cosine[rows], sine[rows]
            cos_turned, sin_turned = s["cosine_turned"][micro], s["sine_turned"][micro]
            gain_turned = jnp.concatenate([s["q_gain_turned"][...]] * 2, axis=1)
            keys = key_rot[rows, columns(group, HEAD)]
            keys_turned = keys.T
            values = heads[rows, columns(12 + group, HEAD)]
            key_rot_grad = jnp.zeros((ROW, HEAD), F32)
            value_grad = jnp.zeros((ROW, HEAD), F32)
            for k in range(2):
                head = 2 * group + k
                here = columns(head, HEAD)
                queries = query_rot[rows, here]
                out_grad = mixed_grad[:, here]
                scores = dot(keys, queries, NT)
                raw = jnp.exp2(scores * (SCORE_SCALE * LOG2_E) + s["bias_turned"][rows])
                chance = raw * (1.0 / jnp.sum(raw, axis=0, keepdims=True))
                weighted = chance * dot(values, out_grad, NT)
                across = jnp.sum(weighted, axis=0, keepdims=True)
                score_grad = (weighted - chance * across).astype(BF16)
                value_grad = value_grad + dot(chance.astype(BF16), out_grad)
                key_rot_grad = key_rot_grad + dot(score_grad, queries)
                passed = dot(keys_turned, score_grad) * SCORE_SCALE
                swapped = jnp.concatenate([passed[HEAD // 2 :], passed[: HEAD // 2]], axis=0)
                turn_grad = passed * cos_turned - swapped * sin_turned
                query = heads[rows, here].T.astype(F32)
                scale = lax.rsqrt(jnp.mean(query * query, axis=0, keepdims=True) + EPSILON)
                scaled = query * scale
                s["q_gain_sum"][...] = s["q_gain_sum"][...] + turn_grad * scaled
                inner = turn_grad * gain_turned
                query_grad = scale * (inner - scaled * jnp.mean(inner * scaled, axis=0, keepdims=True))
                heads[rows, here] = query_grad.astype(BF16).T
            turn_grad = unrotated(key_rot_grad * SCORE_SCALE, cos, sin)
            here = columns(8 + group, HEAD)
            key = heads[rows, here].astype(F32)
            scale = inverse_rms(key)
            add_gain(17, jnp.sum(turn_grad * key * scale, axis=0, keepdims=True))
            heads[rows, here] = norm_back(turn_grad, key, scale, k_gain[...]).astype(BF16)
            heads[rows, columns(12 + group, HEAD)] = value_grad.astype(BF16)

        for index in range(4):
            attend_back(index)

        def normed_back(part):
            value = times_back(heads[rows, :2048], range(QUERY, OUT), part)
            pair_start(1, part, value)
            scaled = hidden[rows, columns(part)].astype(F32) * scale_one[rows, :1]
            add_gains(0, part, jnp.sum(value * scaled, axis=0, keepdims=True))

        for index in range(2):
            normed_back(index)
        pair_wait(1)

        def hidden_back_end(at, block):
            value = stage[at] + norm_back(
                pair_sum(1, block), hidden[at].astype(F32), scale_one[at, :1], attn_gain[...]
            )
            stage[at] = value
            leaving[at] = value.astype(BF16)

        over_rows(micro, hidden_back_end)
        output(1, micro).start()

        @pl.when(section == 1)
        def _():
            cross(1, micro).start()

        return carry

    lax.fori_loop(0, 2, backward, 0)

    add_gain(16, jnp.sum(s["q_gain_sum"][...].T, axis=0, keepdims=True))
    turn(2, normed)
    turn(3, attended_grad)

    def attention_grad(chunk, carry):
        weight_grad(MLP_CHUNKS + chunk, 2 + chunk // 4, heads[:, columns(chunk)])
        ring_start(MLP_CHUNKS + chunk)
        return carry

    lax.fori_loop(0, CHUNKS - MLP_CHUNKS, attention_grad, 0)

    groups = [(count, (None, *lags[1:]), stages) for count, lags, stages in rings]
    groups.append((1, (0, 2, 2, 4, 4, 6, 6, 8), gain_stages(gains_out, scratch, place)))

    def advance(now, carry):
        for step in range(8):
            for count, lags, stages in groups:
                if lags[step] is None:
                    continue
                i = now - lags[step]

                @pl.when((i >= 0) & (i < count))
                def _(i=i, run=stages[step]):
                    run(i)

        return carry

    lax.fori_loop(0, max(count + lags[-1] for count, lags, _ in groups), advance, 0)

    for micro in range(2):
        output(1, micro).wait()

        @pl.when(section == 1)
        def _(micro=micro):
            cross(1, micro).wait_send()


def rope_table():
    half = HEAD // 2
    rates = THETA ** (-2.0 * np.arange(half) / HEAD)
    angle = np.arange(HEAD)[:, None] * np.concatenate([rates, rates])[None]
    sign = np.where(np.arange(HEAD) < half, -1.0, 1.0)
    parts = []
    for value in (np.cos(angle), np.sin(angle) * sign):
        high = value.astype(jnp.bfloat16)
        parts += [high, (value - high.astype(np.float64)).astype(jnp.bfloat16)]
    return jnp.asarray(np.concatenate(parts, axis=1))


def by_place(weight):
    return weight.reshape(4, 2, 4, 32, weight.shape[-1])


def shards(
    block_input,
    doc_lengths,
    out_cotangent,
    attn_gain,
    q_gain,
    k_gain,
    mlp_gain,
    q_weight,
    key_matrix,
    value_matrix,
    o_weight,
    gate_weight,
    up_weight,
    down_weight,
):
    vmem = pl.BlockSpec(memory_space=pltpu.VMEM)
    smem = pl.BlockSpec(memory_space=pltpu.SMEM)
    anywhere = pl.BlockSpec(memory_space=pl.ANY)
    scratch = list(SCRATCH.values())
    for order, count in zip(ORDERS, COUNTS):
        scratch += ring_scratch(order, count)
    scratch += gain_scratch()
    full = jax.ShapeDtypeStruct(block_input.shape, F32)
    outputs, grads_in, grads, gains = pl.pallas_call(
        kernel,
        out_shape=(
            full,
            full,
            jax.ShapeDtypeStruct((CHUNKS, 32, CHUNK), F32),
            jax.ShapeDtypeStruct((GAIN_ROWS, 128), F32),
        ),
        in_specs=[smem, anywhere, anywhere] + [vmem] * 4 + [anywhere] * 7 + [vmem],
        out_specs=[anywhere, anywhere, vmem, vmem],
        scratch_shapes=scratch,
        compiler_params=pltpu.CompilerParams(
            collective_id=0, has_side_effects=True, vmem_limit_bytes=64 * 2**20 - 2**16
        ),
    )(
        doc_lengths,
        block_input,
        out_cotangent,
        attn_gain,
        q_gain,
        k_gain,
        mlp_gain,
        by_place(q_weight),
        by_place(key_matrix),
        by_place(value_matrix),
        by_place(o_weight),
        by_place(gate_weight),
        by_place(up_weight),
        by_place(down_weight),
        rope_table(),
    )

    def matrix(first, count):
        return jnp.concatenate([grads[first + k] for k in range(count)], axis=1)[None]

    flat = gains.reshape(1, -1)
    return (
        outputs[None],
        grads_in[None],
        flat[:, :1024],
        flat[:, 2048:2176],
        flat[:, 2176:2304],
        flat[:, 1024:2048],
        matrix(QUERY, 2),
        matrix(KEY, 1),
        matrix(VALUE, 1),
        matrix(OUT, 2),
        matrix(GATE, 3),
        matrix(UP, 3),
        matrix(DOWN, 3),
    )


def solution(mesh):
    weight = P("section", None, "tensor")
    gain = P("section", None)
    tokens = P("section", "dp", None)
    grad = P("section", "dp", "tensor")
    return jax.shard_map(
        shards,
        mesh=mesh,
        in_specs=(P("dp", None),) * 3 + (gain,) * 4 + (weight,) * 7,
        out_specs=(tokens,) * 2 + (gain,) * 4 + (grad,) * 7,
        check_vma=False,
    )
```

```python
import functools

import jax
import jax.numpy as jnp
import numpy as np
from jax import lax
from jax.experimental import pallas as pl
from jax.experimental.pallas import tpu as pltpu
from jax.sharding import PartitionSpec as P

EPSILON = 1e-06
THETA = 1000000.0
HEAD = 128
ROW = 256
WIDTH = 1024
BLOCK = 32
SCORE_SCALE = HEAD ** (-0.5)
LOG2_E = 1.4426950408889634
MESH = pl.DeviceIdType.MESH
BF16, F32 = jnp.bfloat16, jnp.float32
NT = (((1,), (1,)), ((), ()))
TN = (((0,), (0,)), ((), ()))

CHUNK = 512
DOWN, GATE, UP, QUERY, KEY, VALUE, OUT = 0, 3, 6, 9, 11, 12, 13
CHUNKS = 15
MLP_CHUNKS = 9
ORDERS = (("z", "y", "x"), ("y", "z", "x"))
COUNTS = (8, 7)
LAGS = (0, 0, 2, 2, 4, 6, 6, 8)
LEFT = 3
LEFT_ORDER = ("x", "y", "z")
LEFT_LAGS = (0, 0, 1, 2, 2, 3, 4)
LEFT_FROM = 6
GAIN_ROWS = 24


def remote(src, dst, send_sem, recv_sem, device):
    return pltpu.make_async_remote_copy(
        src_ref=src,
        dst_ref=dst,
        send_sem=send_sem,
        recv_sem=recv_sem,
        device_id=device,
        device_id_type=MESH,
    )


def dot(left, right, form=None):
    if form is None:
        return jnp.dot(left, right, preferred_element_type=F32)
    return lax.dot_general(left, right, form, preferred_element_type=F32)


class Place:
    def __init__(self):
        dp = lax.axis_index("dp")
        self.at = {"z": dp // 8, "x": dp // 4 % 2, "y": dp % 4}

    def device(self, axis, index):
        at = {**self.at, axis: index}
        return {"dp": at["z"] * 8 + at["x"] * 4 + at["y"]}


def ring_phases(order):
    found, done = [], []
    for axis in order:
        left = [name for name in ("z", "x", "y") if name not in done and name != axis]
        halved = None if axis == "x" else "x" if "x" in left else left[0] if left else "row"
        shape = []
        for name in left:
            size = 2 if name == "x" else 4
            shape.append(size // 2 if name == halved else size)
        rows = 16 if halved == "row" else 32
        found.append((axis, tuple(done), halved, (*shape, rows, CHUNK)))
        done.append(axis)
    return found


def ring_scratch(order, count, skipped=0):
    found = []
    for _, _, halved, shape in ring_phases(order)[skipped:]:
        parts = 6 if halved else 1
        found.append(pltpu.VMEM((count, parts, *shape), BF16))
        found.append(pltpu.SemaphoreType.DMA((count, parts)))
        found.append(pltpu.SemaphoreType.DMA((count, parts)))
    return found


def ring_stages(order, grads, at_first, scratch, place, finish, skipped=()):
    stages = []
    phases = ring_phases(order)[len(skipped) :]
    for step, (axis, done, halved, _) in enumerate(phases):
        arrived, send_sem, recv_sem = scratch[3 * step : 3 * step + 3]
        mine = place.at[axis]

        def where(i, index, half, axis=axis, done=done, halved=halved):
            found = list(at_first(i))
            for name in ("z", "x", "y"):
                if name in skipped:
                    continue
                if name in done:
                    found.append(place.at[name])
                elif name == axis:
                    found.append(index)
                elif name == halved:
                    size = 1 if name == "x" else 2
                    found.append(pl.ds(half * size, size))
                else:
                    found.append(slice(None))
            if halved == "row":
                found.append(pl.ds(half * 16, 16))
            return tuple(found)

        def put(i, half, total, step=step, mine=mine, where=where):
            if step == len(phases) - 1:
                finish(i, half, total)
            else:
                grads[where(i, mine, half)] = total.astype(BF16)

        if halved is None:

            def swap(
                i, where=where, arrived=arrived, send_sem=send_sem, recv_sem=recv_sem, mine=mine, axis=axis
            ):
                return remote(
                    grads.at[where(i, 1 - mine, 0)],
                    arrived.at[i, 0],
                    send_sem.at[i, 0],
                    recv_sem.at[i, 0],
                    place.device(axis, 1 - mine),
                )

            def start(i, swap=swap):
                swap(i).start()

            def end(i, swap=swap, arrived=arrived, where=where, mine=mine, put=put):
                swap(i).wait()
                put(i, 0, grads[where(i, mine, 0)].astype(F32) + arrived[i, 0].astype(F32))

            stages += [start, end]
            continue

        right, left = lax.rem(mine + 1, 4), lax.rem(mine + 3, 4)
        across = lax.rem(mine + 2, 4)
        sends = (
            (across, 0, right),
            (across, 1, left),
            (right, 1, right),
            (left, 0, left),
            (right, 0, right),
            (left, 1, left),
        )

        def send(
            i, k, where=where, arrived=arrived, send_sem=send_sem, recv_sem=recv_sem, axis=axis, sends=sends
        ):
            index, half, to = sends[k]
            return remote(
                grads.at[where(i, index, half)],
                arrived.at[i, k],
                send_sem.at[i, k],
                recv_sem.at[i, k],
                place.device(axis, to),
            )

        def start(i, send=send):
            for k in range(4):
                send(i, k).start()

        def pass_on(i, send=send, arrived=arrived, where=where, sends=sends):
            for k in (0, 1):
                send(i, k).wait_recv()
                index, half, _ = sends[4 + k]
                at = where(i, index, half)
                grads[at] = (grads[at].astype(F32) + arrived[i, k].astype(F32)).astype(BF16)
                send(i, 4 + k).start()

        def end(i, send=send, arrived=arrived, where=where, mine=mine, put=put):
            for k in range(2, 6):
                send(i, k).wait_recv()
            for k in range(6):
                send(i, k).wait_send()
            for half in (0, 1):
                own = grads[where(i, mine, half)].astype(F32)
                near = arrived[i, 4 - 2 * half].astype(F32)
                far = arrived[i, 3 + 2 * half].astype(F32)
                put(i, half, own + near + far)

        stages += [start, pass_on, end]
    return stages


def gain_scratch():
    found = [pltpu.VMEM((4, GAIN_ROWS, 128), F32)]
    for size in (4, 4, 2, 2):
        found.append(pltpu.SemaphoreType.DMA((size,)))
        found.append(pltpu.SemaphoreType.DMA((size,)))
        found.append(pltpu.VMEM((size, GAIN_ROWS, 128), F32))
    return found


def gain_axes(place):
    return (
        (4, place.at["y"], lambda k: place.device("y", k)),
        (4, place.at["z"], lambda k: place.device("z", k)),
        (2, place.at["x"], lambda k: place.device("x", k)),
        (2, lax.axis_index("tensor"), lambda k: {"tensor": k}),
    )


def gain_stages(total_ref, scratch, place):
    held = scratch[0]
    stages = []
    for step, (size, mine, device) in enumerate(gain_axes(place)):
        send_sem, recv_sem, slots = scratch[1 + 3 * step : 4 + 3 * step]
        src = held.at[step]
        dst = total_ref if step == 3 else held.at[step + 1]

        def send(k, src=src, slots=slots, send_sem=send_sem, recv_sem=recv_sem, size=size, mine=mine, device=device):
            to = lax.rem(mine + k, size)
            return remote(src, slots.at[mine], send_sem.at[k], recv_sem.at[mine], device(to))

        def arrival(k, src=src, slots=slots, send_sem=send_sem, recv_sem=recv_sem, size=size, mine=mine, device=device):
            frm = lax.rem(mine + k, size)
            return remote(src, slots.at[frm], send_sem.at[k], recv_sem.at[frm], device(frm))

        def start(i, send=send, src=src, slots=slots, size=size, mine=mine):
            slots[mine] = src[...]
            for k in range(1, size):
                send(k).start()

        def end(i, send=send, arrival=arrival, slots=slots, size=size, dst=dst):
            for k in range(1, size):
                arrival(k).wait_recv()
                send(k).wait_send()
            total = slots[0]
            for k in range(1, size):
                total = total + slots[k]
            if dst is total_ref:
                for k in range(GAIN_ROWS):
                    dst[:, k * 128 : (k + 1) * 128] = total[k : k + 1]
            else:
                dst[...] = total

        stages += [start, end]
    return stages


SCRATCH = dict(
    weights=pltpu.VMEM((CHUNKS, 4, 2, 4, 32, CHUNK), BF16),
    hidden=pltpu.VMEM((2 * ROW, WIDTH), BF16),
    normed=pltpu.VMEM((2 * ROW, WIDTH), BF16),
    heads=pltpu.VMEM((2 * ROW, 3072), BF16),
    query_rot=pltpu.VMEM((2 * ROW, 1024), BF16),
    key_rot=pltpu.VMEM((2 * ROW, 512), BF16),
    middle=pltpu.VMEM((2 * ROW, WIDTH), F32),
    normed_two=pltpu.VMEM((2 * ROW, WIDTH), BF16),
    ff=pltpu.VMEM((3, 3, 4, 4, 32, CHUNK), BF16),
    grad=pltpu.VMEM((2 * ROW, WIDTH), BF16),
    attended_grad=pltpu.VMEM((2 * ROW, WIDTH), BF16),
    mixed_grad=pltpu.VMEM((ROW, 1024), BF16),
    turned=pltpu.VMEM((2, 4, 2, 4, 32, CHUNK), BF16),
    mine=pltpu.VMEM((2, 2, ROW, CHUNK), BF16),
    theirs=pltpu.VMEM((2, 2, ROW, CHUNK), BF16),
    leaving=pltpu.VMEM((2 * ROW, WIDTH), BF16),
    stage=pltpu.VMEM((2 * ROW, WIDTH), F32),
    cosine=pltpu.VMEM((2 * ROW, HEAD), F32),
    sine=pltpu.VMEM((2 * ROW, HEAD), F32),
    bias=pltpu.VMEM((2 * ROW, ROW), F32),
    cosine_turned=pltpu.VMEM((2, HEAD, ROW), F32),
    sine_turned=pltpu.VMEM((2, HEAD, ROW), F32),
    bias_turned=pltpu.VMEM((2 * ROW, ROW), F32),
    q_gain_turned=pltpu.VMEM((HEAD, HEAD), F32),
    q_gain_sum=pltpu.VMEM((HEAD, ROW), F32),
    scale_one=pltpu.VMEM((2 * ROW, 128), F32),
    scale_two=pltpu.VMEM((2 * ROW, 128), F32),
    wide=pltpu.VMEM((2, ROW, CHUNK), F32),
    weight_sem=pltpu.SemaphoreType.DMA((CHUNKS,)),
    input_sem=pltpu.SemaphoreType.DMA((2,)),
    output_sem=pltpu.SemaphoreType.DMA((2, 2)),
    mine_sem=pltpu.SemaphoreType.DMA((2, 2)),
    theirs_sem=pltpu.SemaphoreType.DMA((2, 2)),
    cross_send=pltpu.SemaphoreType.DMA((2, 2)),
    cross_recv=pltpu.SemaphoreType.DMA((2, 2)),
    relay_send=pltpu.SemaphoreType.DMA((2, 2)),
    relay_recv=pltpu.SemaphoreType.DMA((2, 2)),
    left_send=pltpu.SemaphoreType.DMA((LEFT, 2)),
    left_recv=pltpu.SemaphoreType.DMA((LEFT, 2)),
    left_sum=pltpu.VMEM((LEFT, 32, CHUNK), F32),
    left_done=pltpu.VMEM((LEFT, 32, CHUNK), F32),
    done_send=pltpu.SemaphoreType.DMA((LEFT,)),
    done_recv=pltpu.SemaphoreType.DMA((LEFT,)),
    left_free=pltpu.SemaphoreType.REGULAR,
)


def rows_of(micro):
    return pl.ds(pl.multiple_of(micro * ROW, ROW), ROW)


def over_rows(micro, body):
    for block in range(ROW // BLOCK):
        body(
            pl.ds(pl.multiple_of(micro * ROW + block * BLOCK, BLOCK), BLOCK),
            pl.ds(block * BLOCK, BLOCK),
            (2 * micro + block // 4, block % 4),
        )


def columns(index, size=CHUNK):
    if isinstance(index, int):
        return pl.ds(index * size, size)
    return pl.ds(pl.multiple_of(index * size, size), size)


def inverse_rms(value):
    return lax.rsqrt(jnp.mean(value * value, axis=-1, keepdims=True) + EPSILON)


def kernel(
    lengths,
    block_input,
    cotangent,
    attn_gain,
    q_gain,
    k_gain,
    mlp_gain,
    q_weight,
    key_matrix,
    value_matrix,
    o_weight,
    gate_weight,
    up_weight,
    down_weight,
    table,
    hidden_out,
    hidden_grad,
    grads_out,
    gains_out,
    *scratch,
):
    s = dict(zip(SCRATCH, scratch))
    scratch = scratch[len(SCRATCH) :]
    weights, hidden, normed, heads = s["weights"], s["hidden"], s["normed"], s["heads"]
    query_rot, key_rot = s["query_rot"], s["key_rot"]
    middle, normed_two, ff, grad = s["middle"], s["normed_two"], s["ff"], s["grad"]
    attended_grad, mixed_grad, turned = s["attended_grad"], s["mixed_grad"], s["turned"]
    mine, theirs, leaving, stage = s["mine"], s["theirs"], s["leaving"], s["stage"]
    cosine, sine, bias = s["cosine"], s["sine"], s["bias"]
    scale_one, scale_two, wide = s["scale_one"], s["scale_two"], s["wide"]
    place = Place()
    section, tensor = lax.axis_index("section"), lax.axis_index("tensor")
    over_tensor, over_section = {"tensor": 1 - tensor}, {"section": 1 - section}
    aslant = {"section": 1 - section, **place.device("x", 1 - place.at["x"])}

    barrier = pltpu.get_barrier_semaphore()
    for size, own, device in gain_axes(place):
        for k in range(1, size):
            pl.semaphore_signal(
                barrier, inc=1, device_id=device(lax.rem(own + k, size)), device_id_type=MESH
            )
    for device in (over_section, aslant):
        pl.semaphore_signal(barrier, inc=1, device_id=device, device_id_type=MESH)

    sources = (
        [(q_weight, 0), (q_weight, 1), (key_matrix, 0), (value_matrix, 0), (o_weight, 0), (o_weight, 1)],
        [(ref, k) for ref in (down_weight, gate_weight, up_weight) for k in range(3)],
    )

    def load(chunk):
        ref, part = sources[1][chunk] if chunk < MLP_CHUNKS else sources[0][chunk - MLP_CHUNKS]
        return pltpu.make_async_copy(
            ref.at[:, :, :, :, columns(part)], weights.at[chunk], s["weight_sem"].at[chunk]
        )

    def load_input(micro):
        rows = rows_of(micro)
        return pltpu.make_async_copy(block_input.at[rows], hidden.at[rows], s["input_sem"].at[micro])

    def load_cotangent(micro):
        rows = rows_of(micro)
        return pltpu.make_async_copy(cotangent.at[rows], grad.at[rows], s["input_sem"].at[micro])

    @pl.when(section == 0)
    def _():
        load_input(0).start()
        load_input(1).start()

    for chunk in (9, 10, 11, 12, 13, 14, 3, 6, 4, 7, 5, 8, 0, 1, 2):
        load(chunk).start()

    @pl.when(section == 1)
    def _():
        load_cotangent(0).start()
        load_cotangent(1).start()

    gains = scratch[-13]
    gains[0] = jnp.zeros((GAIN_ROWS, 128), F32)

    def tables(micro, carry):
        rows = rows_of(micro)
        ends = [lengths[micro, 0]]
        for k in (1, 2):
            ends.append(ends[-1] + lengths[micro, k])

        def begins(shape, dim=0):
            at = lax.broadcasted_iota(jnp.int32, shape, dim)
            found = jnp.zeros(shape, jnp.int32)
            for end in ends:
                found = jnp.where(at >= end, end, found)
            return at, found

        at, begin = begins((ROW, HEAD))
        chosen = (at - begin) == lax.broadcasted_iota(jnp.int32, (ROW, HEAD), 1)
        both = dot(chosen.astype(F32).astype(BF16), table[...])
        cosine[rows] = both[:, :128] + both[:, 128:256]
        sine[rows] = both[:, 256:384] + both[:, 384:]
        s["cosine_turned"][micro] = cosine[rows].T
        s["sine_turned"][micro] = sine[rows].T
        for dim, into in ((0, bias), (1, s["bias_turned"])):
            at, begin = begins((ROW, ROW), dim)
            key = lax.broadcasted_iota(jnp.int32, (ROW, ROW), 1 - dim)
            into[rows] = jnp.where((key >= begin) & (key <= at), 0.0, -1e9)
        return carry

    lax.fori_loop(0, 2, tables, 0)
    s["q_gain_turned"][...] = jnp.broadcast_to(q_gain[...], (HEAD, HEAD)).T
    s["q_gain_sum"][...] = jnp.zeros((HEAD, ROW), F32)

    pl.semaphore_wait(barrier, 10)

    def pair(slot, part):
        return remote(
            mine.at[slot, part],
            theirs.at[slot, part],
            s["mine_sem"].at[slot, part],
            s["theirs_sem"].at[slot, part],
            over_tensor,
        )

    def pair_start(slot, part, value):
        mine[slot, part] = value.astype(BF16)
        pair(slot, part).start()

    def pair_wait(slot):
        for part in range(2):
            pair(slot, part).wait()

    def pair_sum(slot, block):
        return jnp.concatenate(
            [
                mine[slot, part, block].astype(F32) + theirs[slot, part, block].astype(F32)
                for part in range(2)
            ],
            axis=1,
        )

    def half_rows(micro):
        return pl.ds(pl.multiple_of(micro * ROW + tensor * (ROW // 2), ROW // 2), ROW // 2)

    def cross(way, micro):
        rows = half_rows(micro)
        into = hidden if way == 0 else grad
        return remote(
            leaving.at[rows],
            into.at[rows],
            s["cross_send"].at[way, micro],
            s["cross_recv"].at[way, micro],
            over_section,
        )

    def arrive(way, micro):
        rows = half_rows(micro)
        into = hidden if way == 0 else grad
        cross(way, micro).wait_recv()
        relay = remote(
            into.at[rows],
            into.at[rows],
            s["relay_send"].at[way, micro],
            s["relay_recv"].at[way, micro],
            over_tensor,
        )
        relay.start()
        relay.wait()

    def output(way, micro):
        rows = rows_of(micro)
        into = hidden_out if way == 0 else hidden_grad
        return pltpu.make_async_copy(stage.at[rows], into.at[rows], s["output_sem"].at[way, micro])

    def weight(chunk):
        return weights[chunk].reshape(WIDTH, CHUNK)

    def times_back(left, chunks, part):
        right = [weights[chunk, 2 * part : 2 * part + 2].reshape(CHUNK, CHUNK) for chunk in chunks]
        return dot(left, jnp.concatenate(right, axis=1), NT)

    def units(micro, *slots):
        found = [ff[slot, k, pl.ds(2 * micro, 2)].reshape(ROW, CHUNK) for slot in slots for k in range(3)]
        return jnp.concatenate(found, axis=1)

    def once(micro, chunks):
        @pl.when(micro == 0)
        def _():
            for chunk in chunks:
                load(chunk).wait()

    def rotated(value, cos, sin):
        return value * cos + pltpu.roll(value, HEAD // 2, 1) * sin

    def unrotated(value, cos, sin):
        return value * cos - pltpu.roll(value, HEAD // 2, 1) * sin

    def forward(micro, carry):
        rows = rows_of(micro)

        @pl.when(section == 0)
        def _():
            load_input(micro).wait()

        @pl.when(section == 1)
        def _():
            arrive(0, micro)

        def norm_one(at, block, _):
            value = hidden[at].astype(F32)
            scale = inverse_rms(value)
            normed[at] = (value * scale * attn_gain[...]).astype(BF16)
            scale_one[at] = jnp.broadcast_to(scale, (BLOCK, 128))

        over_rows(micro, norm_one)
        once(micro, range(QUERY, OUT))
        for chunk in range(4):
            wide[0] = dot(normed[rows], weight(QUERY + chunk))
            if chunk == 3:
                heads[rows, columns(chunk)] = wide[0].astype(BF16)
                continue
            gain = q_gain if chunk < 2 else k_gain
            for k in range(4):
                value = wide[0, :, columns(k, HEAD)]
                heads[rows, columns(chunk * 4 + k, HEAD)] = value.astype(BF16)
                turn = rotated(value * inverse_rms(value) * gain[...], cosine[rows], sine[rows])
                if chunk < 2:
                    query_rot[rows, columns(chunk * 4 + k, HEAD)] = turn.astype(BF16)
                else:
                    key_rot[rows, columns(k, HEAD)] = turn.astype(BF16)

        ones = jnp.ones((ROW, HEAD), BF16)

        def attend(group):
            keys = key_rot[rows, columns(group, HEAD)]
            values = heads[rows, columns(12 + group, HEAD)]
            for k in range(2):
                head = 2 * group + k
                scores = dot(query_rot[rows, columns(head, HEAD)], keys, NT)
                low = jnp.exp2(scores * (SCORE_SCALE * LOG2_E) + bias[rows]).astype(BF16)
                both = dot(low, jnp.concatenate([values, ones], axis=1))
                inverse = 1.0 / both[:, HEAD:]
                heads[rows, columns(16 + head, HEAD)] = (both[:, :HEAD] * inverse).astype(BF16)

        for index in range(4):
            attend(index)
        once(micro, (OUT, OUT + 1))

        def attended(part):
            value = times_back(heads[rows, 2048:], (OUT, OUT + 1), part)
            pair_start(0, part, value)

        for index in range(2):
            attended(index)

        pair_wait(0)

        def norm_two(at, block, _):
            value = hidden[at].astype(F32) + pair_sum(0, block)
            middle[at] = value
            scale = inverse_rms(value)
            normed_two[at] = (value * scale * mlp_gain[...]).astype(BF16)
            scale_two[at] = jnp.broadcast_to(scale, (BLOCK, 128))

        over_rows(micro, norm_two)
        once(micro, range(QUERY))

        def hidden_units(chunk):
            wide[0] = dot(normed_two[rows], weight(GATE + chunk))
            wide[1] = dot(normed_two[rows], weight(UP + chunk))

            def silu(at, block, place_in):
                gate, up = wide[0, block], wide[1, block]
                ff[1, chunk, *place_in] = gate.astype(BF16)
                ff[2, chunk, *place_in] = up.astype(BF16)
                ff[0, chunk, *place_in] = (gate * jax.nn.sigmoid(gate) * up).astype(BF16)

            over_rows(micro, silu)

        for index in range(3):
            hidden_units(index)

        def moved(part):
            value = times_back(units(micro, 0), range(DOWN, GATE), part)
            pair_start(1, part, value)

        for index in range(2):
            moved(index)

        pair_wait(1)

        def result(at, block, _):
            value = middle[at] + pair_sum(1, block)
            stage[at] = value
            leaving[at] = value.astype(BF16)

        over_rows(micro, result)
        output(0, micro).start()

        @pl.when(section == 0)
        def _():
            cross(0, micro).start()

        return carry

    lax.fori_loop(0, 2, forward, 0)

    def norm_back(total, value, scale, gain):
        inner = total * gain
        return scale * inner - value * (scale * scale * scale) * jnp.mean(
            inner * value, axis=-1, keepdims=True
        )

    def add_gain(row, value):
        gains[0, row : row + 1] = gains[0, row : row + 1] + value

    def add_gains(row, part, value):
        for k in range(4):
            at = slice(row + part * 4 + k, row + part * 4 + k + 1)
            gains[0, at] = gains[0, at] + value[:, k * 128 : (k + 1) * 128]

    def turn(slot, value):
        for k in range(4):
            turned[slot, k] = value[:, columns(k, 256)].T.reshape(2, 4, 32, CHUNK)

    @pl.when(section == 0)
    def _():
        turn(1, normed_two)

    def weight_grad(chunk, slot, right):
        for part in range(4):
            value = dot(turned[slot, part].reshape(256, CHUNK), right)
            weights[chunk, part] = value.astype(BF16).reshape(2, 4, 32, CHUNK)

    rings = []
    for first, (order, count) in enumerate(zip(ORDERS, COUNTS)):
        own, scratch = scratch[:9], scratch[9:]

        def finish(i, half, total, first=first):
            grads_out[2 * i + first] = total

        def chunk_at(i, first=first):
            return (2 * i + first,)

        rings.append((count, LAGS, ring_stages(order, weights, chunk_at, own, place, finish)))

    def kept(chunk):
        return (section == 1) | (lax.rem(chunk, 3) > 0) | (chunk >= MLP_CHUNKS)

    def ring_start(chunk):
        for first in (0, 1):

            @pl.when((lax.rem(chunk, 2) == first) & kept(chunk))
            def _(first=first):
                rings[first][2][0]((chunk - first) // 2)

        @pl.when(jnp.logical_not(kept(chunk)))
        def _():
            leave(chunk // 3, 0).start()
            leave(chunk // 3, 1).start()

    def leave(i, slant):
        side = place.at["x"]
        return remote(
            weights.at[3 * i, :, 1 - side if slant else side],
            ff.at[i, side],
            s["left_send"].at[i, slant],
            s["left_recv"].at[i, side],
            aslant if slant else over_section,
        )

    def left_arrival(i, side):
        return remote(
            weights.at[3 * i, :, side],
            ff.at[i, side],
            s["left_send"].at[i, side],
            s["left_recv"].at[i, side],
            over_section,
        )

    def give_back(i):
        return remote(
            s["left_sum"].at[i],
            s["left_done"].at[i],
            s["done_send"].at[i],
            s["done_recv"].at[i],
            over_section,
        )

    def left_start(i):
        for side in (0, 1):
            left_arrival(i, side).wait_recv()
        ff[i, 2] = (ff[i, 0].astype(F32) + ff[i, 1].astype(F32)).astype(BF16)

    def left_finish(i, half, total):
        s["left_sum"][i, half * 16 : half * 16 + 16] = total
        if half:
            give_back(i).start()

    own, scratch = scratch[:6], scratch[6:]
    left_stages = [left_start] + ring_stages(
        LEFT_ORDER, ff, lambda i: (i, 2), own, place, left_finish, skipped=("x",)
    )

    def backward(micro, carry):
        rows = rows_of(micro)

        @pl.when(section == 0)
        def _():
            arrive(1, micro)
            cross(0, micro).wait_send()

        @pl.when(section == 1)
        def _():
            load_cotangent(micro).wait()

        def hidden_back(chunk):
            wide[0] = dot(grad[rows], weight(DOWN + chunk))

            def silu_back(at, block, place_in):
                act_grad = wide[0, block]
                gate, up = ff[1, chunk, *place_in].astype(F32), ff[2, chunk, *place_in].astype(F32)
                sigma = jax.nn.sigmoid(gate)
                passed = act_grad * sigma
                ff[1, chunk, *place_in] = (passed * up * (1.0 + gate * (1.0 - sigma))).astype(BF16)
                ff[2, chunk, *place_in] = (passed * gate).astype(BF16)

            over_rows(micro, silu_back)

        for index in range(3):
            hidden_back(index)

        def normed_two_back(part):
            value = times_back(units(micro, 1, 2), range(GATE, QUERY), part)
            pair_start(0, part, value)
            scaled = middle[rows, columns(part)] * scale_two[rows, :1]
            add_gains(8, part, jnp.sum(value * scaled, axis=0, keepdims=True))

        def mlp_grad(chunk, carry):
            weight_grad(chunk, jnp.minimum(chunk // 3, 1), ff[chunk // 3, lax.rem(chunk, 3)].reshape(2 * ROW, CHUNK))
            ring_start(chunk)
            return carry

        @pl.when(micro == 1)
        def _():
            turn(0, grad)

            @pl.when(section == 0)
            def _():
                pl.semaphore_wait(s["left_free"], 2)

            lax.fori_loop(DOWN, GATE, mlp_grad, 0)

        for index in range(2):
            normed_two_back(index)

        @pl.when(micro == 1)
        def _():
            @pl.when(section == 1)
            def _():
                turn(1, normed_two)

            lax.fori_loop(GATE, QUERY, mlp_grad, 0)

            @pl.when(section == 1)
            def _():
                for device in (over_section, aslant):
                    pl.semaphore_signal(
                        s["left_free"], inc=1, device_id=device, device_id_type=MESH
                    )

        pair_wait(0)
        output(0, micro).wait()

        def middle_back(at, block, _):
            value = grad[at].astype(F32) + norm_back(
                pair_sum(0, block), middle[at], scale_two[at, :1], mlp_gain[...]
            )
            stage[at] = value
            attended_grad[at] = value.astype(BF16)

        over_rows(micro, middle_back)

        for k in range(2):
            mixed_grad[:, columns(k)] = dot(attended_grad[rows], weight(OUT + k)).astype(BF16)

        def attend_back(group):
            cos, sin = cosine[rows], sine[rows]
            cos_turned, sin_turned = s["cosine_turned"][micro], s["sine_turned"][micro]
            gain_turned = jnp.concatenate([s["q_gain_turned"][...]] * 2, axis=1)
            keys = key_rot[rows, columns(group, HEAD)]
            keys_turned = keys.T
            values = heads[rows, columns(12 + group, HEAD)]
            key_rot_grad = jnp.zeros((ROW, HEAD), F32)
            value_grad = jnp.zeros((ROW, HEAD), F32)
            for k in range(2):
                head = 2 * group + k
                here = columns(head, HEAD)
                queries = query_rot[rows, here]
                out_grad = mixed_grad[:, here]
                scores = dot(keys, queries, NT)
                raw = jnp.exp2(scores * (SCORE_SCALE * LOG2_E) + s["bias_turned"][rows])
                chance = raw * (1.0 / jnp.sum(raw, axis=0, keepdims=True))
                weighted = chance * dot(values, out_grad, NT)
                across = jnp.sum(weighted, axis=0, keepdims=True)
                score_grad = (weighted - chance * across).astype(BF16)
                value_grad = value_grad + dot(chance.astype(BF16), out_grad)
                key_rot_grad = key_rot_grad + dot(score_grad, queries)
                passed = dot(keys_turned, score_grad) * SCORE_SCALE
                swapped = jnp.concatenate([passed[HEAD // 2 :], passed[: HEAD // 2]], axis=0)
                turn_grad = passed * cos_turned - swapped * sin_turned
                query = heads[rows, here].T.astype(F32)
                scale = lax.rsqrt(jnp.mean(query * query, axis=0, keepdims=True) + EPSILON)
                scaled = query * scale
                s["q_gain_sum"][...] = s["q_gain_sum"][...] + turn_grad * scaled
                inner = turn_grad * gain_turned
                query_grad = scale * (inner - scaled * jnp.mean(inner * scaled, axis=0, keepdims=True))
                heads[rows, here] = query_grad.astype(BF16).T
            turn_grad = unrotated(key_rot_grad * SCORE_SCALE, cos, sin)
            here = columns(8 + group, HEAD)
            key = heads[rows, here].astype(F32)
            scale = inverse_rms(key)
            add_gain(17, jnp.sum(turn_grad * key * scale, axis=0, keepdims=True))
            heads[rows, here] = norm_back(turn_grad, key, scale, k_gain[...]).astype(BF16)
            heads[rows, columns(12 + group, HEAD)] = value_grad.astype(BF16)

        for index in range(4):
            attend_back(index)

        def normed_back(part):
            value = times_back(heads[rows, :2048], range(QUERY, OUT), part)
            pair_start(1, part, value)
            scaled = hidden[rows, columns(part)].astype(F32) * scale_one[rows, :1]
            add_gains(0, part, jnp.sum(value * scaled, axis=0, keepdims=True))

        for index in range(2):
            normed_back(index)
        pair_wait(1)

        def hidden_back_end(at, block, _):
            value = stage[at] + norm_back(
                pair_sum(1, block), hidden[at].astype(F32), scale_one[at, :1], attn_gain[...]
            )
            stage[at] = value
            leaving[at] = value.astype(BF16)

        over_rows(micro, hidden_back_end)
        output(1, micro).start()

        @pl.when(section == 1)
        def _():
            cross(1, micro).start()

        return carry

    lax.fori_loop(0, 2, backward, 0)

    add_gain(16, jnp.sum(s["q_gain_sum"][...].T, axis=0, keepdims=True))
    turn(0, normed)
    turn(1, attended_grad)

    def attention_grad(chunk, carry):
        weight_grad(MLP_CHUNKS + chunk, chunk // 4, heads[:, columns(chunk)])
        ring_start(MLP_CHUNKS + chunk)
        return carry

    lax.fori_loop(0, CHUNKS - MLP_CHUNKS, attention_grad, 0)

    def always(i):
        return True

    groups = [
        (count, (None, *lags[1:]), stages, lambda i, first=first: kept(2 * i + first))
        for first, (count, lags, stages) in enumerate(rings)
    ]
    groups.append(
        (LEFT, [LEFT_FROM + lag for lag in LEFT_LAGS], left_stages, lambda i: section == 1)
    )
    groups.append((1, (0, 2, 2, 4, 4, 6, 6, 8), gain_stages(gains_out, scratch, place), always))

    def advance(now, carry):
        for step in range(8):
            for count, lags, stages, runs in groups:
                if step >= len(stages) or lags[step] is None:
                    continue
                i = now - lags[step]

                @pl.when((i >= 0) & (i < count) & runs(i))
                def _(i=i, run=stages[step]):
                    run(i)

        return carry

    lax.fori_loop(0, max(count + lags[-1] for count, lags, _, _ in groups), advance, 0)

    @pl.when(section == 0)
    def _():
        for i in range(LEFT):
            leave(i, 0).wait_send()
            leave(i, 1).wait_send()
            give_back(i).wait_recv()
            grads_out[3 * i] = s["left_done"][i]

    @pl.when(section == 1)
    def _():
        for i in range(LEFT):
            give_back(i).wait_send()

    for micro in range(2):
        output(1, micro).wait()

        @pl.when(section == 1)
        def _(micro=micro):
            cross(1, micro).wait_send()


def rope_table():
    half = HEAD // 2
    rates = THETA ** (-2.0 * np.arange(half) / HEAD)
    angle = np.arange(HEAD)[:, None] * np.concatenate([rates, rates])[None]
    sign = np.where(np.arange(HEAD) < half, -1.0, 1.0)
    parts = []
    for value in (np.cos(angle), np.sin(angle) * sign):
        high = value.astype(jnp.bfloat16)
        parts += [high, (value - high.astype(np.float64)).astype(jnp.bfloat16)]
    return jnp.asarray(np.concatenate(parts, axis=1))


def by_place(weight):
    return weight.reshape(4, 2, 4, 32, weight.shape[-1])


def shards(
    block_input,
    doc_lengths,
    out_cotangent,
    attn_gain,
    q_gain,
    k_gain,
    mlp_gain,
    q_weight,
    key_matrix,
    value_matrix,
    o_weight,
    gate_weight,
    up_weight,
    down_weight,
):
    vmem = pl.BlockSpec(memory_space=pltpu.VMEM)
    smem = pl.BlockSpec(memory_space=pltpu.SMEM)
    anywhere = pl.BlockSpec(memory_space=pl.ANY)
    scratch = list(SCRATCH.values())
    for order, count in zip(ORDERS, COUNTS):
        scratch += ring_scratch(order, count)
    scratch += ring_scratch(LEFT_ORDER, LEFT, 1)
    scratch += gain_scratch()
    full = jax.ShapeDtypeStruct(block_input.shape, F32)
    outputs, grads_in, grads, gains = pl.pallas_call(
        kernel,
        out_shape=(
            full,
            full,
            jax.ShapeDtypeStruct((CHUNKS, 32, CHUNK), F32),
            jax.ShapeDtypeStruct((1, GAIN_ROWS * 128), F32),
        ),
        in_specs=[smem, anywhere, anywhere] + [vmem] * 4 + [anywhere] * 7 + [vmem],
        out_specs=[anywhere, anywhere, vmem, vmem],
        scratch_shapes=scratch,
        compiler_params=pltpu.CompilerParams(
            collective_id=0, has_side_effects=True, vmem_limit_bytes=64 * 2**20 - 2**16
        ),
    )(
        doc_lengths,
        block_input,
        out_cotangent,
        attn_gain,
        q_gain,
        k_gain,
        mlp_gain,
        by_place(q_weight),
        by_place(key_matrix),
        by_place(value_matrix),
        by_place(o_weight),
        by_place(gate_weight),
        by_place(up_weight),
        by_place(down_weight),
        rope_table(),
    )

    return spread(outputs, grads_in, grads, gains)


MATRICES = ((QUERY, 2), (KEY, 1), (VALUE, 1), (OUT, 2), (GATE, 3), (UP, 3), (DOWN, 3))
GAIN_PARTS = ((0, 1024), (2048, 128), (2176, 128), (1024, 1024))


def spread_kernel(outputs, grads_in, grads, gains, *refs):
    results, (tokens, matrices, row, in_sem, out_sem) = refs[:-5], refs[-5:]
    loads, stores = [], []

    def through(src, held, pairs):
        load = pltpu.make_async_copy(src, held, in_sem.at[len(loads)])
        load.start()
        loads.append((load, pairs))

    through(grads, matrices, [])
    for k in range(8):
        rows = pl.ds(k % 4 * 128, 128)
        src, into = ((outputs, results[0]), (grads_in, results[1]))[k // 4]
        through(src.at[rows], tokens.at[k], [(tokens.at[k], into.at[0, rows])])
    through(gains, row, [])
    for (first, count), into in zip(MATRICES, results[6:]):
        for k in range(count):
            pair = (matrices.at[first + k], into.at[0, :, k * CHUNK : (k + 1) * CHUNK])
            loads[0][1].append(pair)
    for (first, size), into in zip(GAIN_PARTS, results[2:6]):
        loads[-1][1].append((row.at[:, first : first + size], into))
    for load, pairs in loads:
        load.wait()
        for src, dst in pairs:
            store = pltpu.make_async_copy(src, dst, out_sem.at[len(stores)])
            store.start()
            stores.append(store)
    for store in stores:
        store.wait()


def spread(outputs, grads_in, grads, gains):
    shapes = [(1, *outputs.shape)] * 2 + [(1, size) for _, size in GAIN_PARTS]
    shapes += [(1, 32, count * CHUNK) for _, count in MATRICES]
    anywhere = pl.BlockSpec(memory_space=pl.ANY)
    return pl.pallas_call(
        spread_kernel,
        out_shape=[jax.ShapeDtypeStruct(shape, F32) for shape in shapes],
        in_specs=[anywhere] * 4,
        out_specs=[anywhere] * len(shapes),
        scratch_shapes=[
            pltpu.VMEM((8, 128, outputs.shape[1]), F32),
            pltpu.VMEM(grads.shape, F32),
            pltpu.VMEM(gains.shape, F32),
            pltpu.SemaphoreType.DMA((10,)),
            pltpu.SemaphoreType.DMA((27,)),
        ],
        compiler_params=pltpu.CompilerParams(vmem_limit_bytes=16 * 2**20),
    )(outputs, grads_in, grads, gains)


def solution(mesh):
    weight = P("section", None, "tensor")
    gain = P("section", None)
    tokens = P("section", "dp", None)
    grad = P("section", "dp", "tensor")
    return jax.shard_map(
        shards,
        mesh=mesh,
        in_specs=(P("dp", None),) * 3 + (gain,) * 4 + (weight,) * 7,
        out_specs=(tokens,) * 2 + (gain,) * 4 + (grad,) * 7,
        check_vma=False,
    )
```

```python
import functools

import jax
import jax.numpy as jnp
import numpy as np
from jax import lax
from jax.experimental import pallas as pl
from jax.experimental.pallas import tpu as pltpu
from jax.sharding import PartitionSpec as P

EPSILON = 1e-06
THETA = 1000000.0
HEAD = 128
ROW = 256
WIDTH = 1024
BLOCK = 32
SCORE_SCALE = HEAD ** (-0.5)
LOG2_E = 1.4426950408889634
MESH = pl.DeviceIdType.MESH
BF16, F32 = jnp.bfloat16, jnp.float32
NT = (((1,), (1,)), ((), ()))
TN = (((0,), (0,)), ((), ()))

CHUNK = 512
DOWN, GATE, UP, QUERY, KEY, VALUE, OUT = 0, 3, 6, 9, 11, 12, 13
CHUNKS = 15
MLP_CHUNKS = 9
ORDERS = (("z", "y", "x"), ("y", "z", "x"))
COUNTS = (8, 7)
LAGS = (0, 0, 2, 2, 4, 6, 6, 8)
LEFT = 3
LEFT_ORDER = ("x", "y", "z")
LEFT_LAGS = (0, 0, 1, 2, 2, 3, 4)
LEFT_FROM = 6
GAIN_ROWS = 24


def remote(src, dst, send_sem, recv_sem, device):
    return pltpu.make_async_remote_copy(
        src_ref=src,
        dst_ref=dst,
        send_sem=send_sem,
        recv_sem=recv_sem,
        device_id=device,
        device_id_type=MESH,
    )


def dot(left, right, form=None):
    if form is None:
        return jnp.dot(left, right, preferred_element_type=F32)
    return lax.dot_general(left, right, form, preferred_element_type=F32)


class Place:
    def __init__(self):
        dp = lax.axis_index("dp")
        self.at = {"z": dp // 8, "x": dp // 4 % 2, "y": dp % 4}

    def device(self, axis, index):
        at = {**self.at, axis: index}
        return {"dp": at["z"] * 8 + at["x"] * 4 + at["y"]}


def ring_phases(order):
    found, done = [], []
    for axis in order:
        left = [name for name in ("z", "x", "y") if name not in done and name != axis]
        halved = None if axis == "x" else "x" if "x" in left else left[0] if left else "row"
        shape = []
        for name in left:
            size = 2 if name == "x" else 4
            shape.append(size // 2 if name == halved else size)
        rows = 16 if halved == "row" else 32
        found.append((axis, tuple(done), halved, (*shape, rows, CHUNK)))
        done.append(axis)
    return found


def ring_scratch(order, count, skipped=0):
    found = []
    for _, _, halved, shape in ring_phases(order)[skipped:]:
        parts = 6 if halved else 1
        found.append(pltpu.VMEM((count, parts, *shape), BF16))
        found.append(pltpu.SemaphoreType.DMA((count, parts)))
        found.append(pltpu.SemaphoreType.DMA((count, parts)))
    return found


def ring_stages(order, grads, at_first, scratch, place, finish, skipped=()):
    stages = []
    phases = ring_phases(order)[len(skipped) :]
    for step, (axis, done, halved, _) in enumerate(phases):
        arrived, send_sem, recv_sem = scratch[3 * step : 3 * step + 3]
        mine = place.at[axis]

        def where(i, index, half, axis=axis, done=done, halved=halved):
            found = list(at_first(i))
            for name in ("z", "x", "y"):
                if name in skipped:
                    continue
                if name in done:
                    found.append(place.at[name])
                elif name == axis:
                    found.append(index)
                elif name == halved:
                    size = 1 if name == "x" else 2
                    found.append(pl.ds(half * size, size))
                else:
                    found.append(slice(None))
            if halved == "row":
                found.append(pl.ds(half * 16, 16))
            return tuple(found)

        def put(i, half, total, step=step, mine=mine, where=where):
            if step == len(phases) - 1:
                finish(i, half, total)
            else:
                grads[where(i, mine, half)] = total.astype(BF16)

        if halved is None:

            def swap(
                i, where=where, arrived=arrived, send_sem=send_sem, recv_sem=recv_sem, mine=mine, axis=axis
            ):
                return remote(
                    grads.at[where(i, 1 - mine, 0)],
                    arrived.at[i, 0],
                    send_sem.at[i, 0],
                    recv_sem.at[i, 0],
                    place.device(axis, 1 - mine),
                )

            def start(i, swap=swap):
                swap(i).start()

            def end(i, swap=swap, arrived=arrived, where=where, mine=mine, put=put):
                swap(i).wait()
                put(i, 0, grads[where(i, mine, 0)].astype(F32) + arrived[i, 0].astype(F32))

            stages += [start, end]
            continue

        right, left = lax.rem(mine + 1, 4), lax.rem(mine + 3, 4)
        across = lax.rem(mine + 2, 4)
        sends = (
            (across, 0, right),
            (across, 1, left),
            (right, 1, right),
            (left, 0, left),
            (right, 0, right),
            (left, 1, left),
        )

        def send(
            i, k, where=where, arrived=arrived, send_sem=send_sem, recv_sem=recv_sem, axis=axis, sends=sends
        ):
            index, half, to = sends[k]
            return remote(
                grads.at[where(i, index, half)],
                arrived.at[i, k],
                send_sem.at[i, k],
                recv_sem.at[i, k],
                place.device(axis, to),
            )

        def start(i, send=send):
            for k in range(4):
                send(i, k).start()

        def pass_on(i, send=send, arrived=arrived, where=where, sends=sends):
            for k in (0, 1):
                send(i, k).wait_recv()
                index, half, _ = sends[4 + k]
                at = where(i, index, half)
                grads[at] = (grads[at].astype(F32) + arrived[i, k].astype(F32)).astype(BF16)
                send(i, 4 + k).start()

        def end(i, send=send, arrived=arrived, where=where, mine=mine, put=put):
            for k in range(2, 6):
                send(i, k).wait_recv()
            for k in range(6):
                send(i, k).wait_send()
            for half in (0, 1):
                own = grads[where(i, mine, half)].astype(F32)
                near = arrived[i, 4 - 2 * half].astype(F32)
                far = arrived[i, 3 + 2 * half].astype(F32)
                put(i, half, own + near + far)

        stages += [start, pass_on, end]
    return stages


def gain_scratch():
    found = [pltpu.VMEM((4, GAIN_ROWS, 128), F32)]
    for size in (4, 4, 2, 2):
        found.append(pltpu.SemaphoreType.DMA((size,)))
        found.append(pltpu.SemaphoreType.DMA((size,)))
        found.append(pltpu.VMEM((size, GAIN_ROWS, 128), F32))
    return found


def gain_axes(place):
    return (
        (4, place.at["y"], lambda k: place.device("y", k)),
        (4, place.at["z"], lambda k: place.device("z", k)),
        (2, place.at["x"], lambda k: place.device("x", k)),
        (2, lax.axis_index("tensor"), lambda k: {"tensor": k}),
    )


def gain_stages(total_ref, scratch, place):
    held = scratch[0]
    stages = []
    for step, (size, mine, device) in enumerate(gain_axes(place)):
        send_sem, recv_sem, slots = scratch[1 + 3 * step : 4 + 3 * step]
        src = held.at[step]
        dst = total_ref if step == 3 else held.at[step + 1]

        def send(k, src=src, slots=slots, send_sem=send_sem, recv_sem=recv_sem, size=size, mine=mine, device=device):
            to = lax.rem(mine + k, size)
            return remote(src, slots.at[mine], send_sem.at[k], recv_sem.at[mine], device(to))

        def arrival(k, src=src, slots=slots, send_sem=send_sem, recv_sem=recv_sem, size=size, mine=mine, device=device):
            frm = lax.rem(mine + k, size)
            return remote(src, slots.at[frm], send_sem.at[k], recv_sem.at[frm], device(frm))

        def start(i, send=send, src=src, slots=slots, size=size, mine=mine):
            slots[mine] = src[...]
            for k in range(1, size):
                send(k).start()

        def end(i, send=send, arrival=arrival, slots=slots, size=size, dst=dst):
            for k in range(1, size):
                arrival(k).wait_recv()
                send(k).wait_send()
            total = slots[0]
            for k in range(1, size):
                total = total + slots[k]
            if dst is total_ref:
                for k in range(GAIN_ROWS):
                    dst[:, k * 128 : (k + 1) * 128] = total[k : k + 1]
            else:
                dst[...] = total

        stages += [start, end]
    return stages


SCRATCH = dict(
    weights=pltpu.VMEM((CHUNKS, 4, 2, 4, 32, CHUNK), BF16),
    hidden=pltpu.VMEM((2 * ROW, WIDTH), BF16),
    normed=pltpu.VMEM((2 * ROW, WIDTH), BF16),
    heads=pltpu.VMEM((2 * ROW, 3072), BF16),
    query_rot=pltpu.VMEM((2 * ROW, 1024), BF16),
    key_rot=pltpu.VMEM((2 * ROW, 512), BF16),
    middle=pltpu.VMEM((2 * ROW, WIDTH), F32),
    normed_two=pltpu.VMEM((2 * ROW, WIDTH), BF16),
    ff=pltpu.VMEM((3, 3, 4, 4, 32, CHUNK), BF16),
    grad=pltpu.VMEM((2 * ROW, WIDTH), BF16),
    attended_grad=pltpu.VMEM((2 * ROW, WIDTH), BF16),
    mixed_grad=pltpu.VMEM((ROW, 1024), BF16),
    turned=pltpu.VMEM((2, 4, 2, 4, 32, CHUNK), BF16),
    mine=pltpu.VMEM((4, 2, ROW, CHUNK), BF16),
    theirs=pltpu.VMEM((4, 2, ROW, CHUNK), BF16),
    leaving=pltpu.VMEM((2, ROW // 2, WIDTH), BF16),
    stage=pltpu.VMEM((2 * ROW, WIDTH), F32),
    cosine=pltpu.VMEM((2 * ROW, HEAD), F32),
    sine=pltpu.VMEM((2 * ROW, HEAD), F32),
    bias=pltpu.VMEM((2 * ROW, ROW), F32),
    cosine_turned=pltpu.VMEM((2, HEAD, ROW), F32),
    sine_turned=pltpu.VMEM((2, HEAD, ROW), F32),
    bias_turned=pltpu.VMEM((2 * ROW, ROW), F32),
    q_gain_turned=pltpu.VMEM((HEAD, HEAD), F32),
    q_gain_sum=pltpu.VMEM((HEAD, ROW), F32),
    scale_one=pltpu.VMEM((2 * ROW, 128), F32),
    scale_two=pltpu.VMEM((2 * ROW, 128), F32),
    wide=pltpu.VMEM((2, ROW, CHUNK), F32),
    weight_sem=pltpu.SemaphoreType.DMA((CHUNKS,)),
    input_sem=pltpu.SemaphoreType.DMA((2,)),
    output_sem=pltpu.SemaphoreType.DMA((2, 2)),
    mine_sem=pltpu.SemaphoreType.DMA((4, 2)),
    theirs_sem=pltpu.SemaphoreType.DMA((4, 2)),
    cross_send=pltpu.SemaphoreType.DMA((2, 2)),
    cross_recv=pltpu.SemaphoreType.DMA((2, 2)),
    relay_send=pltpu.SemaphoreType.DMA((2, 2)),
    relay_recv=pltpu.SemaphoreType.DMA((2, 2)),
    left_send=pltpu.SemaphoreType.DMA((LEFT, 2)),
    left_recv=pltpu.SemaphoreType.DMA((LEFT, 2)),
    left_sum=pltpu.VMEM((LEFT, 32, CHUNK), F32),
    left_done=pltpu.VMEM((LEFT, 32, CHUNK), F32),
    done_send=pltpu.SemaphoreType.DMA((LEFT,)),
    done_recv=pltpu.SemaphoreType.DMA((LEFT,)),
    left_free=pltpu.SemaphoreType.REGULAR,
)


def rows_of(micro):
    return pl.ds(pl.multiple_of(micro * ROW, ROW), ROW)


def over_rows(micro, body):
    for block in range(ROW // BLOCK):
        body(
            pl.ds(pl.multiple_of(micro * ROW + block * BLOCK, BLOCK), BLOCK),
            pl.ds(block * BLOCK, BLOCK),
            (2 * micro + block // 4, block % 4),
        )


def columns(index, size=CHUNK):
    if isinstance(index, int):
        return pl.ds(index * size, size)
    return pl.ds(pl.multiple_of(index * size, size), size)


def inverse_rms(value):
    return lax.rsqrt(jnp.mean(value * value, axis=-1, keepdims=True) + EPSILON)


def kernel(
    lengths,
    block_input,
    cotangent,
    attn_gain,
    q_gain,
    k_gain,
    mlp_gain,
    q_weight,
    key_matrix,
    value_matrix,
    o_weight,
    gate_weight,
    up_weight,
    down_weight,
    table,
    hidden_out,
    hidden_grad,
    grads_out,
    gains_out,
    *scratch,
):
    s = dict(zip(SCRATCH, scratch))
    scratch = scratch[len(SCRATCH) :]
    weights, hidden, normed, heads = s["weights"], s["hidden"], s["normed"], s["heads"]
    query_rot, key_rot = s["query_rot"], s["key_rot"]
    middle, normed_two, ff, grad = s["middle"], s["normed_two"], s["ff"], s["grad"]
    attended_grad, mixed_grad, turned = s["attended_grad"], s["mixed_grad"], s["turned"]
    mine, theirs, leaving, stage = s["mine"], s["theirs"], s["leaving"], s["stage"]
    cosine, sine, bias = s["cosine"], s["sine"], s["bias"]
    scale_one, scale_two, wide = s["scale_one"], s["scale_two"], s["wide"]
    place = Place()
    section, tensor = lax.axis_index("section"), lax.axis_index("tensor")
    over_tensor, over_section = {"tensor": 1 - tensor}, {"section": 1 - section}
    aslant = {"section": 1 - section, **place.device("x", 1 - place.at["x"])}

    barrier = pltpu.get_barrier_semaphore()
    for size, own, device in gain_axes(place):
        for k in range(1, size):
            pl.semaphore_signal(
                barrier, inc=1, device_id=device(lax.rem(own + k, size)), device_id_type=MESH
            )
    for device in (over_section, aslant):
        pl.semaphore_signal(barrier, inc=1, device_id=device, device_id_type=MESH)

    sources = (
        [(q_weight, 0), (q_weight, 1), (key_matrix, 0), (value_matrix, 0), (o_weight, 0), (o_weight, 1)],
        [(ref, k) for ref in (down_weight, gate_weight, up_weight) for k in range(3)],
    )

    def load(chunk):
        ref, part = sources[1][chunk] if chunk < MLP_CHUNKS else sources[0][chunk - MLP_CHUNKS]
        return pltpu.make_async_copy(
            ref.at[:, :, :, :, columns(part)], weights.at[chunk], s["weight_sem"].at[chunk]
        )

    def load_input(micro):
        rows = rows_of(micro)
        return pltpu.make_async_copy(block_input.at[rows], hidden.at[rows], s["input_sem"].at[micro])

    def load_cotangent(micro):
        rows = rows_of(micro)
        return pltpu.make_async_copy(cotangent.at[rows], grad.at[rows], s["input_sem"].at[micro])

    @pl.when(section == 0)
    def _():
        load_input(0).start()
        load_input(1).start()

    for chunk in (9, 10, 11, 12, 13, 14, 3, 6, 4, 7, 5, 8, 0, 1, 2):
        load(chunk).start()

    @pl.when(section == 1)
    def _():
        load_cotangent(0).start()
        load_cotangent(1).start()

    gains = scratch[-13]
    gains[0] = jnp.zeros((GAIN_ROWS, 128), F32)

    def tables(micro, carry):
        rows = rows_of(micro)
        ends = [lengths[micro, 0]]
        for k in (1, 2):
            ends.append(ends[-1] + lengths[micro, k])

        def begins(shape, dim=0):
            at = lax.broadcasted_iota(jnp.int32, shape, dim)
            found = jnp.zeros(shape, jnp.int32)
            for end in ends:
                found = jnp.where(at >= end, end, found)
            return at, found

        at, begin = begins((ROW, HEAD))
        chosen = (at - begin) == lax.broadcasted_iota(jnp.int32, (ROW, HEAD), 1)
        both = dot(chosen.astype(F32).astype(BF16), table[...])
        cosine[rows] = both[:, :128] + both[:, 128:256]
        sine[rows] = both[:, 256:384] + both[:, 384:]
        s["cosine_turned"][micro] = cosine[rows].T
        s["sine_turned"][micro] = sine[rows].T
        for dim, into in ((0, bias), (1, s["bias_turned"])):
            at, begin = begins((ROW, ROW), dim)
            key = lax.broadcasted_iota(jnp.int32, (ROW, ROW), 1 - dim)
            into[rows] = jnp.where((key >= begin) & (key <= at), 0.0, -1e9)
        return carry

    lax.fori_loop(0, 2, tables, 0)
    s["q_gain_turned"][...] = jnp.broadcast_to(q_gain[...], (HEAD, HEAD)).T
    s["q_gain_sum"][...] = jnp.zeros((HEAD, ROW), F32)

    pl.semaphore_wait(barrier, 10)

    def pair(slot, part):
        return remote(
            mine.at[slot, part],
            theirs.at[slot, part],
            s["mine_sem"].at[slot, part],
            s["theirs_sem"].at[slot, part],
            over_tensor,
        )

    def pair_start(slot, part, value):
        mine[slot, part] = value.astype(BF16)
        pair(slot, part).start()

    def pair_wait(slot):
        for part in range(2):
            pair(slot, part).wait()

    def pair_sum(slot, block):
        return jnp.concatenate(
            [
                mine[slot, part, block].astype(F32) + theirs[slot, part, block].astype(F32)
                for part in range(2)
            ],
            axis=1,
        )

    def half_rows(micro):
        return pl.ds(pl.multiple_of(micro * ROW + tensor * (ROW // 2), ROW // 2), ROW // 2)

    def cross(way, micro):
        rows = half_rows(micro)
        into = hidden if way == 0 else grad
        return remote(
            leaving.at[micro],
            into.at[rows],
            s["cross_send"].at[way, micro],
            s["cross_recv"].at[way, micro],
            over_section,
        )

    def arrive(way, micro):
        rows = half_rows(micro)
        into = hidden if way == 0 else grad
        cross(way, micro).wait_recv()
        relay = remote(
            into.at[rows],
            into.at[rows],
            s["relay_send"].at[way, micro],
            s["relay_recv"].at[way, micro],
            over_tensor,
        )
        relay.start()
        relay.wait()

    def pack(micro):
        for block in range(ROW // 2 // BLOCK):
            at = pl.multiple_of(micro * ROW + tensor * (ROW // 2) + block * BLOCK, BLOCK)
            leaving[micro, block * BLOCK : (block + 1) * BLOCK] = stage[pl.ds(at, BLOCK)].astype(BF16)

    def output(way, micro):
        rows = rows_of(micro)
        into = hidden_out if way == 0 else hidden_grad
        return pltpu.make_async_copy(stage.at[rows], into.at[rows], s["output_sem"].at[way, micro])

    def weight(chunk):
        return weights[chunk].reshape(WIDTH, CHUNK)

    def times_back(left, chunks, part):
        right = [weights[chunk, 2 * part : 2 * part + 2].reshape(CHUNK, CHUNK) for chunk in chunks]
        return dot(left, jnp.concatenate(right, axis=1), NT)

    def units(micro, *slots):
        found = [ff[slot, k, pl.ds(2 * micro, 2)].reshape(ROW, CHUNK) for slot in slots for k in range(3)]
        return jnp.concatenate(found, axis=1)

    def once(micro, chunks):
        @pl.when(micro == 0)
        def _():
            for chunk in chunks:
                load(chunk).wait()

    def rotated(value, cos, sin):
        return value * cos + pltpu.roll(value, HEAD // 2, 1) * sin

    def unrotated(value, cos, sin):
        return value * cos - pltpu.roll(value, HEAD // 2, 1) * sin

    def forward_one(micro):
        rows = rows_of(micro)

        @pl.when(section == 0)
        def _():
            load_input(micro).wait()

        @pl.when(section == 1)
        def _():
            arrive(0, micro)

        def norm_one(at, block, _):
            value = hidden[at].astype(F32)
            scale = inverse_rms(value)
            normed[at] = (value * scale * attn_gain[...]).astype(BF16)
            scale_one[at] = jnp.broadcast_to(scale, (BLOCK, 128))

        over_rows(micro, norm_one)
        once(micro, range(QUERY, OUT))
        for chunk in range(4):
            wide[0] = dot(normed[rows], weight(QUERY + chunk))
            if chunk == 3:
                heads[rows, columns(chunk)] = wide[0].astype(BF16)
                continue
            gain = q_gain if chunk < 2 else k_gain
            for k in range(4):
                value = wide[0, :, columns(k, HEAD)]
                heads[rows, columns(chunk * 4 + k, HEAD)] = value.astype(BF16)
                turn = rotated(value * inverse_rms(value) * gain[...], cosine[rows], sine[rows])
                if chunk < 2:
                    query_rot[rows, columns(chunk * 4 + k, HEAD)] = turn.astype(BF16)
                else:
                    key_rot[rows, columns(k, HEAD)] = turn.astype(BF16)

        ones = jnp.ones((ROW, HEAD), BF16)

        def attend(group):
            keys = key_rot[rows, columns(group, HEAD)]
            values = heads[rows, columns(12 + group, HEAD)]
            for k in range(2):
                head = 2 * group + k
                scores = dot(query_rot[rows, columns(head, HEAD)], keys, NT)
                low = jnp.exp2(scores * (SCORE_SCALE * LOG2_E) + bias[rows]).astype(BF16)
                both = dot(low, jnp.concatenate([values, ones], axis=1))
                inverse = 1.0 / both[:, HEAD:]
                heads[rows, columns(16 + head, HEAD)] = (both[:, :HEAD] * inverse).astype(BF16)

        for index in range(4):
            attend(index)
        once(micro, (OUT, OUT + 1))

        def attended(part):
            value = times_back(heads[rows, 2048:], (OUT, OUT + 1), part)
            pair_start(0, part, value)

        for index in range(2):
            attended(index)

    def forward_two(micro):
        rows = rows_of(micro)
        pair_wait(0)

        def norm_two(at, block, _):
            value = hidden[at].astype(F32) + pair_sum(0, block)
            middle[at] = value
            scale = inverse_rms(value)
            normed_two[at] = (value * scale * mlp_gain[...]).astype(BF16)
            scale_two[at] = jnp.broadcast_to(scale, (BLOCK, 128))

        over_rows(micro, norm_two)
        once(micro, range(QUERY))

        def hidden_units(chunk):
            wide[0] = dot(normed_two[rows], weight(GATE + chunk))
            wide[1] = dot(normed_two[rows], weight(UP + chunk))

            def silu(at, block, place_in):
                gate, up = wide[0, block], wide[1, block]
                ff[1, chunk, *place_in] = gate.astype(BF16)
                ff[2, chunk, *place_in] = up.astype(BF16)
                ff[0, chunk, *place_in] = (gate * jax.nn.sigmoid(gate) * up).astype(BF16)

            over_rows(micro, silu)

        for index in range(3):
            hidden_units(index)

        def moved(part):
            value = times_back(units(micro, 0), range(DOWN, GATE), part)
            pair_start(1, part, value)

        for index in range(2):
            moved(index)

    def forward_three(micro):
        pair_wait(1)

        def result(at, block, _):
            stage[at] = middle[at] + pair_sum(1, block)

        over_rows(micro, result)
        output(0, micro).start()

        @pl.when(section == 0)
        def _():
            pack(micro)
            cross(0, micro).start()

    def norm_back(total, value, scale, gain):
        inner = total * gain
        return scale * inner - value * (scale * scale * scale) * jnp.mean(
            inner * value, axis=-1, keepdims=True
        )

    def add_gain(row, value):
        gains[0, row : row + 1] = gains[0, row : row + 1] + value

    def add_gains(row, part, value):
        for k in range(4):
            at = slice(row + part * 4 + k, row + part * 4 + k + 1)
            gains[0, at] = gains[0, at] + value[:, k * 128 : (k + 1) * 128]

    def turn(slot, value):
        for k in range(4):
            turned[slot, k] = value[:, columns(k, 256)].T.reshape(2, 4, 32, CHUNK)

    def weight_grad(chunk, slot, right):
        for part in range(4):
            value = dot(turned[slot, part].reshape(256, CHUNK), right)
            weights[chunk, part] = value.astype(BF16).reshape(2, 4, 32, CHUNK)

    rings = []
    for first, (order, count) in enumerate(zip(ORDERS, COUNTS)):
        own, scratch = scratch[:9], scratch[9:]

        def finish(i, half, total, first=first):
            grads_out[2 * i + first] = total

        def chunk_at(i, first=first):
            return (2 * i + first,)

        rings.append((count, LAGS, ring_stages(order, weights, chunk_at, own, place, finish)))

    def kept(chunk):
        return (section == 1) | (lax.rem(chunk, 3) > 0) | (chunk >= MLP_CHUNKS)

    def ring_start(chunk):
        for first in (0, 1):

            @pl.when((lax.rem(chunk, 2) == first) & kept(chunk))
            def _(first=first):
                rings[first][2][0]((chunk - first) // 2)

        @pl.when(jnp.logical_not(kept(chunk)))
        def _():
            leave(chunk // 3, 0).start()
            leave(chunk // 3, 1).start()

    def leave(i, slant):
        side = place.at["x"]
        return remote(
            weights.at[3 * i, :, 1 - side if slant else side],
            ff.at[i, side],
            s["left_send"].at[i, slant],
            s["left_recv"].at[i, side],
            aslant if slant else over_section,
        )

    def left_arrival(i, side):
        return remote(
            weights.at[3 * i, :, side],
            ff.at[i, side],
            s["left_send"].at[i, side],
            s["left_recv"].at[i, side],
            over_section,
        )

    def give_back(i):
        return remote(
            s["left_sum"].at[i],
            s["left_done"].at[i],
            s["done_send"].at[i],
            s["done_recv"].at[i],
            over_section,
        )

    def left_start(i):
        for side in (0, 1):
            left_arrival(i, side).wait_recv()
        ff[i, 2] = (ff[i, 0].astype(F32) + ff[i, 1].astype(F32)).astype(BF16)

    def left_finish(i, half, total):
        s["left_sum"][i, half * 16 : half * 16 + 16] = total
        if half:
            give_back(i).start()

    own, scratch = scratch[:6], scratch[6:]
    left_stages = [left_start] + ring_stages(
        LEFT_ORDER, ff, lambda i: (i, 2), own, place, left_finish, skipped=("x",)
    )

    def backward_one(micro):
        rows = rows_of(micro)

        @pl.when(section == 0)
        def _():
            arrive(1, micro)
            cross(0, micro).wait_send()

        @pl.when(section == 1)
        def _():
            load_cotangent(micro).wait()

        def hidden_back(chunk):
            wide[0] = dot(grad[rows], weight(DOWN + chunk))

            def silu_back(at, block, place_in):
                act_grad = wide[0, block]
                gate, up = ff[1, chunk, *place_in].astype(F32), ff[2, chunk, *place_in].astype(F32)
                sigma = jax.nn.sigmoid(gate)
                passed = act_grad * sigma
                ff[1, chunk, *place_in] = (passed * up * (1.0 + gate * (1.0 - sigma))).astype(BF16)
                ff[2, chunk, *place_in] = (passed * gate).astype(BF16)

            over_rows(micro, silu_back)

        for index in range(3):
            hidden_back(index)

        def normed_two_back(part):
            value = times_back(units(micro, 1, 2), range(GATE, QUERY), part)
            pair_start(2, part, value)
            scaled = middle[rows, columns(part)] * scale_two[rows, :1]
            add_gains(8, part, jnp.sum(value * scaled, axis=0, keepdims=True))

        def mlp_grad(chunk, carry):
            weight_grad(chunk, jnp.minimum(chunk // 3, 1), ff[chunk // 3, lax.rem(chunk, 3)].reshape(2 * ROW, CHUNK))
            ring_start(chunk)
            return carry

        @pl.when(micro == 1)
        def _():
            turn(0, grad)

            @pl.when(section == 0)
            def _():
                pl.semaphore_wait(s["left_free"], 2)

            lax.fori_loop(DOWN, GATE, mlp_grad, 0)

        for index in range(2):
            normed_two_back(index)

        @pl.when(micro == 1)
        def _():
            @pl.when(section == 1)
            def _():
                turn(1, normed_two)

            lax.fori_loop(GATE, QUERY, mlp_grad, 0)

            @pl.when(section == 1)
            def _():
                for device in (over_section, aslant):
                    pl.semaphore_signal(
                        s["left_free"], inc=1, device_id=device, device_id_type=MESH
                    )

    def backward_two(micro):
        rows = rows_of(micro)
        pair_wait(2)
        output(0, micro).wait()

        def middle_back(at, block, _):
            value = grad[at].astype(F32) + norm_back(
                pair_sum(2, block), middle[at], scale_two[at, :1], mlp_gain[...]
            )
            stage[at] = value
            attended_grad[at] = value.astype(BF16)

        over_rows(micro, middle_back)

        for k in range(2):
            mixed_grad[:, columns(k)] = dot(attended_grad[rows], weight(OUT + k)).astype(BF16)

        def attend_back(group):
            cos, sin = cosine[rows], sine[rows]
            cos_turned, sin_turned = s["cosine_turned"][micro], s["sine_turned"][micro]
            gain_turned = jnp.concatenate([s["q_gain_turned"][...]] * 2, axis=1)
            keys = key_rot[rows, columns(group, HEAD)]
            keys_turned = keys.T
            values = heads[rows, columns(12 + group, HEAD)]
            key_rot_grad = jnp.zeros((ROW, HEAD), F32)
            value_grad = jnp.zeros((ROW, HEAD), F32)
            for k in range(2):
                head = 2 * group + k
                here = columns(head, HEAD)
                queries = query_rot[rows, here]
                out_grad = mixed_grad[:, here]
                scores = dot(keys, queries, NT)
                raw = jnp.exp2(scores * (SCORE_SCALE * LOG2_E) + s["bias_turned"][rows])
                chance = raw * (1.0 / jnp.sum(raw, axis=0, keepdims=True))
                weighted = chance * dot(values, out_grad, NT)
                across = jnp.sum(weighted, axis=0, keepdims=True)
                score_grad = (weighted - chance * across).astype(BF16)
                value_grad = value_grad + dot(chance.astype(BF16), out_grad)
                key_rot_grad = key_rot_grad + dot(score_grad, queries)
                passed = dot(keys_turned, score_grad) * SCORE_SCALE
                swapped = jnp.concatenate([passed[HEAD // 2 :], passed[: HEAD // 2]], axis=0)
                turn_grad = passed * cos_turned - swapped * sin_turned
                query = heads[rows, here].T.astype(F32)
                scale = lax.rsqrt(jnp.mean(query * query, axis=0, keepdims=True) + EPSILON)
                scaled = query * scale
                s["q_gain_sum"][...] = s["q_gain_sum"][...] + turn_grad * scaled
                inner = turn_grad * gain_turned
                query_grad = scale * (inner - scaled * jnp.mean(inner * scaled, axis=0, keepdims=True))
                heads[rows, here] = query_grad.astype(BF16).T
            turn_grad = unrotated(key_rot_grad * SCORE_SCALE, cos, sin)
            here = columns(8 + group, HEAD)
            key = heads[rows, here].astype(F32)
            scale = inverse_rms(key)
            add_gain(17, jnp.sum(turn_grad * key * scale, axis=0, keepdims=True))
            heads[rows, here] = norm_back(turn_grad, key, scale, k_gain[...]).astype(BF16)
            heads[rows, columns(12 + group, HEAD)] = value_grad.astype(BF16)

        for index in range(4):
            attend_back(index)

        def normed_back(part):
            value = times_back(heads[rows, :2048], range(QUERY, OUT), part)
            pair_start(3, part, value)
            scaled = hidden[rows, columns(part)].astype(F32) * scale_one[rows, :1]
            add_gains(0, part, jnp.sum(value * scaled, axis=0, keepdims=True))

        for index in range(2):
            normed_back(index)
    def backward_three(micro):
        pair_wait(3)

        def hidden_back_end(at, block, _):
            stage[at] = stage[at] + norm_back(
                pair_sum(3, block), hidden[at].astype(F32), scale_one[at, :1], attn_gain[...]
            )

        over_rows(micro, hidden_back_end)
        output(1, micro).start()

        @pl.when(section == 1)
        def _():
            pack(micro)
            cross(1, micro).start()

    def step(turn_of, carry):
        back = turn_of - 2 + section

        @pl.when((turn_of == 2) & (section == 0))
        def _():
            turn(1, normed_two)

        for ahead, behind in (
            (forward_one, backward_one),
            (forward_two, backward_two),
            (forward_three, backward_three),
        ):

            @pl.when((back >= 0) & (back < 2))
            def _(behind=behind):
                behind(back)

            @pl.when(turn_of < 2)
            def _(ahead=ahead):
                ahead(turn_of)

        return carry

    lax.fori_loop(0, 4, step, 0)

    add_gain(16, jnp.sum(s["q_gain_sum"][...].T, axis=0, keepdims=True))
    turn(0, normed)
    turn(1, attended_grad)

    def attention_grad(chunk, carry):
        weight_grad(MLP_CHUNKS + chunk, chunk // 4, heads[:, columns(chunk)])
        ring_start(MLP_CHUNKS + chunk)
        return carry

    lax.fori_loop(0, CHUNKS - MLP_CHUNKS, attention_grad, 0)

    def always(i):
        return True

    groups = [
        (count, (None, *lags[1:]), stages, lambda i, first=first: kept(2 * i + first))
        for first, (count, lags, stages) in enumerate(rings)
    ]
    groups.append(
        (LEFT, [LEFT_FROM + lag for lag in LEFT_LAGS], left_stages, lambda i: section == 1)
    )
    groups.append((1, (0, 2, 2, 4, 4, 6, 6, 8), gain_stages(gains_out, scratch, place), always))

    def advance(now, carry):
        for step in range(8):
            for count, lags, stages, runs in groups:
                if step >= len(stages) or lags[step] is None:
                    continue
                i = now - lags[step]

                @pl.when((i >= 0) & (i < count) & runs(i))
                def _(i=i, run=stages[step]):
                    run(i)

        return carry

    lax.fori_loop(0, max(count + lags[-1] for count, lags, _, _ in groups), advance, 0)

    @pl.when(section == 0)
    def _():
        for i in range(LEFT):
            leave(i, 0).wait_send()
            leave(i, 1).wait_send()
            give_back(i).wait_recv()
            grads_out[3 * i] = s["left_done"][i]

    @pl.when(section == 1)
    def _():
        for i in range(LEFT):
            give_back(i).wait_send()

    for micro in range(2):
        output(1, micro).wait()

        @pl.when(section == 1)
        def _(micro=micro):
            cross(1, micro).wait_send()


def rope_table():
    half = HEAD // 2
    rates = THETA ** (-2.0 * np.arange(half) / HEAD)
    angle = np.arange(HEAD)[:, None] * np.concatenate([rates, rates])[None]
    sign = np.where(np.arange(HEAD) < half, -1.0, 1.0)
    parts = []
    for value in (np.cos(angle), np.sin(angle) * sign):
        high = value.astype(jnp.bfloat16)
        parts += [high, (value - high.astype(np.float64)).astype(jnp.bfloat16)]
    return jnp.asarray(np.concatenate(parts, axis=1))


def by_place(weight):
    return weight.reshape(4, 2, 4, 32, weight.shape[-1])


def shards(
    block_input,
    doc_lengths,
    out_cotangent,
    attn_gain,
    q_gain,
    k_gain,
    mlp_gain,
    q_weight,
    key_matrix,
    value_matrix,
    o_weight,
    gate_weight,
    up_weight,
    down_weight,
):
    vmem = pl.BlockSpec(memory_space=pltpu.VMEM)
    smem = pl.BlockSpec(memory_space=pltpu.SMEM)
    anywhere = pl.BlockSpec(memory_space=pl.ANY)
    scratch = list(SCRATCH.values())
    for order, count in zip(ORDERS, COUNTS):
        scratch += ring_scratch(order, count)
    scratch += ring_scratch(LEFT_ORDER, LEFT, 1)
    scratch += gain_scratch()
    full = jax.ShapeDtypeStruct(block_input.shape, F32)
    outputs, grads_in, grads, gains = pl.pallas_call(
        kernel,
        out_shape=(
            full,
            full,
            jax.ShapeDtypeStruct((CHUNKS, 32, CHUNK), F32),
            jax.ShapeDtypeStruct((1, GAIN_ROWS * 128), F32),
        ),
        in_specs=[smem, anywhere, anywhere] + [vmem] * 4 + [anywhere] * 7 + [vmem],
        out_specs=[anywhere, anywhere, vmem, vmem],
        scratch_shapes=scratch,
        compiler_params=pltpu.CompilerParams(
            collective_id=0, has_side_effects=True, vmem_limit_bytes=64 * 2**20 - 2**16
        ),
    )(
        doc_lengths,
        block_input,
        out_cotangent,
        attn_gain,
        q_gain,
        k_gain,
        mlp_gain,
        by_place(q_weight),
        by_place(key_matrix),
        by_place(value_matrix),
        by_place(o_weight),
        by_place(gate_weight),
        by_place(up_weight),
        by_place(down_weight),
        rope_table(),
    )

    return spread(outputs, grads_in, grads, gains)


MATRICES = ((QUERY, 2), (KEY, 1), (VALUE, 1), (OUT, 2), (GATE, 3), (UP, 3), (DOWN, 3))
GAIN_PARTS = ((0, 1024), (2048, 128), (2176, 128), (1024, 1024))


def spread_kernel(outputs, grads_in, grads, gains, *refs):
    results, (tokens, matrices, row, in_sem, out_sem) = refs[:-5], refs[-5:]
    loads, stores = [], []

    def through(src, held, pairs):
        load = pltpu.make_async_copy(src, held, in_sem.at[len(loads)])
        load.start()
        loads.append((load, pairs))

    through(grads, matrices, [])
    for k in range(8):
        rows = pl.ds(k % 4 * 128, 128)
        src, into = ((outputs, results[0]), (grads_in, results[1]))[k // 4]
        through(src.at[rows], tokens.at[k], [(tokens.at[k], into.at[0, rows])])
    through(gains, row, [])
    for (first, count), into in zip(MATRICES, results[6:]):
        for k in range(count):
            pair = (matrices.at[first + k], into.at[0, :, k * CHUNK : (k + 1) * CHUNK])
            loads[0][1].append(pair)
    for (first, size), into in zip(GAIN_PARTS, results[2:6]):
        loads[-1][1].append((row.at[:, first : first + size], into))
    for load, pairs in loads:
        load.wait()
        for src, dst in pairs:
            store = pltpu.make_async_copy(src, dst, out_sem.at[len(stores)])
            store.start()
            stores.append(store)
    for store in stores:
        store.wait()


def spread(outputs, grads_in, grads, gains):
    shapes = [(1, *outputs.shape)] * 2 + [(1, size) for _, size in GAIN_PARTS]
    shapes += [(1, 32, count * CHUNK) for _, count in MATRICES]
    anywhere = pl.BlockSpec(memory_space=pl.ANY)
    return pl.pallas_call(
        spread_kernel,
        out_shape=[jax.ShapeDtypeStruct(shape, F32) for shape in shapes],
        in_specs=[anywhere] * 4,
        out_specs=[anywhere] * len(shapes),
        scratch_shapes=[
            pltpu.VMEM((8, 128, outputs.shape[1]), F32),
            pltpu.VMEM(grads.shape, F32),
            pltpu.VMEM(gains.shape, F32),
            pltpu.SemaphoreType.DMA((10,)),
            pltpu.SemaphoreType.DMA((27,)),
        ],
        compiler_params=pltpu.CompilerParams(vmem_limit_bytes=16 * 2**20),
    )(outputs, grads_in, grads, gains)


def solution(mesh):
    weight = P("section", None, "tensor")
    gain = P("section", None)
    tokens = P("section", "dp", None)
    grad = P("section", "dp", "tensor")
    return jax.shard_map(
        shards,
        mesh=mesh,
        in_specs=(P("dp", None),) * 3 + (gain,) * 4 + (weight,) * 7,
        out_specs=(tokens,) * 2 + (gain,) * 4 + (grad,) * 7,
        check_vma=False,
    )
```

```python
import functools

import jax
import jax.numpy as jnp
import numpy as np
from jax import lax
from jax.experimental import pallas as pl
from jax.experimental.pallas import tpu as pltpu
from jax.sharding import PartitionSpec as P

EPSILON = 1e-06
THETA = 1000000.0
HEAD = 128
ROW = 256
WIDTH = 1024
BLOCK = 32
SCORE_SCALE = HEAD ** (-0.5)
LOG2_E = 1.4426950408889634
MESH = pl.DeviceIdType.MESH
BF16, F32 = jnp.bfloat16, jnp.float32
NT = (((1,), (1,)), ((), ()))
TN = (((0,), (0,)), ((), ()))

CHUNK = 512
DOWN, GATE, UP, QUERY, KEY, VALUE, OUT = 0, 3, 6, 9, 11, 12, 13
CHUNKS = 15
MLP_CHUNKS = 9
SOON = 7
ORDERS = (("z", "y", "x"), ("y", "z", "x"))
COUNTS = (8, 7)
LAGS = (0, 0, 2, 2, 4, 6, 6, 8)
LEFT = 3
LEFT_ORDER = ("x", "y", "z")
LEFT_LAGS = (0, 0, 1, 2, 2, 3, 4)
LEFT_FROM = 6
GAIN_ROWS = 24


def remote(src, dst, send_sem, recv_sem, device):
    return pltpu.make_async_remote_copy(
        src_ref=src,
        dst_ref=dst,
        send_sem=send_sem,
        recv_sem=recv_sem,
        device_id=device,
        device_id_type=MESH,
    )


def dot(left, right, form=None):
    if form is None:
        return jnp.dot(left, right, preferred_element_type=F32)
    return lax.dot_general(left, right, form, preferred_element_type=F32)


class Place:
    def __init__(self):
        dp = lax.axis_index("dp")
        self.at = {"z": dp // 8, "x": dp // 4 % 2, "y": dp % 4}

    def device(self, axis, index):
        at = {**self.at, axis: index}
        return {"dp": at["z"] * 8 + at["x"] * 4 + at["y"]}


def ring_phases(order):
    found, done = [], []
    for axis in order:
        left = [name for name in ("z", "x", "y") if name not in done and name != axis]
        halved = None if axis == "x" else "x" if "x" in left else left[0] if left else "row"
        shape = []
        for name in left:
            size = 2 if name == "x" else 4
            shape.append(size // 2 if name == halved else size)
        rows = 16 if halved == "row" else 32
        found.append((axis, tuple(done), halved, (*shape, rows, CHUNK)))
        done.append(axis)
    return found


def ring_scratch(order, count, skipped=0):
    found = []
    for _, _, halved, shape in ring_phases(order)[skipped:]:
        parts = 6 if halved else 1
        found.append(pltpu.VMEM((count, parts, *shape), BF16))
        found.append(pltpu.SemaphoreType.DMA((count, parts)))
        found.append(pltpu.SemaphoreType.DMA((count, parts)))
    return found


def ring_stages(order, grads, at_first, scratch, place, finish, skipped=()):
    stages = []
    phases = ring_phases(order)[len(skipped) :]
    for step, (axis, done, halved, _) in enumerate(phases):
        arrived, send_sem, recv_sem = scratch[3 * step : 3 * step + 3]
        mine = place.at[axis]

        def where(i, index, half, axis=axis, done=done, halved=halved):
            found = list(at_first(i))
            for name in ("z", "x", "y"):
                if name in skipped:
                    continue
                if name in done:
                    found.append(place.at[name])
                elif name == axis:
                    found.append(index)
                elif name == halved:
                    size = 1 if name == "x" else 2
                    found.append(pl.ds(half * size, size))
                else:
                    found.append(slice(None))
            if halved == "row":
                found.append(pl.ds(half * 16, 16))
            return tuple(found)

        def put(i, half, total, step=step, mine=mine, where=where):
            if step == len(phases) - 1:
                finish(i, half, total)
            else:
                grads[where(i, mine, half)] = total.astype(BF16)

        if halved is None:

            def swap(
                i, where=where, arrived=arrived, send_sem=send_sem, recv_sem=recv_sem, mine=mine, axis=axis
            ):
                return remote(
                    grads.at[where(i, 1 - mine, 0)],
                    arrived.at[i, 0],
                    send_sem.at[i, 0],
                    recv_sem.at[i, 0],
                    place.device(axis, 1 - mine),
                )

            def start(i, swap=swap):
                swap(i).start()

            def end(i, swap=swap, arrived=arrived, where=where, mine=mine, put=put):
                swap(i).wait()
                put(i, 0, grads[where(i, mine, 0)].astype(F32) + arrived[i, 0].astype(F32))

            stages += [start, end]
            continue

        right, left = lax.rem(mine + 1, 4), lax.rem(mine + 3, 4)
        across = lax.rem(mine + 2, 4)
        sends = (
            (across, 0, right),
            (across, 1, left),
            (right, 1, right),
            (left, 0, left),
            (right, 0, right),
            (left, 1, left),
        )

        def send(
            i, k, where=where, arrived=arrived, send_sem=send_sem, recv_sem=recv_sem, axis=axis, sends=sends
        ):
            index, half, to = sends[k]
            return remote(
                grads.at[where(i, index, half)],
                arrived.at[i, k],
                send_sem.at[i, k],
                recv_sem.at[i, k],
                place.device(axis, to),
            )

        def start(i, send=send):
            for k in range(4):
                send(i, k).start()

        def pass_on(i, send=send, arrived=arrived, where=where, sends=sends):
            for k in (0, 1):
                send(i, k).wait_recv()
                index, half, _ = sends[4 + k]
                at = where(i, index, half)
                grads[at] = (grads[at].astype(F32) + arrived[i, k].astype(F32)).astype(BF16)
                send(i, 4 + k).start()

        def end(i, send=send, arrived=arrived, where=where, mine=mine, put=put):
            for k in range(2, 6):
                send(i, k).wait_recv()
            for k in range(6):
                send(i, k).wait_send()
            for half in (0, 1):
                own = grads[where(i, mine, half)].astype(F32)
                near = arrived[i, 4 - 2 * half].astype(F32)
                far = arrived[i, 3 + 2 * half].astype(F32)
                put(i, half, own + near + far)

        stages += [start, pass_on, end]
    return stages


def gain_scratch():
    found = [pltpu.VMEM((4, GAIN_ROWS, 128), F32)]
    for size in (4, 4, 2, 2):
        found.append(pltpu.SemaphoreType.DMA((size,)))
        found.append(pltpu.SemaphoreType.DMA((size,)))
        found.append(pltpu.VMEM((size, GAIN_ROWS, 128), F32))
    return found


def gain_axes(place):
    return (
        (4, place.at["y"], lambda k: place.device("y", k)),
        (4, place.at["z"], lambda k: place.device("z", k)),
        (2, place.at["x"], lambda k: place.device("x", k)),
        (2, lax.axis_index("tensor"), lambda k: {"tensor": k}),
    )


def gain_stages(total_ref, scratch, place):
    held = scratch[0]
    stages = []
    for step, (size, mine, device) in enumerate(gain_axes(place)):
        send_sem, recv_sem, slots = scratch[1 + 3 * step : 4 + 3 * step]
        src = held.at[step]
        dst = total_ref if step == 3 else held.at[step + 1]

        def send(k, src=src, slots=slots, send_sem=send_sem, recv_sem=recv_sem, size=size, mine=mine, device=device):
            to = lax.rem(mine + k, size)
            return remote(src, slots.at[mine], send_sem.at[k], recv_sem.at[mine], device(to))

        def arrival(k, src=src, slots=slots, send_sem=send_sem, recv_sem=recv_sem, size=size, mine=mine, device=device):
            frm = lax.rem(mine + k, size)
            return remote(src, slots.at[frm], send_sem.at[k], recv_sem.at[frm], device(frm))

        def start(i, send=send, src=src, slots=slots, size=size, mine=mine):
            slots[mine] = src[...]
            for k in range(1, size):
                send(k).start()

        def end(i, send=send, arrival=arrival, slots=slots, size=size, dst=dst):
            for k in range(1, size):
                arrival(k).wait_recv()
                send(k).wait_send()
            total = slots[0]
            for k in range(1, size):
                total = total + slots[k]
            if dst is total_ref:
                for k in range(GAIN_ROWS):
                    dst[:, k * 128 : (k + 1) * 128] = total[k : k + 1]
            else:
                dst[...] = total

        stages += [start, end]
    return stages


SCRATCH = dict(
    weights=pltpu.VMEM((CHUNKS, 4, 2, 4, 32, CHUNK), BF16),
    hidden=pltpu.VMEM((2 * ROW, WIDTH), BF16),
    normed=pltpu.VMEM((2 * ROW, WIDTH), BF16),
    heads=pltpu.VMEM((2 * ROW, 3072), BF16),
    query_rot=pltpu.VMEM((2 * ROW, 1024), BF16),
    key_rot=pltpu.VMEM((2 * ROW, 512), BF16),
    middle=pltpu.VMEM((2 * ROW, WIDTH), F32),
    normed_two=pltpu.VMEM((2 * ROW, WIDTH), BF16),
    ff=pltpu.VMEM((3, 3, 4, 4, 32, CHUNK), BF16),
    grad=pltpu.VMEM((2 * ROW, WIDTH), BF16),
    attended_grad=pltpu.VMEM((2 * ROW, WIDTH), BF16),
    mixed_grad=pltpu.VMEM((ROW, 1024), BF16),
    turned=pltpu.VMEM((2, 4, 2, 4, 32, CHUNK), BF16),
    mine=pltpu.VMEM((4, 2, ROW, CHUNK), BF16),
    theirs=pltpu.VMEM((4, 2, ROW, CHUNK), BF16),
    leaving=pltpu.VMEM((2, 2, ROW // 2, CHUNK), BF16),
    stage=pltpu.VMEM((2 * ROW, WIDTH), F32),
    cosine=pltpu.VMEM((2 * ROW, HEAD), F32),
    sine=pltpu.VMEM((2 * ROW, HEAD), F32),
    bias=pltpu.VMEM((2 * ROW, ROW), F32),
    cosine_turned=pltpu.VMEM((2, HEAD, ROW), F32),
    sine_turned=pltpu.VMEM((2, HEAD, ROW), F32),
    bias_turned=pltpu.VMEM((2 * ROW, ROW), F32),
    q_gain_turned=pltpu.VMEM((HEAD, HEAD), F32),
    q_gain_sum=pltpu.VMEM((HEAD, ROW), F32),
    scale_one=pltpu.VMEM((2 * ROW, 128), F32),
    scale_two=pltpu.VMEM((2 * ROW, 128), F32),
    wide=pltpu.VMEM((2, ROW, CHUNK), F32),
    weight_sem=pltpu.SemaphoreType.DMA((CHUNKS,)),
    input_sem=pltpu.SemaphoreType.DMA((2,)),
    output_sem=pltpu.SemaphoreType.DMA((2, 2)),
    mine_sem=pltpu.SemaphoreType.DMA((4, 2)),
    theirs_sem=pltpu.SemaphoreType.DMA((4, 2)),
    cross_send=pltpu.SemaphoreType.DMA((2, 2, 2)),
    cross_recv=pltpu.SemaphoreType.DMA((2, 2, 2)),
    relay_send=pltpu.SemaphoreType.DMA((2, 2, 2)),
    relay_recv=pltpu.SemaphoreType.DMA((2, 2, 2)),
    left_send=pltpu.SemaphoreType.DMA((LEFT, 2)),
    left_recv=pltpu.SemaphoreType.DMA((LEFT, 2)),
    left_sum=pltpu.VMEM((LEFT, 32, CHUNK), F32),
    left_done=pltpu.VMEM((LEFT, 32, CHUNK), F32),
    done_send=pltpu.SemaphoreType.DMA((LEFT,)),
    done_recv=pltpu.SemaphoreType.DMA((LEFT,)),
    left_free=pltpu.SemaphoreType.REGULAR,
)


def rows_of(micro):
    return pl.ds(pl.multiple_of(micro * ROW, ROW), ROW)


def over_rows(micro, body):
    for block in range(ROW // BLOCK):
        body(
            pl.ds(pl.multiple_of(micro * ROW + block * BLOCK, BLOCK), BLOCK),
            pl.ds(block * BLOCK, BLOCK),
            (2 * micro + block // 4, block % 4),
        )


def columns(index, size=CHUNK):
    if isinstance(index, int):
        return pl.ds(index * size, size)
    return pl.ds(pl.multiple_of(index * size, size), size)


def inverse_rms(value):
    return lax.rsqrt(jnp.mean(value * value, axis=-1, keepdims=True) + EPSILON)


def kernel(
    lengths,
    block_input,
    cotangent,
    attn_gain,
    q_gain,
    k_gain,
    mlp_gain,
    q_weight,
    key_matrix,
    value_matrix,
    o_weight,
    gate_weight,
    up_weight,
    down_weight,
    table,
    hidden_out,
    hidden_grad,
    grads_out,
    gains_out,
    *scratch,
):
    s = dict(zip(SCRATCH, scratch))
    scratch = scratch[len(SCRATCH) :]
    weights, hidden, normed, heads = s["weights"], s["hidden"], s["normed"], s["heads"]
    query_rot, key_rot = s["query_rot"], s["key_rot"]
    middle, normed_two, ff, grad = s["middle"], s["normed_two"], s["ff"], s["grad"]
    attended_grad, mixed_grad, turned = s["attended_grad"], s["mixed_grad"], s["turned"]
    mine, theirs, leaving, stage = s["mine"], s["theirs"], s["leaving"], s["stage"]
    cosine, sine, bias = s["cosine"], s["sine"], s["bias"]
    scale_one, scale_two, wide = s["scale_one"], s["scale_two"], s["wide"]
    place = Place()
    section, tensor = lax.axis_index("section"), lax.axis_index("tensor")
    over_tensor, over_section = {"tensor": 1 - tensor}, {"section": 1 - section}
    aslant = {"section": 1 - section, **place.device("x", 1 - place.at["x"])}

    barrier = pltpu.get_barrier_semaphore()
    for size, own, device in gain_axes(place):
        for k in range(1, size):
            pl.semaphore_signal(
                barrier, inc=1, device_id=device(lax.rem(own + k, size)), device_id_type=MESH
            )
    for device in (over_section, aslant):
        pl.semaphore_signal(barrier, inc=1, device_id=device, device_id_type=MESH)

    sources = (
        [(q_weight, 0), (q_weight, 1), (key_matrix, 0), (value_matrix, 0), (o_weight, 0), (o_weight, 1)],
        [(ref, k) for ref in (down_weight, gate_weight, up_weight) for k in range(3)],
    )

    def load(chunk):
        ref, part = sources[1][chunk] if chunk < MLP_CHUNKS else sources[0][chunk - MLP_CHUNKS]
        return pltpu.make_async_copy(
            ref.at[:, :, :, :, columns(part)], weights.at[chunk], s["weight_sem"].at[chunk]
        )

    def load_input(micro):
        rows = rows_of(micro)
        return pltpu.make_async_copy(block_input.at[rows], hidden.at[rows], s["input_sem"].at[micro])

    def load_cotangent(micro):
        rows = rows_of(micro)
        return pltpu.make_async_copy(cotangent.at[rows], grad.at[rows], s["input_sem"].at[micro])

    @pl.when(section == 0)
    def _():
        load_input(0).start()
        load_input(1).start()

    for chunk in (9, 10, 11, 12, 13, 14, 3, 6, 4, 7, 5, 8, 0, 1, 2):
        load(chunk).start()

    @pl.when(section == 1)
    def _():
        load_cotangent(0).start()
        load_cotangent(1).start()

    gains = scratch[-13]
    gains[0] = jnp.zeros((GAIN_ROWS, 128), F32)

    def tables(micro, carry):
        rows = rows_of(micro)
        ends = [lengths[micro, 0]]
        for k in (1, 2):
            ends.append(ends[-1] + lengths[micro, k])

        def begins(shape, dim=0):
            at = lax.broadcasted_iota(jnp.int32, shape, dim)
            found = jnp.zeros(shape, jnp.int32)
            for end in ends:
                found = jnp.where(at >= end, end, found)
            return at, found

        at, begin = begins((ROW, HEAD))
        chosen = (at - begin) == lax.broadcasted_iota(jnp.int32, (ROW, HEAD), 1)
        both = dot(chosen.astype(F32).astype(BF16), table[...])
        cosine[rows] = both[:, :128] + both[:, 128:256]
        sine[rows] = both[:, 256:384] + both[:, 384:]
        s["cosine_turned"][micro] = cosine[rows].T
        s["sine_turned"][micro] = sine[rows].T
        for dim, into in ((0, bias), (1, s["bias_turned"])):
            at, begin = begins((ROW, ROW), dim)
            key = lax.broadcasted_iota(jnp.int32, (ROW, ROW), 1 - dim)
            into[rows] = jnp.where((key >= begin) & (key <= at), 0.0, -1e9)
        return carry

    lax.fori_loop(0, 2, tables, 0)
    s["q_gain_turned"][...] = jnp.broadcast_to(q_gain[...], (HEAD, HEAD)).T
    s["q_gain_sum"][...] = jnp.zeros((HEAD, ROW), F32)

    pl.semaphore_wait(barrier, 10)

    def pair(slot, part):
        return remote(
            mine.at[slot, part],
            theirs.at[slot, part],
            s["mine_sem"].at[slot, part],
            s["theirs_sem"].at[slot, part],
            over_tensor,
        )

    def pair_start(slot, part, value):
        mine[slot, part] = value.astype(BF16)
        pair(slot, part).start()

    def pair_wait(slot):
        for part in range(2):
            pair(slot, part).wait()

    def pair_part(slot, part, block):
        return mine[slot, part, block].astype(F32) + theirs[slot, part, block].astype(F32)

    def pair_sum(slot, block):
        return jnp.concatenate(
            [
                mine[slot, part, block].astype(F32) + theirs[slot, part, block].astype(F32)
                for part in range(2)
            ],
            axis=1,
        )

    def half_rows(micro):
        return pl.ds(pl.multiple_of(micro * ROW + tensor * (ROW // 2), ROW // 2), ROW // 2)

    def cross(way, micro, part):
        into = hidden if way == 0 else grad
        return remote(
            leaving.at[micro, part],
            into.at[half_rows(micro), columns(part)],
            s["cross_send"].at[way, micro, part],
            s["cross_recv"].at[way, micro, part],
            over_section,
        )

    def cross_sent(way, micro):
        for part in range(2):
            cross(way, micro, part).wait_send()

    def arrive(way, micro):
        into = hidden if way == 0 else grad

        def relay(part):
            here = into.at[half_rows(micro), columns(part)]
            return remote(
                here,
                here,
                s["relay_send"].at[way, micro, part],
                s["relay_recv"].at[way, micro, part],
                over_tensor,
            )

        for part in range(2):
            cross(way, micro, part).wait_recv()
            relay(part).start()
        for part in range(2):
            relay(part).wait()

    def leave_for(way, micro, part):
        for block in range(ROW // 2 // BLOCK):
            at = pl.multiple_of(micro * ROW + tensor * (ROW // 2) + block * BLOCK, BLOCK)
            value = stage[pl.ds(at, BLOCK), columns(part)]
            leaving[micro, part, block * BLOCK : (block + 1) * BLOCK] = value.astype(BF16)
        cross(way, micro, part).start()

    def output(way, micro):
        rows = rows_of(micro)
        into = hidden_out if way == 0 else hidden_grad
        return pltpu.make_async_copy(stage.at[rows], into.at[rows], s["output_sem"].at[way, micro])

    def weight(chunk):
        return weights[chunk].reshape(WIDTH, CHUNK)

    def times_back(left, chunks, part):
        right = [weights[chunk, 2 * part : 2 * part + 2].reshape(CHUNK, CHUNK) for chunk in chunks]
        return dot(left, jnp.concatenate(right, axis=1), NT)

    def units(micro, *slots):
        found = [ff[slot, k, pl.ds(2 * micro, 2)].reshape(ROW, CHUNK) for slot in slots for k in range(3)]
        return jnp.concatenate(found, axis=1)

    def once(micro, chunks):
        @pl.when(micro == 0)
        def _():
            for chunk in chunks:
                load(chunk).wait()

    def rotated(value, cos, sin):
        return value * cos + pltpu.roll(value, HEAD // 2, 1) * sin

    def unrotated(value, cos, sin):
        return value * cos - pltpu.roll(value, HEAD // 2, 1) * sin

    def forward_one(micro):
        rows = rows_of(micro)

        @pl.when(section == 0)
        def _():
            load_input(micro).wait()

        @pl.when(section == 1)
        def _():
            arrive(0, micro)

        def norm_one(at, block, _):
            value = hidden[at].astype(F32)
            scale = inverse_rms(value)
            normed[at] = (value * scale * attn_gain[...]).astype(BF16)
            scale_one[at] = jnp.broadcast_to(scale, (BLOCK, 128))

        over_rows(micro, norm_one)
        once(micro, range(QUERY, OUT))
        for chunk in range(4):
            wide[0] = dot(normed[rows], weight(QUERY + chunk))
            if chunk == 3:
                heads[rows, columns(chunk)] = wide[0].astype(BF16)
                continue
            gain = q_gain if chunk < 2 else k_gain
            for k in range(4):
                value = wide[0, :, columns(k, HEAD)]
                heads[rows, columns(chunk * 4 + k, HEAD)] = value.astype(BF16)
                turn = rotated(value * inverse_rms(value) * gain[...], cosine[rows], sine[rows])
                if chunk < 2:
                    query_rot[rows, columns(chunk * 4 + k, HEAD)] = turn.astype(BF16)
                else:
                    key_rot[rows, columns(k, HEAD)] = turn.astype(BF16)

        ones = jnp.ones((ROW, HEAD), BF16)

        def attend(group):
            keys = key_rot[rows, columns(group, HEAD)]
            values = heads[rows, columns(12 + group, HEAD)]
            for k in range(2):
                head = 2 * group + k
                scores = dot(query_rot[rows, columns(head, HEAD)], keys, NT)
                low = jnp.exp2(scores * (SCORE_SCALE * LOG2_E) + bias[rows]).astype(BF16)
                both = dot(low, jnp.concatenate([values, ones], axis=1))
                inverse = 1.0 / both[:, HEAD:]
                heads[rows, columns(16 + head, HEAD)] = (both[:, :HEAD] * inverse).astype(BF16)

        for index in range(4):
            attend(index)
        once(micro, (OUT, OUT + 1))

        def attended(part):
            value = times_back(heads[rows, 2048:], (OUT, OUT + 1), part)
            pair_start(0, part, value)

        for index in range(2):
            attended(index)

    def forward_two(micro):
        rows = rows_of(micro)
        pair_wait(0)

        def norm_two(at, block, _):
            value = hidden[at].astype(F32) + pair_sum(0, block)
            middle[at] = value
            scale = inverse_rms(value)
            normed_two[at] = (value * scale * mlp_gain[...]).astype(BF16)
            scale_two[at] = jnp.broadcast_to(scale, (BLOCK, 128))

        over_rows(micro, norm_two)
        once(micro, range(QUERY))

        def hidden_units(chunk):
            wide[0] = dot(normed_two[rows], weight(GATE + chunk))
            wide[1] = dot(normed_two[rows], weight(UP + chunk))

            def silu(at, block, place_in):
                gate, up = wide[0, block], wide[1, block]
                ff[1, chunk, *place_in] = gate.astype(BF16)
                ff[2, chunk, *place_in] = up.astype(BF16)
                ff[0, chunk, *place_in] = (gate * jax.nn.sigmoid(gate) * up).astype(BF16)

            over_rows(micro, silu)

        for index in range(3):
            hidden_units(index)

        def moved(part):
            value = times_back(units(micro, 0), range(DOWN, GATE), part)
            pair_start(1, part, value)

        for index in range(2):
            moved(index)

    def forward_three(micro):
        for part in range(2):
            pair(1, part).wait()

            def result(at, block, _, part=part):
                here = columns(part)
                stage[at, here] = middle[at, here] + pair_part(1, part, block)

            over_rows(micro, result)

            @pl.when(section == 0)
            def _(part=part):
                leave_for(0, micro, part)

        output(0, micro).start()

    def norm_back(total, value, scale, gain):
        inner = total * gain
        return scale * inner - value * (scale * scale * scale) * jnp.mean(
            inner * value, axis=-1, keepdims=True
        )

    def add_gain(row, value):
        gains[0, row : row + 1] = gains[0, row : row + 1] + value

    def add_gains(row, part, value):
        for k in range(4):
            at = slice(row + part * 4 + k, row + part * 4 + k + 1)
            gains[0, at] = gains[0, at] + value[:, k * 128 : (k + 1) * 128]

    def turn(slot, value):
        for k in range(4):
            turned[slot, k] = value[:, columns(k, 256)].T.reshape(2, 4, 32, CHUNK)

    def weight_grad(chunk, slot, right):
        for part in range(4):
            value = dot(turned[slot, part].reshape(256, CHUNK), right)
            weights[chunk, part] = value.astype(BF16).reshape(2, 4, 32, CHUNK)

    rings = []
    for first, (order, count) in enumerate(zip(ORDERS, COUNTS)):
        own, scratch = scratch[:9], scratch[9:]

        def finish(i, half, total, first=first):
            grads_out[2 * i + first] = total

        def chunk_at(i, first=first):
            return (2 * i + first,)

        rings.append((count, LAGS, ring_stages(order, weights, chunk_at, own, place, finish)))

    def kept(chunk):
        return (section == 1) | (lax.rem(chunk, 3) > 0) | (chunk >= MLP_CHUNKS)

    def ring_start(chunk):
        for first in (0, 1):

            @pl.when((lax.rem(chunk, 2) == first) & kept(chunk))
            def _(first=first):
                rings[first][2][0]((chunk - first) // 2)

        @pl.when(jnp.logical_not(kept(chunk)))
        def _():
            leave(chunk // 3, 0).start()
            leave(chunk // 3, 1).start()

    def leave(i, slant):
        side = place.at["x"]
        return remote(
            weights.at[3 * i, :, 1 - side if slant else side],
            ff.at[i, side],
            s["left_send"].at[i, slant],
            s["left_recv"].at[i, side],
            aslant if slant else over_section,
        )

    def left_arrival(i, side):
        return remote(
            weights.at[3 * i, :, side],
            ff.at[i, side],
            s["left_send"].at[i, side],
            s["left_recv"].at[i, side],
            over_section,
        )

    def give_back(i):
        return remote(
            s["left_sum"].at[i],
            s["left_done"].at[i],
            s["done_send"].at[i],
            s["done_recv"].at[i],
            over_section,
        )

    def left_start(i):
        for side in (0, 1):
            left_arrival(i, side).wait_recv()
        ff[i, 2] = (ff[i, 0].astype(F32) + ff[i, 1].astype(F32)).astype(BF16)

    def left_finish(i, half, total):
        s["left_sum"][i, half * 16 : half * 16 + 16] = total
        if half:
            give_back(i).start()

    own, scratch = scratch[:6], scratch[6:]
    left_stages = [left_start] + ring_stages(
        LEFT_ORDER, ff, lambda i: (i, 2), own, place, left_finish, skipped=("x",)
    )

    def mlp_grad(chunk, carry):
        weight_grad(chunk, jnp.minimum(chunk // 3, 1), ff[chunk // 3, lax.rem(chunk, 3)].reshape(2 * ROW, CHUNK))
        ring_start(chunk)
        return carry

    def backward_one(micro):
        rows = rows_of(micro)

        @pl.when(section == 0)
        def _():
            arrive(1, micro)
            cross_sent(0, micro)

        def hidden_back(chunk):
            wide[0] = dot(grad[rows], weight(DOWN + chunk))

            def silu_back(at, block, place_in):
                act_grad = wide[0, block]
                gate, up = ff[1, chunk, *place_in].astype(F32), ff[2, chunk, *place_in].astype(F32)
                sigma = jax.nn.sigmoid(gate)
                passed = act_grad * sigma
                ff[1, chunk, *place_in] = (passed * up * (1.0 + gate * (1.0 - sigma))).astype(BF16)
                ff[2, chunk, *place_in] = (passed * gate).astype(BF16)

            over_rows(micro, silu_back)

        for index in range(3):
            hidden_back(index)

        def normed_two_back(part):
            value = times_back(units(micro, 1, 2), range(GATE, QUERY), part)
            pair_start(2, part, value)
            scaled = middle[rows, columns(part)] * scale_two[rows, :1]
            add_gains(8, part, jnp.sum(value * scaled, axis=0, keepdims=True))

        @pl.when(micro == 1)
        def _():
            @pl.when(section == 0)
            def _():
                turn(0, grad)
                pl.semaphore_wait(s["left_free"], 2)

            lax.fori_loop(DOWN + 1, GATE, mlp_grad, 0)
            mlp_grad(DOWN, 0)

        for index in range(2):
            normed_two_back(index)

        @pl.when(micro == 1)
        def _():
            @pl.when(section == 1)
            def _():
                turn(1, normed_two)

            lax.fori_loop(GATE, jnp.where(section == 0, QUERY, SOON), mlp_grad, 0)

    def backward_two(micro):
        rows = rows_of(micro)
        pair_wait(2)
        output(0, micro).wait()

        def middle_back(at, block, _):
            value = grad[at].astype(F32) + norm_back(
                pair_sum(2, block), middle[at], scale_two[at, :1], mlp_gain[...]
            )
            stage[at] = value
            attended_grad[at] = value.astype(BF16)

        over_rows(micro, middle_back)

        for k in range(2):
            mixed_grad[:, columns(k)] = dot(attended_grad[rows], weight(OUT + k)).astype(BF16)

        def attend_back(group):
            cos, sin = cosine[rows], sine[rows]
            cos_turned, sin_turned = s["cosine_turned"][micro], s["sine_turned"][micro]
            gain_turned = jnp.concatenate([s["q_gain_turned"][...]] * 2, axis=1)
            keys = key_rot[rows, columns(group, HEAD)]
            keys_turned = keys.T
            values = heads[rows, columns(12 + group, HEAD)]
            key_rot_grad = jnp.zeros((ROW, HEAD), F32)
            value_grad = jnp.zeros((ROW, HEAD), F32)
            for k in range(2):
                head = 2 * group + k
                here = columns(head, HEAD)
                queries = query_rot[rows, here]
                out_grad = mixed_grad[:, here]
                scores = dot(keys, queries, NT)
                raw = jnp.exp2(scores * (SCORE_SCALE * LOG2_E) + s["bias_turned"][rows])
                chance = raw * (1.0 / jnp.sum(raw, axis=0, keepdims=True))
                weighted = chance * dot(values, out_grad, NT)
                across = jnp.sum(weighted, axis=0, keepdims=True)
                score_grad = (weighted - chance * across).astype(BF16)
                value_grad = value_grad + dot(chance.astype(BF16), out_grad)
                key_rot_grad = key_rot_grad + dot(score_grad, queries)
                passed = dot(keys_turned, score_grad) * SCORE_SCALE
                swapped = jnp.concatenate([passed[HEAD // 2 :], passed[: HEAD // 2]], axis=0)
                turn_grad = passed * cos_turned - swapped * sin_turned
                query = heads[rows, here].T.astype(F32)
                scale = lax.rsqrt(jnp.mean(query * query, axis=0, keepdims=True) + EPSILON)
                scaled = query * scale
                s["q_gain_sum"][...] = s["q_gain_sum"][...] + turn_grad * scaled
                inner = turn_grad * gain_turned
                query_grad = scale * (inner - scaled * jnp.mean(inner * scaled, axis=0, keepdims=True))
                heads[rows, here] = query_grad.astype(BF16).T
            turn_grad = unrotated(key_rot_grad * SCORE_SCALE, cos, sin)
            here = columns(8 + group, HEAD)
            key = heads[rows, here].astype(F32)
            scale = inverse_rms(key)
            add_gain(17, jnp.sum(turn_grad * key * scale, axis=0, keepdims=True))
            heads[rows, here] = norm_back(turn_grad, key, scale, k_gain[...]).astype(BF16)
            heads[rows, columns(12 + group, HEAD)] = value_grad.astype(BF16)

        for index in range(4):
            attend_back(index)

        def normed_back(part):
            value = times_back(heads[rows, :2048], range(QUERY, OUT), part)
            pair_start(3, part, value)
            scaled = hidden[rows, columns(part)].astype(F32) * scale_one[rows, :1]
            add_gains(0, part, jnp.sum(value * scaled, axis=0, keepdims=True))

        for index in range(2):
            normed_back(index)
    def backward_three(micro):
        pair_wait(3)

        def hidden_back_end(at, block, _):
            stage[at] = stage[at] + norm_back(
                pair_sum(3, block), hidden[at].astype(F32), scale_one[at, :1], attn_gain[...]
            )

        over_rows(micro, hidden_back_end)
        output(1, micro).start()

        @pl.when(section == 1)
        def _():
            leave_for(1, micro, 0)
            leave_for(1, micro, 1)

        @pl.when((section == 1) & (micro == 1))
        def _():
            lax.fori_loop(SOON, QUERY, mlp_grad, 0)
            for device in (over_section, aslant):
                pl.semaphore_signal(s["left_free"], inc=1, device_id=device, device_id_type=MESH)

    @pl.when(section == 1)
    def _():
        for micro in range(2):
            load_cotangent(micro).wait()
        turn(0, grad)

    def step(turn_of, carry):
        back = turn_of - 2 + section

        @pl.when((turn_of == 2) & (section == 0))
        def _():
            turn(1, normed_two)

        for ahead, behind in (
            (forward_one, backward_one),
            (forward_two, backward_two),
            (forward_three, backward_three),
        ):

            @pl.when((back >= 0) & (back < 2))
            def _(behind=behind):
                behind(back)

            @pl.when(turn_of < 2)
            def _(ahead=ahead):
                ahead(turn_of)

        return carry

    lax.fori_loop(0, 4, step, 0)

    add_gain(16, jnp.sum(s["q_gain_sum"][...].T, axis=0, keepdims=True))
    turn(0, normed)
    turn(1, attended_grad)

    def attention_grad(chunk, carry):
        weight_grad(MLP_CHUNKS + chunk, chunk // 4, heads[:, columns(chunk)])
        ring_start(MLP_CHUNKS + chunk)
        return carry

    lax.fori_loop(0, CHUNKS - MLP_CHUNKS, attention_grad, 0)

    def always(i):
        return True

    groups = [
        (count, (None, *lags[1:]), stages, lambda i, first=first: kept(2 * i + first))
        for first, (count, lags, stages) in enumerate(rings)
    ]
    groups.append(
        (LEFT, [LEFT_FROM + lag for lag in LEFT_LAGS], left_stages, lambda i: section == 1)
    )
    groups.append((1, (0, 2, 2, 4, 4, 6, 6, 8), gain_stages(gains_out, scratch, place), always))

    def advance(now, carry):
        for step in range(8):
            for count, lags, stages, runs in groups:
                if step >= len(stages) or lags[step] is None:
                    continue
                i = now - lags[step]

                @pl.when((i >= 0) & (i < count) & runs(i))
                def _(i=i, run=stages[step]):
                    run(i)

        return carry

    lax.fori_loop(0, max(count + lags[-1] for count, lags, _, _ in groups), advance, 0)

    @pl.when(section == 0)
    def _():
        for i in range(LEFT):
            leave(i, 0).wait_send()
            leave(i, 1).wait_send()
            give_back(i).wait_recv()
            grads_out[3 * i] = s["left_done"][i]

    @pl.when(section == 1)
    def _():
        for i in range(LEFT):
            give_back(i).wait_send()

    for micro in range(2):
        output(1, micro).wait()

        @pl.when(section == 1)
        def _(micro=micro):
            cross_sent(1, micro)


def rope_table():
    half = HEAD // 2
    rates = THETA ** (-2.0 * np.arange(half) / HEAD)
    angle = np.arange(HEAD)[:, None] * np.concatenate([rates, rates])[None]
    sign = np.where(np.arange(HEAD) < half, -1.0, 1.0)
    parts = []
    for value in (np.cos(angle), np.sin(angle) * sign):
        high = value.astype(jnp.bfloat16)
        parts += [high, (value - high.astype(np.float64)).astype(jnp.bfloat16)]
    return jnp.asarray(np.concatenate(parts, axis=1))


def by_place(weight):
    return weight.reshape(4, 2, 4, 32, weight.shape[-1])


def shards(
    block_input,
    doc_lengths,
    out_cotangent,
    attn_gain,
    q_gain,
    k_gain,
    mlp_gain,
    q_weight,
    key_matrix,
    value_matrix,
    o_weight,
    gate_weight,
    up_weight,
    down_weight,
):
    vmem = pl.BlockSpec(memory_space=pltpu.VMEM)
    smem = pl.BlockSpec(memory_space=pltpu.SMEM)
    anywhere = pl.BlockSpec(memory_space=pl.ANY)
    scratch = list(SCRATCH.values())
    for order, count in zip(ORDERS, COUNTS):
        scratch += ring_scratch(order, count)
    scratch += ring_scratch(LEFT_ORDER, LEFT, 1)
    scratch += gain_scratch()
    full = jax.ShapeDtypeStruct(block_input.shape, F32)
    outputs, grads_in, grads, gains = pl.pallas_call(
        kernel,
        out_shape=(
            full,
            full,
            jax.ShapeDtypeStruct((CHUNKS, 32, CHUNK), F32),
            jax.ShapeDtypeStruct((1, GAIN_ROWS * 128), F32),
        ),
        in_specs=[smem, anywhere, anywhere] + [vmem] * 4 + [anywhere] * 7 + [vmem],
        out_specs=[anywhere, anywhere, vmem, vmem],
        scratch_shapes=scratch,
        compiler_params=pltpu.CompilerParams(
            collective_id=0, has_side_effects=True, vmem_limit_bytes=64 * 2**20 - 2**16
        ),
    )(
        doc_lengths,
        block_input,
        out_cotangent,
        attn_gain,
        q_gain,
        k_gain,
        mlp_gain,
        by_place(q_weight),
        by_place(key_matrix),
        by_place(value_matrix),
        by_place(o_weight),
        by_place(gate_weight),
        by_place(up_weight),
        by_place(down_weight),
        rope_table(),
    )

    return spread(outputs, grads_in, grads, gains)


MATRICES = ((QUERY, 2), (KEY, 1), (VALUE, 1), (OUT, 2), (GATE, 3), (UP, 3), (DOWN, 3))
GAIN_PARTS = ((0, 1024), (2048, 128), (2176, 128), (1024, 1024))


def spread_kernel(outputs, grads_in, grads, gains, *refs):
    results, (tokens, matrices, row, in_sem, out_sem) = refs[:-5], refs[-5:]
    loads, stores = [], []

    def through(src, held, pairs):
        load = pltpu.make_async_copy(src, held, in_sem.at[len(loads)])
        load.start()
        loads.append((load, pairs))

    through(grads, matrices, [])
    for k in range(8):
        rows = pl.ds(k % 4 * 128, 128)
        src, into = ((outputs, results[0]), (grads_in, results[1]))[k // 4]
        through(src.at[rows], tokens.at[k], [(tokens.at[k], into.at[0, rows])])
    through(gains, row, [])
    for (first, count), into in zip(MATRICES, results[6:]):
        for k in range(count):
            pair = (matrices.at[first + k], into.at[0, :, k * CHUNK : (k + 1) * CHUNK])
            loads[0][1].append(pair)
    for (first, size), into in zip(GAIN_PARTS, results[2:6]):
        loads[-1][1].append((row.at[:, first : first + size], into))
    for load, pairs in loads:
        load.wait()
        for src, dst in pairs:
            store = pltpu.make_async_copy(src, dst, out_sem.at[len(stores)])
            store.start()
            stores.append(store)
    for store in stores:
        store.wait()


def spread(outputs, grads_in, grads, gains):
    shapes = [(1, *outputs.shape)] * 2 + [(1, size) for _, size in GAIN_PARTS]
    shapes += [(1, 32, count * CHUNK) for _, count in MATRICES]
    anywhere = pl.BlockSpec(memory_space=pl.ANY)
    return pl.pallas_call(
        spread_kernel,
        out_shape=[jax.ShapeDtypeStruct(shape, F32) for shape in shapes],
        in_specs=[anywhere] * 4,
        out_specs=[anywhere] * len(shapes),
        scratch_shapes=[
            pltpu.VMEM((8, 128, outputs.shape[1]), F32),
            pltpu.VMEM(grads.shape, F32),
            pltpu.VMEM(gains.shape, F32),
            pltpu.SemaphoreType.DMA((10,)),
            pltpu.SemaphoreType.DMA((27,)),
        ],
        compiler_params=pltpu.CompilerParams(vmem_limit_bytes=16 * 2**20),
    )(outputs, grads_in, grads, gains)


def solution(mesh):
    weight = P("section", None, "tensor")
    gain = P("section", None)
    tokens = P("section", "dp", None)
    grad = P("section", "dp", "tensor")
    return jax.shard_map(
        shards,
        mesh=mesh,
        in_specs=(P("dp", None),) * 3 + (gain,) * 4 + (weight,) * 7,
        out_specs=(tokens,) * 2 + (gain,) * 4 + (grad,) * 7,
        check_vma=False,
    )
```

```python
import functools

import jax
import jax.numpy as jnp
import numpy as np
from jax import lax
from jax.experimental import pallas as pl
from jax.experimental.pallas import tpu as pltpu
from jax.sharding import PartitionSpec as P

EPSILON = 1e-06
THETA = 1000000.0
HEAD = 128
ROW = 256
WIDTH = 1024
BLOCK = 32
SCORE_SCALE = HEAD ** (-0.5)
LOG2_E = 1.4426950408889634
MESH = pl.DeviceIdType.MESH
BF16, F32 = jnp.bfloat16, jnp.float32
NT = (((1,), (1,)), ((), ()))
TN = (((0,), (0,)), ((), ()))

CHUNK = 512
DOWN, GATE, UP, QUERY, KEY, VALUE, OUT = 0, 3, 6, 9, 11, 12, 13
CHUNKS = 15
MLP_CHUNKS = 9
SOON = 7
ORDERS = (("z", "y", "x"), ("y", "z", "x"))
COUNTS = (8, 7)
LAGS = (0, 0, 2, 2, 4, 6, 6, 8)
LEFT = 3
LEFT_ORDER = ("x", "y", "z")
LEFT_LAGS = (0, 0, 1, 2, 2, 3, 4)
LEFT_FROM = 6
GAIN_ROWS = 24


def remote(src, dst, send_sem, recv_sem, device):
    return pltpu.make_async_remote_copy(
        src_ref=src,
        dst_ref=dst,
        send_sem=send_sem,
        recv_sem=recv_sem,
        device_id=device,
        device_id_type=MESH,
    )


def dot(left, right, form=None):
    if form is None:
        return jnp.dot(left, right, preferred_element_type=F32)
    return lax.dot_general(left, right, form, preferred_element_type=F32)


class Place:
    def __init__(self):
        dp = lax.axis_index("dp")
        self.at = {"z": dp // 8, "x": dp // 4 % 2, "y": dp % 4}

    def device(self, axis, index):
        at = {**self.at, axis: index}
        return {"dp": at["z"] * 8 + at["x"] * 4 + at["y"]}


def ring_phases(order):
    found, done = [], []
    for axis in order:
        left = [name for name in ("z", "x", "y") if name not in done and name != axis]
        halved = None if axis == "x" else "x" if "x" in left else left[0] if left else "row"
        shape = []
        for name in left:
            size = 2 if name == "x" else 4
            shape.append(size // 2 if name == halved else size)
        rows = 16 if halved == "row" else 32
        found.append((axis, tuple(done), halved, (*shape, rows, CHUNK)))
        done.append(axis)
    return found


def ring_scratch(order, count, skipped=0):
    found = []
    for _, _, halved, shape in ring_phases(order)[skipped:]:
        parts = 6 if halved else 1
        found.append(pltpu.VMEM((count, parts, *shape), BF16))
        found.append(pltpu.SemaphoreType.DMA((count, parts)))
        found.append(pltpu.SemaphoreType.DMA((count, parts)))
    return found


def ring_stages(order, grads, at_first, scratch, place, finish, skipped=()):
    stages = []
    phases = ring_phases(order)[len(skipped) :]
    for step, (axis, done, halved, _) in enumerate(phases):
        arrived, send_sem, recv_sem = scratch[3 * step : 3 * step + 3]
        mine = place.at[axis]

        def where(i, index, half, axis=axis, done=done, halved=halved):
            found = list(at_first(i))
            for name in ("z", "x", "y"):
                if name in skipped:
                    continue
                if name in done:
                    found.append(place.at[name])
                elif name == axis:
                    found.append(index)
                elif name == halved:
                    size = 1 if name == "x" else 2
                    found.append(pl.ds(half * size, size))
                else:
                    found.append(slice(None))
            if halved == "row":
                found.append(pl.ds(half * 16, 16))
            return tuple(found)

        def put(i, half, total, step=step, mine=mine, where=where):
            if step == len(phases) - 1:
                finish(i, half, total)
            else:
                grads[where(i, mine, half)] = total.astype(BF16)

        if halved is None:

            def swap(
                i, where=where, arrived=arrived, send_sem=send_sem, recv_sem=recv_sem, mine=mine, axis=axis
            ):
                return remote(
                    grads.at[where(i, 1 - mine, 0)],
                    arrived.at[i, 0],
                    send_sem.at[i, 0],
                    recv_sem.at[i, 0],
                    place.device(axis, 1 - mine),
                )

            def start(i, swap=swap):
                swap(i).start()

            def end(i, swap=swap, arrived=arrived, where=where, mine=mine, put=put):
                swap(i).wait()
                put(i, 0, grads[where(i, mine, 0)].astype(F32) + arrived[i, 0].astype(F32))

            stages += [start, end]
            continue

        right, left = lax.rem(mine + 1, 4), lax.rem(mine + 3, 4)
        across = lax.rem(mine + 2, 4)
        sends = (
            (across, 0, right),
            (across, 1, left),
            (right, 1, right),
            (left, 0, left),
            (right, 0, right),
            (left, 1, left),
        )

        def send(
            i, k, where=where, arrived=arrived, send_sem=send_sem, recv_sem=recv_sem, axis=axis, sends=sends
        ):
            index, half, to = sends[k]
            return remote(
                grads.at[where(i, index, half)],
                arrived.at[i, k],
                send_sem.at[i, k],
                recv_sem.at[i, k],
                place.device(axis, to),
            )

        def start(i, send=send):
            for k in range(4):
                send(i, k).start()

        def pass_on(i, send=send, arrived=arrived, where=where, sends=sends):
            for k in (0, 1):
                send(i, k).wait_recv()
                index, half, _ = sends[4 + k]
                at = where(i, index, half)
                grads[at] = (grads[at].astype(F32) + arrived[i, k].astype(F32)).astype(BF16)
                send(i, 4 + k).start()

        def end(i, send=send, arrived=arrived, where=where, mine=mine, put=put):
            for k in range(2, 6):
                send(i, k).wait_recv()
            for k in range(6):
                send(i, k).wait_send()
            for half in (0, 1):
                own = grads[where(i, mine, half)].astype(F32)
                near = arrived[i, 4 - 2 * half].astype(F32)
                far = arrived[i, 3 + 2 * half].astype(F32)
                put(i, half, own + near + far)

        stages += [start, pass_on, end]
    return stages


def gain_scratch():
    found = [pltpu.VMEM((4, GAIN_ROWS, 128), F32)]
    for size in (4, 4, 2, 2):
        found.append(pltpu.SemaphoreType.DMA((size,)))
        found.append(pltpu.SemaphoreType.DMA((size,)))
        found.append(pltpu.VMEM((size, GAIN_ROWS, 128), F32))
    return found


def gain_axes(place):
    return (
        (4, place.at["y"], lambda k: place.device("y", k)),
        (4, place.at["z"], lambda k: place.device("z", k)),
        (2, place.at["x"], lambda k: place.device("x", k)),
        (2, lax.axis_index("tensor"), lambda k: {"tensor": k}),
    )


def gain_stages(total_ref, scratch, place):
    held = scratch[0]
    stages = []
    for step, (size, mine, device) in enumerate(gain_axes(place)):
        send_sem, recv_sem, slots = scratch[1 + 3 * step : 4 + 3 * step]
        src = held.at[step]
        dst = total_ref if step == 3 else held.at[step + 1]

        def send(k, src=src, slots=slots, send_sem=send_sem, recv_sem=recv_sem, size=size, mine=mine, device=device):
            to = lax.rem(mine + k, size)
            return remote(src, slots.at[mine], send_sem.at[k], recv_sem.at[mine], device(to))

        def arrival(k, src=src, slots=slots, send_sem=send_sem, recv_sem=recv_sem, size=size, mine=mine, device=device):
            frm = lax.rem(mine + k, size)
            return remote(src, slots.at[frm], send_sem.at[k], recv_sem.at[frm], device(frm))

        def start(i, send=send, src=src, slots=slots, size=size, mine=mine):
            slots[mine] = src[...]
            for k in range(1, size):
                send(k).start()

        def end(i, send=send, arrival=arrival, slots=slots, size=size, dst=dst):
            for k in range(1, size):
                arrival(k).wait_recv()
                send(k).wait_send()
            total = slots[0]
            for k in range(1, size):
                total = total + slots[k]
            if dst is total_ref:
                for k in range(GAIN_ROWS):
                    dst[:, k * 128 : (k + 1) * 128] = total[k : k + 1]
            else:
                dst[...] = total

        stages += [start, end]
    return stages


SCRATCH = dict(
    weights=pltpu.VMEM((CHUNKS, 4, 2, 4, 32, CHUNK), BF16),
    hidden=pltpu.VMEM((2 * ROW, WIDTH), BF16),
    normed=pltpu.VMEM((2 * ROW, WIDTH), BF16),
    heads=pltpu.VMEM((2 * ROW, 3072), BF16),
    query_rot=pltpu.VMEM((2 * ROW, 1024), BF16),
    key_rot=pltpu.VMEM((2 * ROW, 512), BF16),
    middle=pltpu.VMEM((2 * ROW, WIDTH), F32),
    normed_two=pltpu.VMEM((2 * ROW, WIDTH), BF16),
    ff=pltpu.VMEM((3, 3, 4, 4, 32, CHUNK), BF16),
    grad=pltpu.VMEM((2 * ROW, WIDTH), BF16),
    attended_grad=pltpu.VMEM((2 * ROW, WIDTH), BF16),
    mixed_grad=pltpu.VMEM((ROW, 1024), BF16),
    turned=pltpu.VMEM((2, 4, 2, 4, 32, CHUNK), BF16),
    mine=pltpu.VMEM((4, 2, ROW, CHUNK), BF16),
    theirs=pltpu.VMEM((4, 2, ROW, CHUNK), BF16),
    leaving=pltpu.VMEM((2, 2, ROW // 2, CHUNK), BF16),
    stage=pltpu.VMEM((2 * ROW, WIDTH), F32),
    cosine=pltpu.VMEM((2 * ROW, HEAD), F32),
    sine=pltpu.VMEM((2 * ROW, HEAD), F32),
    bias=pltpu.VMEM((2 * ROW, ROW), F32),
    cosine_turned=pltpu.VMEM((2, HEAD, ROW), F32),
    sine_turned=pltpu.VMEM((2, HEAD, ROW), F32),
    bias_turned=pltpu.VMEM((2 * ROW, ROW), F32),
    q_gain_turned=pltpu.VMEM((HEAD, HEAD), F32),
    q_gain_sum=pltpu.VMEM((HEAD, ROW), F32),
    scale_one=pltpu.VMEM((2 * ROW, 128), F32),
    scale_two=pltpu.VMEM((2 * ROW, 128), F32),
    wide=pltpu.VMEM((2, ROW, CHUNK), F32),
    weight_sem=pltpu.SemaphoreType.DMA((CHUNKS,)),
    input_sem=pltpu.SemaphoreType.DMA((2,)),
    output_sem=pltpu.SemaphoreType.DMA((2, 2)),
    mine_sem=pltpu.SemaphoreType.DMA((4, 2)),
    theirs_sem=pltpu.SemaphoreType.DMA((4, 2)),
    cross_send=pltpu.SemaphoreType.DMA((2, 2, 2)),
    cross_recv=pltpu.SemaphoreType.DMA((2, 2, 2)),
    relay_send=pltpu.SemaphoreType.DMA((2, 2, 2)),
    relay_recv=pltpu.SemaphoreType.DMA((2, 2, 2)),
    left_send=pltpu.SemaphoreType.DMA((LEFT, 2)),
    left_recv=pltpu.SemaphoreType.DMA((LEFT, 2)),
    left_sum=pltpu.VMEM((LEFT, 32, CHUNK), F32),
    left_done=pltpu.VMEM((LEFT, 32, CHUNK), F32),
    done_send=pltpu.SemaphoreType.DMA((LEFT,)),
    done_recv=pltpu.SemaphoreType.DMA((LEFT,)),
    left_free=pltpu.SemaphoreType.REGULAR,
)


def rows_of(micro):
    return pl.ds(pl.multiple_of(micro * ROW, ROW), ROW)


def over_rows(micro, body):
    for block in range(ROW // BLOCK):
        body(
            pl.ds(pl.multiple_of(micro * ROW + block * BLOCK, BLOCK), BLOCK),
            pl.ds(block * BLOCK, BLOCK),
            (2 * micro + block // 4, block % 4),
        )


def columns(index, size=CHUNK):
    if isinstance(index, int):
        return pl.ds(index * size, size)
    return pl.ds(pl.multiple_of(index * size, size), size)


def inverse_rms(value):
    return lax.rsqrt(jnp.mean(value * value, axis=-1, keepdims=True) + EPSILON)


def kernel(
    lengths,
    block_input,
    cotangent,
    attn_gain,
    q_gain,
    k_gain,
    mlp_gain,
    q_weight,
    key_matrix,
    value_matrix,
    o_weight,
    gate_weight,
    up_weight,
    down_weight,
    table,
    hidden_out,
    hidden_grad,
    grads_out,
    gains_out,
    *scratch,
):
    s = dict(zip(SCRATCH, scratch))
    scratch = scratch[len(SCRATCH) :]
    weights, hidden, normed, heads = s["weights"], s["hidden"], s["normed"], s["heads"]
    query_rot, key_rot = s["query_rot"], s["key_rot"]
    middle, normed_two, ff, grad = s["middle"], s["normed_two"], s["ff"], s["grad"]
    attended_grad, mixed_grad, turned = s["attended_grad"], s["mixed_grad"], s["turned"]
    mine, theirs, leaving, stage = s["mine"], s["theirs"], s["leaving"], s["stage"]
    cosine, sine, bias = s["cosine"], s["sine"], s["bias"]
    scale_one, scale_two, wide = s["scale_one"], s["scale_two"], s["wide"]
    place = Place()
    section, tensor = lax.axis_index("section"), lax.axis_index("tensor")
    over_tensor, over_section = {"tensor": 1 - tensor}, {"section": 1 - section}
    aslant = {"section": 1 - section, **place.device("x", 1 - place.at["x"])}

    barrier = pltpu.get_barrier_semaphore()
    for size, own, device in gain_axes(place):
        for k in range(1, size):
            pl.semaphore_signal(
                barrier, inc=1, device_id=device(lax.rem(own + k, size)), device_id_type=MESH
            )
    for device in (over_section, aslant):
        pl.semaphore_signal(barrier, inc=1, device_id=device, device_id_type=MESH)

    sources = (
        [(q_weight, 0), (q_weight, 1), (key_matrix, 0), (value_matrix, 0), (o_weight, 0), (o_weight, 1)],
        [(ref, k) for ref in (down_weight, gate_weight, up_weight) for k in range(3)],
    )

    def load(chunk):
        ref, part = sources[1][chunk] if chunk < MLP_CHUNKS else sources[0][chunk - MLP_CHUNKS]
        return pltpu.make_async_copy(
            ref.at[:, :, :, :, columns(part)], weights.at[chunk], s["weight_sem"].at[chunk]
        )

    def load_input(micro):
        rows = rows_of(micro)
        return pltpu.make_async_copy(block_input.at[rows], hidden.at[rows], s["input_sem"].at[micro])

    def load_cotangent(micro):
        rows = rows_of(micro)
        return pltpu.make_async_copy(cotangent.at[rows], grad.at[rows], s["input_sem"].at[micro])

    @pl.when(section == 0)
    def _():
        load_input(0).start()
        load_input(1).start()

    for chunk in (9, 10, 11, 12, 13, 14, 3, 6, 4, 7, 5, 8, 0, 1, 2):
        load(chunk).start()

    @pl.when(section == 1)
    def _():
        load_cotangent(0).start()
        load_cotangent(1).start()

    gains = scratch[-13]
    gains[0] = jnp.zeros((GAIN_ROWS, 128), F32)

    def tables(micro, carry):
        rows = rows_of(micro)
        ends = [lengths[micro, 0]]
        for k in (1, 2):
            ends.append(ends[-1] + lengths[micro, k])

        def begins(shape, dim=0):
            at = lax.broadcasted_iota(jnp.int32, shape, dim)
            found = jnp.zeros(shape, jnp.int32)
            for end in ends:
                found = jnp.where(at >= end, end, found)
            return at, found

        at, begin = begins((ROW, HEAD))
        chosen = (at - begin) == lax.broadcasted_iota(jnp.int32, (ROW, HEAD), 1)
        both = dot(chosen.astype(F32).astype(BF16), table[...])
        cosine[rows] = both[:, :128] + both[:, 128:256]
        sine[rows] = both[:, 256:384] + both[:, 384:]
        s["cosine_turned"][micro] = cosine[rows].T
        s["sine_turned"][micro] = sine[rows].T
        for dim, into in ((0, bias), (1, s["bias_turned"])):
            at, begin = begins((ROW, ROW), dim)
            key = lax.broadcasted_iota(jnp.int32, (ROW, ROW), 1 - dim)
            into[rows] = jnp.where((key >= begin) & (key <= at), 0.0, -1e9)
        return carry

    lax.fori_loop(0, 2, tables, 0)
    s["q_gain_turned"][...] = jnp.broadcast_to(q_gain[...], (HEAD, HEAD)).T
    s["q_gain_sum"][...] = jnp.zeros((HEAD, ROW), F32)

    pl.semaphore_wait(barrier, 10)

    def pair(slot, part):
        return remote(
            mine.at[slot, part],
            theirs.at[slot, part],
            s["mine_sem"].at[slot, part],
            s["theirs_sem"].at[slot, part],
            over_tensor,
        )

    def pair_start(slot, part, value):
        mine[slot, part] = value.astype(BF16)
        pair(slot, part).start()

    def pair_wait(slot):
        for part in range(2):
            pair(slot, part).wait()

    def pair_part(slot, part, block):
        return mine[slot, part, block].astype(F32) + theirs[slot, part, block].astype(F32)

    def pair_sum(slot, block):
        return jnp.concatenate(
            [
                mine[slot, part, block].astype(F32) + theirs[slot, part, block].astype(F32)
                for part in range(2)
            ],
            axis=1,
        )

    def half_rows(micro):
        return pl.ds(pl.multiple_of(micro * ROW + tensor * (ROW // 2), ROW // 2), ROW // 2)

    def cross(way, micro, part):
        into = hidden if way == 0 else grad
        return remote(
            leaving.at[micro, part],
            into.at[half_rows(micro), columns(part)],
            s["cross_send"].at[way, micro, part],
            s["cross_recv"].at[way, micro, part],
            over_section,
        )

    def cross_sent(way, micro):
        for part in range(2):
            cross(way, micro, part).wait_send()

    def arrive(way, micro):
        into = hidden if way == 0 else grad

        def relay(part):
            here = into.at[half_rows(micro), columns(part)]
            return remote(
                here,
                here,
                s["relay_send"].at[way, micro, part],
                s["relay_recv"].at[way, micro, part],
                over_tensor,
            )

        for part in range(2):
            cross(way, micro, part).wait_recv()
            relay(part).start()
        for part in range(2):
            relay(part).wait()

    def leave_for(way, micro, part):
        for block in range(ROW // 2 // BLOCK):
            at = pl.multiple_of(micro * ROW + tensor * (ROW // 2) + block * BLOCK, BLOCK)
            value = stage[pl.ds(at, BLOCK), columns(part)]
            leaving[micro, part, block * BLOCK : (block + 1) * BLOCK] = value.astype(BF16)
        cross(way, micro, part).start()

    def output(way, micro):
        rows = rows_of(micro)
        into = hidden_out if way == 0 else hidden_grad
        return pltpu.make_async_copy(stage.at[rows], into.at[rows], s["output_sem"].at[way, micro])

    def weight(chunk):
        return weights[chunk].reshape(WIDTH, CHUNK)

    def times_back(left, chunks, part):
        right = [weights[chunk, 2 * part : 2 * part + 2].reshape(CHUNK, CHUNK) for chunk in chunks]
        return dot(left, jnp.concatenate(right, axis=1), NT)

    def units(micro, *slots):
        found = [ff[slot, k, pl.ds(2 * micro, 2)].reshape(ROW, CHUNK) for slot in slots for k in range(3)]
        return jnp.concatenate(found, axis=1)

    def once(micro, chunks):
        @pl.when(micro == 0)
        def _():
            for chunk in chunks:
                load(chunk).wait()

    def rotated(value, cos, sin):
        return value * cos + pltpu.roll(value, HEAD // 2, 1) * sin

    def unrotated(value, cos, sin):
        return value * cos - pltpu.roll(value, HEAD // 2, 1) * sin

    def forward_one(micro):
        rows = rows_of(micro)

        @pl.when(section == 0)
        def _():
            load_input(micro).wait()

        @pl.when(section == 1)
        def _():
            arrive(0, micro)

        def norm_one(at, block, _):
            value = hidden[at].astype(F32)
            scale = inverse_rms(value)
            normed[at] = (value * scale * attn_gain[...]).astype(BF16)
            scale_one[at] = jnp.broadcast_to(scale, (BLOCK, 128))

        over_rows(micro, norm_one)
        once(micro, range(QUERY, OUT))
        for chunk in range(4):
            wide[0] = dot(normed[rows], weight(QUERY + chunk))
            if chunk == 3:
                heads[rows, columns(chunk)] = wide[0].astype(BF16)
                continue
            gain = q_gain if chunk < 2 else k_gain
            for k in range(4):
                value = wide[0, :, columns(k, HEAD)]
                heads[rows, columns(chunk * 4 + k, HEAD)] = value.astype(BF16)
                turn = rotated(value * inverse_rms(value) * gain[...], cosine[rows], sine[rows])
                if chunk < 2:
                    query_rot[rows, columns(chunk * 4 + k, HEAD)] = turn.astype(BF16)
                else:
                    key_rot[rows, columns(k, HEAD)] = turn.astype(BF16)

        ones = jnp.ones((ROW, HEAD), BF16)

        def attend(group):
            keys = key_rot[rows, columns(group, HEAD)]
            values = heads[rows, columns(12 + group, HEAD)]
            for k in range(2):
                head = 2 * group + k
                scores = dot(query_rot[rows, columns(head, HEAD)], keys, NT)
                low = jnp.exp2(scores * (SCORE_SCALE * LOG2_E) + bias[rows]).astype(BF16)
                both = dot(low, jnp.concatenate([values, ones], axis=1))
                inverse = 1.0 / both[:, HEAD:]
                heads[rows, columns(16 + head, HEAD)] = (both[:, :HEAD] * inverse).astype(BF16)

        for index in range(4):
            attend(index)
        once(micro, (OUT, OUT + 1))

        def attended(part):
            value = times_back(heads[rows, 2048:], (OUT, OUT + 1), part)
            pair_start(0, part, value)

        for index in range(2):
            attended(index)

    def forward_two(micro):
        rows = rows_of(micro)
        pair_wait(0)

        def norm_two(at, block, _):
            value = hidden[at].astype(F32) + pair_sum(0, block)
            middle[at] = value
            scale = inverse_rms(value)
            normed_two[at] = (value * scale * mlp_gain[...]).astype(BF16)
            scale_two[at] = jnp.broadcast_to(scale, (BLOCK, 128))

        over_rows(micro, norm_two)
        once(micro, range(QUERY))

        def hidden_units(chunk):
            wide[0] = dot(normed_two[rows], weight(GATE + chunk))
            wide[1] = dot(normed_two[rows], weight(UP + chunk))

            def silu(at, block, place_in):
                gate, up = wide[0, block], wide[1, block]
                ff[1, chunk, *place_in] = gate.astype(BF16)
                ff[2, chunk, *place_in] = up.astype(BF16)
                ff[0, chunk, *place_in] = (gate * jax.nn.sigmoid(gate) * up).astype(BF16)

            over_rows(micro, silu)

        for index in range(3):
            hidden_units(index)

        def moved(part):
            value = times_back(units(micro, 0), range(DOWN, GATE), part)
            pair_start(1, part, value)

        for index in range(2):
            moved(index)

    def forward_three(micro):
        for part in range(2):
            pair(1, part).wait()

            def result(at, block, _, part=part):
                here = columns(part)
                stage[at, here] = middle[at, here] + pair_part(1, part, block)

            over_rows(micro, result)

            @pl.when(section == 0)
            def _(part=part):
                leave_for(0, micro, part)

        output(0, micro).start()

    def norm_back(total, value, scale, gain):
        inner = total * gain
        return scale * inner - value * (scale * scale * scale) * jnp.mean(
            inner * value, axis=-1, keepdims=True
        )

    def add_gain(row, value):
        gains[0, row : row + 1] = gains[0, row : row + 1] + value

    def add_gains(row, part, value):
        for k in range(4):
            at = slice(row + part * 4 + k, row + part * 4 + k + 1)
            gains[0, at] = gains[0, at] + value[:, k * 128 : (k + 1) * 128]

    def turn(slot, value):
        for k in range(4):
            turned[slot, k] = value[:, columns(k, 256)].T.reshape(2, 4, 32, CHUNK)

    def weight_grad(chunk, slot, right):
        for part in range(4):
            value = dot(turned[slot, part].reshape(256, CHUNK), right)
            weights[chunk, part] = value.astype(BF16).reshape(2, 4, 32, CHUNK)

    rings = []
    for first, (order, count) in enumerate(zip(ORDERS, COUNTS)):
        own, scratch = scratch[:9], scratch[9:]

        def finish(i, half, total, first=first):
            grads_out[2 * i + first] = total

        def chunk_at(i, first=first):
            return (2 * i + first,)

        rings.append((count, LAGS, ring_stages(order, weights, chunk_at, own, place, finish)))

    def kept(chunk):
        return (section == 1) | (lax.rem(chunk, 3) > 0) | (chunk >= MLP_CHUNKS)

    def ring_start(chunk):
        for first in (0, 1):

            @pl.when((lax.rem(chunk, 2) == first) & kept(chunk))
            def _(first=first):
                rings[first][2][0]((chunk - first) // 2)

        @pl.when(jnp.logical_not(kept(chunk)))
        def _():
            leave(chunk // 3, 0).start()
            leave(chunk // 3, 1).start()

    def leave(i, slant):
        side = place.at["x"]
        return remote(
            weights.at[3 * i, :, 1 - side if slant else side],
            ff.at[i, side],
            s["left_send"].at[i, slant],
            s["left_recv"].at[i, side],
            aslant if slant else over_section,
        )

    def left_arrival(i, side):
        return remote(
            weights.at[3 * i, :, side],
            ff.at[i, side],
            s["left_send"].at[i, side],
            s["left_recv"].at[i, side],
            over_section,
        )

    def give_back(i):
        return remote(
            s["left_sum"].at[i],
            s["left_done"].at[i],
            s["done_send"].at[i],
            s["done_recv"].at[i],
            over_section,
        )

    def left_start(i):
        for side in (0, 1):
            left_arrival(i, side).wait_recv()
        ff[i, 2] = (ff[i, 0].astype(F32) + ff[i, 1].astype(F32)).astype(BF16)

    def left_finish(i, half, total):
        s["left_sum"][i, half * 16 : half * 16 + 16] = total
        if half:
            give_back(i).start()

    own, scratch = scratch[:6], scratch[6:]
    left_stages = [left_start] + ring_stages(
        LEFT_ORDER, ff, lambda i: (i, 2), own, place, left_finish, skipped=("x",)
    )

    def mlp_grad(chunk, carry):
        weight_grad(chunk, jnp.minimum(chunk // 3, 1), ff[chunk // 3, lax.rem(chunk, 3)].reshape(2 * ROW, CHUNK))
        ring_start(chunk)
        return carry

    def backward_one(micro):
        rows = rows_of(micro)

        @pl.when(section == 0)
        def _():
            arrive(1, micro)
            cross_sent(0, micro)

        def hidden_back(chunk):
            wide[0] = dot(grad[rows], weight(DOWN + chunk))

            def silu_back(at, block, place_in):
                act_grad = wide[0, block]
                gate, up = ff[1, chunk, *place_in].astype(F32), ff[2, chunk, *place_in].astype(F32)
                sigma = jax.nn.sigmoid(gate)
                passed = act_grad * sigma
                ff[1, chunk, *place_in] = (passed * up * (1.0 + gate * (1.0 - sigma))).astype(BF16)
                ff[2, chunk, *place_in] = (passed * gate).astype(BF16)

            over_rows(micro, silu_back)

        @pl.when((micro == 1) & (section == 0))
        def _():
            turn(0, grad)
            pl.semaphore_wait(s["left_free"], 2)

        for index in (1, 2, 0):
            hidden_back(index)

            @pl.when(micro == 1)
            def _(index=index):
                mlp_grad(DOWN + index, 0)


        def normed_two_back(part):
            value = times_back(units(micro, 1, 2), range(GATE, QUERY), part)
            pair_start(2, part, value)
            scaled = middle[rows, columns(part)] * scale_two[rows, :1]
            add_gains(8, part, jnp.sum(value * scaled, axis=0, keepdims=True))

        for index in range(2):
            normed_two_back(index)

        @pl.when(micro == 1)
        def _():
            @pl.when(section == 1)
            def _():
                turn(1, normed_two)

            lax.fori_loop(GATE, jnp.where(section == 0, QUERY, SOON), mlp_grad, 0)

    def backward_two(micro):
        rows = rows_of(micro)
        pair_wait(2)
        output(0, micro).wait()

        def middle_back(at, block, _):
            value = grad[at].astype(F32) + norm_back(
                pair_sum(2, block), middle[at], scale_two[at, :1], mlp_gain[...]
            )
            stage[at] = value
            attended_grad[at] = value.astype(BF16)

        over_rows(micro, middle_back)

        for k in range(2):
            mixed_grad[:, columns(k)] = dot(attended_grad[rows], weight(OUT + k)).astype(BF16)

        def attend_back(group):
            cos, sin = cosine[rows], sine[rows]
            cos_turned, sin_turned = s["cosine_turned"][micro], s["sine_turned"][micro]
            gain_turned = jnp.concatenate([s["q_gain_turned"][...]] * 2, axis=1)
            keys = key_rot[rows, columns(group, HEAD)]
            keys_turned = keys.T
            values = heads[rows, columns(12 + group, HEAD)]
            key_rot_grad = jnp.zeros((ROW, HEAD), F32)
            value_grad = jnp.zeros((ROW, HEAD), F32)
            for k in range(2):
                head = 2 * group + k
                here = columns(head, HEAD)
                queries = query_rot[rows, here]
                out_grad = mixed_grad[:, here]
                scores = dot(keys, queries, NT)
                raw = jnp.exp2(scores * (SCORE_SCALE * LOG2_E) + s["bias_turned"][rows])
                chance = raw * (1.0 / jnp.sum(raw, axis=0, keepdims=True))
                weighted = chance * dot(values, out_grad, NT)
                across = jnp.sum(weighted, axis=0, keepdims=True)
                score_grad = (weighted - chance * across).astype(BF16)
                value_grad = value_grad + dot(chance.astype(BF16), out_grad)
                key_rot_grad = key_rot_grad + dot(score_grad, queries)
                passed = dot(keys_turned, score_grad) * SCORE_SCALE
                swapped = jnp.concatenate([passed[HEAD // 2 :], passed[: HEAD // 2]], axis=0)
                turn_grad = passed * cos_turned - swapped * sin_turned
                query = heads[rows, here].T.astype(F32)
                scale = lax.rsqrt(jnp.mean(query * query, axis=0, keepdims=True) + EPSILON)
                scaled = query * scale
                s["q_gain_sum"][...] = s["q_gain_sum"][...] + turn_grad * scaled
                inner = turn_grad * gain_turned
                query_grad = scale * (inner - scaled * jnp.mean(inner * scaled, axis=0, keepdims=True))
                heads[rows, here] = query_grad.astype(BF16).T
            turn_grad = unrotated(key_rot_grad * SCORE_SCALE, cos, sin)
            here = columns(8 + group, HEAD)
            key = heads[rows, here].astype(F32)
            scale = inverse_rms(key)
            add_gain(17, jnp.sum(turn_grad * key * scale, axis=0, keepdims=True))
            heads[rows, here] = norm_back(turn_grad, key, scale, k_gain[...]).astype(BF16)
            heads[rows, columns(12 + group, HEAD)] = value_grad.astype(BF16)

        for index in range(4):
            attend_back(index)

        def normed_back(part):
            value = times_back(heads[rows, :2048], range(QUERY, OUT), part)
            pair_start(3, part, value)
            scaled = hidden[rows, columns(part)].astype(F32) * scale_one[rows, :1]
            add_gains(0, part, jnp.sum(value * scaled, axis=0, keepdims=True))

        for index in range(2):
            normed_back(index)
    def backward_three(micro):
        pair_wait(3)

        def hidden_back_end(at, block, _):
            stage[at] = stage[at] + norm_back(
                pair_sum(3, block), hidden[at].astype(F32), scale_one[at, :1], attn_gain[...]
            )

        over_rows(micro, hidden_back_end)
        output(1, micro).start()

        @pl.when(section == 1)
        def _():
            leave_for(1, micro, 0)
            leave_for(1, micro, 1)

        @pl.when((section == 1) & (micro == 1))
        def _():
            lax.fori_loop(SOON, QUERY, mlp_grad, 0)
            for device in (over_section, aslant):
                pl.semaphore_signal(s["left_free"], inc=1, device_id=device, device_id_type=MESH)

    @pl.when(section == 1)
    def _():
        for micro in range(2):
            load_cotangent(micro).wait()
        turn(0, grad)

    def step(turn_of, carry):
        back = turn_of - 2 + section

        @pl.when((turn_of == 2) & (section == 0))
        def _():
            turn(1, normed_two)

        for ahead, behind in (
            (forward_one, backward_one),
            (forward_two, backward_two),
            (forward_three, backward_three),
        ):

            @pl.when((back >= 0) & (back < 2))
            def _(behind=behind):
                behind(back)

            @pl.when(turn_of < 2)
            def _(ahead=ahead):
                ahead(turn_of)

        return carry

    lax.fori_loop(0, 4, step, 0)

    add_gain(16, jnp.sum(s["q_gain_sum"][...].T, axis=0, keepdims=True))
    turn(0, normed)
    turn(1, attended_grad)

    def attention_grad(chunk, carry):
        weight_grad(MLP_CHUNKS + chunk, chunk // 4, heads[:, columns(chunk)])
        ring_start(MLP_CHUNKS + chunk)
        return carry

    lax.fori_loop(0, CHUNKS - MLP_CHUNKS, attention_grad, 0)

    def always(i):
        return True

    groups = [
        (count, (None, *lags[1:]), stages, lambda i, first=first: kept(2 * i + first))
        for first, (count, lags, stages) in enumerate(rings)
    ]
    groups.append(
        (LEFT, [LEFT_FROM + lag for lag in LEFT_LAGS], left_stages, lambda i: section == 1)
    )
    groups.append((1, (0, 2, 2, 4, 4, 6, 6, 8), gain_stages(gains_out, scratch, place), always))

    def advance(now, carry):
        for step in range(8):
            for count, lags, stages, runs in groups:
                if step >= len(stages) or lags[step] is None:
                    continue
                i = now - lags[step]

                @pl.when((i >= 0) & (i < count) & runs(i))
                def _(i=i, run=stages[step]):
                    run(i)

        return carry

    lax.fori_loop(0, max(count + lags[-1] for count, lags, _, _ in groups), advance, 0)

    @pl.when(section == 0)
    def _():
        for i in range(LEFT):
            leave(i, 0).wait_send()
            leave(i, 1).wait_send()
            give_back(i).wait_recv()
            grads_out[3 * i] = s["left_done"][i]

    @pl.when(section == 1)
    def _():
        for i in range(LEFT):
            give_back(i).wait_send()

    for micro in range(2):
        output(1, micro).wait()

        @pl.when(section == 1)
        def _(micro=micro):
            cross_sent(1, micro)


def rope_table():
    half = HEAD // 2
    rates = THETA ** (-2.0 * np.arange(half) / HEAD)
    angle = np.arange(HEAD)[:, None] * np.concatenate([rates, rates])[None]
    sign = np.where(np.arange(HEAD) < half, -1.0, 1.0)
    parts = []
    for value in (np.cos(angle), np.sin(angle) * sign):
        high = value.astype(jnp.bfloat16)
        parts += [high, (value - high.astype(np.float64)).astype(jnp.bfloat16)]
    return jnp.asarray(np.concatenate(parts, axis=1))


def by_place(weight):
    return weight.reshape(4, 2, 4, 32, weight.shape[-1])


def shards(
    block_input,
    doc_lengths,
    out_cotangent,
    attn_gain,
    q_gain,
    k_gain,
    mlp_gain,
    q_weight,
    key_matrix,
    value_matrix,
    o_weight,
    gate_weight,
    up_weight,
    down_weight,
):
    vmem = pl.BlockSpec(memory_space=pltpu.VMEM)
    smem = pl.BlockSpec(memory_space=pltpu.SMEM)
    anywhere = pl.BlockSpec(memory_space=pl.ANY)
    scratch = list(SCRATCH.values())
    for order, count in zip(ORDERS, COUNTS):
        scratch += ring_scratch(order, count)
    scratch += ring_scratch(LEFT_ORDER, LEFT, 1)
    scratch += gain_scratch()
    full = jax.ShapeDtypeStruct(block_input.shape, F32)
    outputs, grads_in, grads, gains = pl.pallas_call(
        kernel,
        out_shape=(
            full,
            full,
            jax.ShapeDtypeStruct((CHUNKS, 32, CHUNK), F32),
            jax.ShapeDtypeStruct((1, GAIN_ROWS * 128), F32),
        ),
        in_specs=[smem, anywhere, anywhere] + [vmem] * 4 + [anywhere] * 7 + [vmem],
        out_specs=[anywhere, anywhere, vmem, vmem],
        scratch_shapes=scratch,
        compiler_params=pltpu.CompilerParams(
            collective_id=0, has_side_effects=True, vmem_limit_bytes=64 * 2**20 - 2**16
        ),
    )(
        doc_lengths,
        block_input,
        out_cotangent,
        attn_gain,
        q_gain,
        k_gain,
        mlp_gain,
        by_place(q_weight),
        by_place(key_matrix),
        by_place(value_matrix),
        by_place(o_weight),
        by_place(gate_weight),
        by_place(up_weight),
        by_place(down_weight),
        rope_table(),
    )

    return spread(outputs, grads_in, grads, gains)


MATRICES = ((QUERY, 2), (KEY, 1), (VALUE, 1), (OUT, 2), (GATE, 3), (UP, 3), (DOWN, 3))
GAIN_PARTS = ((0, 1024), (2048, 128), (2176, 128), (1024, 1024))


def spread_kernel(outputs, grads_in, grads, gains, *refs):
    results, (tokens, matrices, row, in_sem, out_sem) = refs[:-5], refs[-5:]
    loads, stores = [], []

    def through(src, held, pairs):
        load = pltpu.make_async_copy(src, held, in_sem.at[len(loads)])
        load.start()
        loads.append((load, pairs))

    through(grads, matrices, [])
    for k in range(8):
        rows = pl.ds(k % 4 * 128, 128)
        src, into = ((outputs, results[0]), (grads_in, results[1]))[k // 4]
        through(src.at[rows], tokens.at[k], [(tokens.at[k], into.at[0, rows])])
    through(gains, row, [])
    for (first, count), into in zip(MATRICES, results[6:]):
        for k in range(count):
            pair = (matrices.at[first + k], into.at[0, :, k * CHUNK : (k + 1) * CHUNK])
            loads[0][1].append(pair)
    for (first, size), into in zip(GAIN_PARTS, results[2:6]):
        loads[-1][1].append((row.at[:, first : first + size], into))
    for load, pairs in loads:
        load.wait()
        for src, dst in pairs:
            store = pltpu.make_async_copy(src, dst, out_sem.at[len(stores)])
            store.start()
            stores.append(store)
    for store in stores:
        store.wait()


def spread(outputs, grads_in, grads, gains):
    shapes = [(1, *outputs.shape)] * 2 + [(1, size) for _, size in GAIN_PARTS]
    shapes += [(1, 32, count * CHUNK) for _, count in MATRICES]
    anywhere = pl.BlockSpec(memory_space=pl.ANY)
    return pl.pallas_call(
        spread_kernel,
        out_shape=[jax.ShapeDtypeStruct(shape, F32) for shape in shapes],
        in_specs=[anywhere] * 4,
        out_specs=[anywhere] * len(shapes),
        scratch_shapes=[
            pltpu.VMEM((8, 128, outputs.shape[1]), F32),
            pltpu.VMEM(grads.shape, F32),
            pltpu.VMEM(gains.shape, F32),
            pltpu.SemaphoreType.DMA((10,)),
            pltpu.SemaphoreType.DMA((27,)),
        ],
        compiler_params=pltpu.CompilerParams(vmem_limit_bytes=16 * 2**20),
    )(outputs, grads_in, grads, gains)


def solution(mesh):
    weight = P("section", None, "tensor")
    gain = P("section", None)
    tokens = P("section", "dp", None)
    grad = P("section", "dp", "tensor")
    return jax.shard_map(
        shards,
        mesh=mesh,
        in_specs=(P("dp", None),) * 3 + (gain,) * 4 + (weight,) * 7,
        out_specs=(tokens,) * 2 + (gain,) * 4 + (grad,) * 7,
        check_vma=False,
    )
```
